512 devices in a mesh: depth: 8 (over y_hi, core), height: 8 (over z), filt: 8 (over x, y_lo).
Axes of the slice: x: 4, y: 8 (y_hi: 4, y_lo: 2; y = y_hi * 2 + y_lo), z: 8, core: 2. Of those that a mesh axis runs over, the one named last changes fastest.
Arguments:
- activations: bfloat16 [64, 16, 64, 128], P('filt', 'depth', 'height'), may hold values from -6 to 6
- weights: bfloat16 [27, 64, 128], P(None, None, 'filt'), may hold values from -0.15625 to 0.15625
- bias: float32 [128], P('filt'), may hold values from -3 to 3
- cotangent: bfloat16 [128, 16, 64, 128], P('filt', 'depth', 'height'), may hold values from -6 to 6
Outputs:
- output: bfloat16 [128, 16, 64, 128], P('filt', 'depth', 'height')
- input_grad: bfloat16 [64, 16, 64, 128], P('filt', 'depth', 'height')
- weight_grad: float32 [27, 64, 128], P(None, None, 'filt')
- bias_grad: float32 [128], P('filt')
The draws below stay inside these ranges and needn't reach their ends.
All inputs are finite; a program needn't handle non-finite values.
Results may differ from the reference program's by a relative error of at most 0.017.
Values may be sent and summed in bfloat16 or wider, within the bound.
No kernel may reach another device: no remote copies, remote signals or barrier semaphores. Data moves between devices by JAX's collectives and lax.ppermute only.
A program may use at most 64 MiB of HBM per device.

```python
import jax
import jax.numpy as jnp
from jax import lax

CIN = 64
COUT = 128
WID = 128
NDEP = 16
NHEI = 64
N_FILT = 8


def levels(rng, shape, split, least, high):
    level = 1.0
    for axis_at, blocks in split:
        draws = jax.random.uniform(jax.random.fold_in(jax.random.fold_in(rng, 6), axis_at), (blocks,), jnp.float32, least / len(split), high / len(split))
        level = level * jnp.repeat(jnp.exp(draws), shape[axis_at] // blocks).reshape((-1,) + (1,) * (len(shape) - 1 - axis_at))
    return level


def bell_draw(key, extent, deviation, most, shards=(), held_as=jnp.bfloat16):
    result = jax.random.normal(key, extent, jnp.float32) * deviation
    if len(shards) > 0:
        result = levels(key, extent, shards, -0.22, 0.18) * result
    return jnp.clip(result, min=-most, max=most).astype(held_as)


def setup_inputs(seed: int = 0) -> dict:
    key_list = jax.random.split(jax.random.key(seed), 5)
    return {
        "activations": bell_draw(key_list[0], (CIN, NDEP, NHEI, WID), 1.0, 6.0, ((0, 8), (1, 8), (2, 8))),
        "weights": bell_draw(key_list[1], (27, CIN, COUT), (27 * CIN) ** -0.5, 0.15625, ((2, 8),)),
        "bias": bell_draw(key_list[2], (COUT,), 0.5, 3.0, ((0, 8),), jnp.float32),
        "cotangent": bell_draw(key_list[3], (COUT, NDEP, NHEI, WID), 1.0, 6.0, ((0, 8), (1, 8), (2, 8))),
    }


dims = ("NCDHW", "OIDHW", "NCDHW")


def correlate(lhs, rhs, pad):
    return lax.conv_general_dilated(lhs, rhs, (1, 1, 1), ((pad, pad),) * 3, dimension_numbers=dims, precision=lax.Precision.HIGHEST)


def reference(activations, weights, bias, cotangent):
    x_full = activations.astype(jnp.float32)
    w_full = weights.astype(jnp.float32).reshape(3, 3, 3, CIN, COUT)
    kernel = jnp.transpose(w_full, (4, 3, 0, 1, 2))
    pre = correlate(x_full[None], kernel, 1)[0] + bias[:, None, None, None]
    output = (0.2 * pre + 0.8 * jax.nn.softplus(pre)).astype(jnp.bfloat16)
    pre_grad = (cotangent.astype(jnp.float32) * (0.2 + 0.8 * jax.nn.sigmoid(pre))).astype(jnp.bfloat16)
    grad_full = pre_grad.astype(jnp.float32)
    flipped = jnp.transpose(w_full[::-1, ::-1, ::-1], (3, 4, 0, 1, 2))
    group = COUT // N_FILT
    total = jnp.zeros(activations.shape, jnp.float32)
    for index in range(N_FILT):
        part = correlate(grad_full[None, index * group:(index + 1) * group], flipped[:, index * group:(index + 1) * group], 1)[0]
        total = total + part.astype(jnp.bfloat16).astype(jnp.float32)
    input_grad = total.astype(jnp.bfloat16)
    taps = correlate(x_full[:, None], grad_full[:, None], 1)
    weight_grad = jnp.transpose(taps, (2, 3, 4, 0, 1)).reshape(27, CIN, COUT)
    bias_grad = jnp.sum(grad_full, axis=(1, 2, 3))
    return output, input_grad, weight_grad, bias_grad
```

```python
import jax
import jax.numpy as jnp
from jax import lax
from jax.sharding import PartitionSpec as P

BF16 = jnp.bfloat16
F32 = jnp.float32


def padded_2(cells, sides, width):
    for axis, dim in sides:
        count = lax.axis_size(axis)
        ends = count - 1
        head = lax.slice_in_dim(cells, 0, width, axis=dim)
        tail = lax.slice_in_dim(cells, cells.shape[dim] - width, cells.shape[dim], axis=dim)
        cells = jnp.concatenate(
            [
                lax.ppermute(tail, axis, [(i, (i + 1) % count) for i in range(ends)]),
                cells,
                lax.ppermute(head, axis, [((i + 1) % count, i) for i in range(ends)]),
            ],
            axis=dim,
        )
    return cells


def spread(block, axis, groups=None):
    members = lax.axis_size(axis) if groups is None else len(groups[0])
    copies = jnp.broadcast_to(block[None], (members,) + block.shape)
    return lax.all_to_all(copies, axis, 0, 0, tiled=True, axis_index_groups=groups)


def widen(block):
    return jnp.pad(block, ((0, 0), (0, 0), (0, 0), (1, 1)))


def forward_stack(padded, first_d, first_h, planes, rows, width):
    return jnp.concatenate(
        [
            padded[:, first_d : first_d + planes, first_h : first_h + rows, kw : kw + width]
            for kw in range(3)
        ],
        axis=0,
    )


def input_term(grad_pad, w_part, planes, rows, width):
    total = jnp.zeros((w_part.shape[1], planes, rows, width), F32)
    for kd in range(3):
        for kh in range(3):
            stack = jnp.concatenate(
                [
                    grad_pad[
                        :, 2 - kd : 2 - kd + planes, 2 - kh : 2 - kh + rows, 2 - kw : 2 - kw + width
                    ]
                    for kw in range(3)
                ],
                axis=0,
            )
            block = jnp.concatenate([w_part[kd * 9 + kh * 3 + kw] for kw in range(3)], axis=1)
            total = total + jnp.einsum("ik,kdhw->idhw", block, stack, preferred_element_type=F32)
    return total


def sum_over_blocks(part):
    half = part.shape[1] // 2
    core = lax.axis_index("depth") % 2
    depth = lax.axis_size("depth")
    pairs = [(i, i ^ 1) for i in range(depth)]
    groups = [[i for i in range(depth) if i % 2 == c] for c in range(2)]
    low, high = part[:, :half], part[:, half:]
    sent = jnp.where(core == 0, high, low).astype(BF16)
    kept = jnp.where(core == 0, low, high)
    mine = (kept + lax.ppermute(sent, "depth", pairs).astype(F32)).astype(BF16)
    mine = jnp.sum(spread(mine, "depth", groups).astype(F32), axis=0).astype(BF16)
    mine = jnp.sum(spread(mine, "height").astype(F32), axis=0)
    other = lax.ppermute(mine, "depth", pairs)
    return jnp.concatenate(
        [jnp.where(core == 0, mine, other), jnp.where(core == 0, other, mine)], axis=1
    )


def per_device(activations, weights, bias, cotangent):
    cin_dev, planes, rows, width = activations.shape
    taps, cin_all, cout_dev = weights.shape
    sides = (("depth", 1), ("height", 2))
    rimmed = padded_2(activations, sides, 1)
    padded = widen(spread(rimmed, "filt").reshape((cin_all,) + rimmed.shape[1:]))
    pre = jnp.zeros((cout_dev, planes, rows, width), F32) + bias[:, None, None, None]
    for kd in range(3):
        for kh in range(3):
            stack = forward_stack(padded, kd, kh, planes, rows, width)
            first = kd * 9 + kh * 3
            block = weights[first : first + 3].reshape(3 * cin_all, cout_dev)
            pre = pre + jnp.einsum("kc,kdhw->cdhw", block, stack, preferred_element_type=F32)
    output = (0.2 * pre + 0.8 * jax.nn.softplus(pre)).astype(BF16)
    pre_grad = (cotangent.astype(F32) * (0.2 + 0.8 * jax.nn.sigmoid(pre))).astype(BF16)
    blocks = []
    for kd in range(3):
        for kh in range(3):
            stack = forward_stack(padded, kd, kh, planes, rows, width)
            blocks.append(jnp.einsum("kdhw,cdhw->ck", stack, pre_grad, preferred_element_type=F32))
    bias_part = jnp.sum(pre_grad.astype(F32), axis=(1, 2, 3))
    used = taps * cin_all
    blocks.append(jnp.pad(bias_part[:, None], ((0, 0), (0, -used % 256 - 1))))
    total = sum_over_blocks(jnp.concatenate(blocks, axis=1))
    weight_grad = total[:, :used].reshape(cout_dev, taps, cin_all).transpose(1, 2, 0)
    bias_grad = total[:, used]
    grad_pad = widen(padded_2(pre_grad, sides, 1))
    part = input_term(grad_pad, weights, planes, rows, width).astype(BF16)
    parts = lax.all_to_all(part, "filt", 0, 0, tiled=True)
    parts = parts.reshape((-1, cin_dev) + part.shape[1:])
    summed = jnp.sum(parts.astype(F32), axis=0).astype(BF16)
    return (output, summed, weight_grad, bias_grad)


def solution(mesh):
    placed = (
        P("filt", "depth", "height", None),
        P(None, None, "filt"),
        P("filt"),
        P("filt", "depth", "height", None),
    )
    return jax.shard_map(
        per_device,
        mesh=mesh,
        in_specs=placed,
        out_specs=(
            P("filt", "depth", "height", None),
            P("filt", "depth", "height", None),
            P(None, None, "filt"),
            P("filt"),
        ),
        check_vma=False,
    )
```

```python
import functools

import jax
import jax.numpy as jnp
from jax import lax
from jax.experimental import pallas as pl
from jax.experimental.pallas import tpu as pltpu
from jax.sharding import PartitionSpec as P

BF16 = jnp.bfloat16
F32 = jnp.float32


def exchange(first, last, axis):
    ends = lax.axis_size(axis) - 1
    before = lax.ppermute(last, axis, [(i, i + 1) for i in range(ends)])
    after = lax.ppermute(first, axis, [(i + 1, i) for i in range(ends)])
    return before, after


def spread(block, axis, groups=None):
    members = lax.axis_size(axis) if groups is None else len(groups[0])
    copies = jnp.broadcast_to(block[None], (members,) + block.shape)
    return lax.all_to_all(copies, axis, 0, 0, tiled=True, axis_index_groups=groups)


def rim_rows(planes, count):
    return (
        jnp.concatenate([p[:count] for p in planes], axis=0),
        jnp.concatenate([p[-count:] for p in planes], axis=0),
    )


def shifted(value, lane):
    width = value.shape[-1]
    ahead = jnp.where(lane == width - 1, 0.0, pltpu.roll(value, width - 1, 1))
    behind = jnp.where(lane == 0, 0.0, pltpu.roll(value, 1, 1))
    return jnp.concatenate([ahead, value, behind], axis=0)


def three_rows(plane, before, after, p, h, rows, count):
    if h == 0:
        return jnp.concatenate([before[p * count : (p + 1) * count, :], plane[: 2 * count, :]], axis=0)
    if h == rows - 1:
        return jnp.concatenate([plane[(h - 1) * count :, :], after[p * count : (p + 1) * count, :]], axis=0)
    return plane[(h - 1) * count : (h + 2) * count, :]


def forward_kernel(
    rows, planes, core, w_ref, bias_ref, cot_ref, *refs
):
    grid = refs[: planes + 2]
    before, after, out_ref, pg_ref, sent_ref, kept_ref, total = refs[planes + 2 :]
    cin = before.shape[0] // (planes + 2)
    cout, width = cot_ref.shape[1:]
    lane = lax.broadcasted_iota(jnp.int32, (cout, width), 1)
    bias = bias_ref[...]
    sums = [None] * 3
    bias_sum = jnp.zeros((cout, width), F32)
    for d in range(planes):
        for h in range(0, rows, 2):
            cells = [
                jnp.concatenate(
                    [three_rows(grid[d + kd], before, after, d + kd, h + e, rows, cin) for e in range(2)],
                    axis=1,
                )
                for kd in range(3)
            ]
            acc = jnp.dot(w_ref[0], cells[0], preferred_element_type=F32)
            for kd in range(1, 3):
                acc = acc + jnp.dot(w_ref[kd], cells[kd], preferred_element_type=F32)
            grads = []
            for e in range(2):
                z = acc[:, e * width : (e + 1) * width]
                pre = (
                    z[cout : 2 * cout]
                    + jnp.where(lane == 0, 0.0, pltpu.roll(z[:cout], 1, 1))
                    + jnp.where(lane == width - 1, 0.0, pltpu.roll(z[2 * cout :], width - 1, 1))
                    + bias
                )
                small = jnp.exp(-jnp.abs(pre))
                softplus = jnp.maximum(pre, 0.0) + jnp.log1p(small)
                sigmoid = jnp.where(pre >= 0, 1.0, small) / (1.0 + small)
                at = d * rows + h + e
                out_ref[at] = (0.2 * pre + 0.8 * softplus).astype(BF16)
                grad = (cot_ref[at].astype(F32) * (0.2 + 0.8 * sigmoid)).astype(BF16)
                pg_ref[at] = grad
                grad = grad.astype(F32)
                bias_sum = bias_sum + grad
                grads.append(shifted(grad, lane).astype(BF16))
            both = jnp.concatenate(grads, axis=1)
            for kd in range(3):
                term = lax.dot_general(
                    both, cells[kd], (((1,), (1,)), ((), ())), preferred_element_type=F32
                )
                sums[kd] = term if sums[kd] is None else sums[kd] + term
    for kw in range(3):
        for kd in range(3):
            for kh in range(3):
                at = (kw * 9 + kd * 3 + kh) * cin
                total[:, at : at + cin] = sums[kd][kw * cout : (kw + 1) * cout, kh * cin : (kh + 1) * cin]
    total[:, 27 * cin :] = jnp.broadcast_to(jnp.sum(bias_sum, axis=1, keepdims=True), (cout, cin))
    half = 14 * cin
    even = core[0] == 0
    low, high = total[:, :half], total[:, half:]
    sent_ref[...] = jnp.where(even, high, low).astype(BF16)
    kept_ref[...] = jnp.where(even, low, high)


def backward_kernel(rows, planes, w_ref, own, low, high, before, after, out_ref, stack):
    cout, width = own.shape[1:]
    cin = w_ref.shape[0]
    groups = out_ref.shape[0]
    part = cin // groups
    lane = lax.broadcasted_iota(jnp.int32, (cout, width), 1)
    step = 3 * cout
    for p in range(planes + 2):
        for r in range(rows + 2):
            if r == 0:
                value = before[p]
            elif r == rows + 1:
                value = after[p]
            elif p == 0:
                value = low[r - 1]
            elif p == planes + 1:
                value = high[r - 1]
            else:
                value = own[(p - 1) * rows + r - 1]
            stack[p, r * step : (r + 1) * step, :] = shifted(value.astype(F32), lane).astype(BF16)
    w = w_ref[...]
    for d in range(planes):
        for h in range(0, rows, 2):
            cells = jnp.concatenate(
                [
                    jnp.concatenate(
                        [stack[d + a, (h + e) * step : (h + e + 3) * step, :] for a in range(3)], axis=0
                    )
                    for e in range(2)
                ],
                axis=1,
            )
            acc = jnp.dot(w, cells, preferred_element_type=F32)
            at = (d * rows + h) // 2
            for f in range(groups):
                piece = acc[f * part : (f + 1) * part]
                out_ref[f, at] = jnp.concatenate([piece[:, :width], piece[:, width:]], axis=0).astype(BF16)


def per_device(activations, weights, bias, cotangent):
    cin_dev, planes, rows, width = activations.shape
    taps, cin, cout = weights.shape
    cells = planes * rows
    depth = lax.axis_size("depth")
    core = lax.axis_index("depth") % 2
    pairs = [(i, i ^ 1) for i in range(depth)]
    groups = [[i for i in range(depth) if i % 2 == c] for c in range(2)]
    struct = jax.ShapeDtypeStruct

    mine = activations.transpose(1, 2, 0, 3)
    full = spread(mine, "filt").transpose(1, 2, 0, 3, 4).reshape(planes, rows * cin, width)
    low, high = exchange(full[0], full[planes - 1], "depth")
    grid = [low] + [full[d] for d in range(planes)] + [high]
    before, after = exchange(*rim_rows(grid, cin), "height")

    split = weights.reshape(3, 3, 3, cin, cout)
    w_forward = split.transpose(0, 2, 4, 1, 3).reshape(3, 3 * cout, 3 * cin)
    w_back = split[::-1, ::-1].transpose(3, 0, 1, 2, 4).reshape(cin, taps * cout)
    cot = cotangent.transpose(1, 2, 0, 3).reshape(cells, cout, width)
    work = 2 * cells * width * taps * cin * cout
    half = 14 * cin
    vmem = pl.BlockSpec(memory_space=pltpu.VMEM)
    out, grad, sent, kept = pl.pallas_call(
        functools.partial(forward_kernel, rows, planes),
        out_shape=(
            struct((cells, cout, width), BF16),
            struct((cells, cout, width), BF16),
            struct((cout, half), BF16),
            struct((cout, half), F32),
        ),
        in_specs=[pl.BlockSpec(memory_space=pltpu.SMEM)] + [vmem] * (planes + 7),
        out_specs=(vmem,) * 4,
        scratch_shapes=[pltpu.VMEM((cout, 2 * half), F32)],
        cost_estimate=pl.CostEstimate(flops=2 * work, bytes_accessed=1 << 20, transcendentals=1 << 17),
        name="forward",
    )(
        core.reshape(1).astype(jnp.int32),
        w_forward,
        jnp.broadcast_to(bias[:, None], (cout, width)),
        cot,
        *grid,
        before,
        after,
    )
    output = out.reshape(planes, rows, cout, width).transpose(2, 0, 1, 3)

    mine = (kept + lax.ppermute(sent, "depth", pairs).astype(F32)).astype(BF16)
    mine, grad = lax.optimization_barrier((mine, grad))
    mine = jnp.sum(spread(mine, "depth", groups).astype(F32), axis=0).astype(BF16)
    mine = jnp.sum(spread(mine, "height").astype(F32), axis=0)
    other = lax.ppermute(mine, "depth", pairs)
    total = jnp.concatenate(
        [jnp.where(core == 0, mine, other), jnp.where(core == 0, other, mine)], axis=1
    )
    weight_grad = total[:, : taps * cin].reshape(cout, 3, 3, 3, cin)
    weight_grad = weight_grad.transpose(2, 3, 1, 4, 0).reshape(taps, cin, cout)
    bias_grad = total[:, taps * cin]

    by_plane = grad.reshape(planes, rows, cout, width)
    low, high = exchange(by_plane[0], by_plane[planes - 1], "depth")
    edge = [low] + [by_plane[d] for d in range(planes)] + [high]
    before, after = exchange(
        jnp.stack([p[0] for p in edge]), jnp.stack([p[rows - 1] for p in edge]), "height"
    )
    filt = lax.axis_size("filt")
    parts = pl.pallas_call(
        functools.partial(backward_kernel, rows, planes),
        out_shape=struct((filt, cells // 2, 2 * cin_dev, width), BF16),
        in_specs=[vmem] * 6,
        out_specs=vmem,
        scratch_shapes=[pltpu.VMEM((planes + 2, (rows + 2) * 3 * cout, width), BF16)],
        cost_estimate=pl.CostEstimate(flops=work, bytes_accessed=1 << 19, transcendentals=0),
        name="backward",
    )(w_back, grad, low, high, before, after)
    parts = lax.all_to_all(parts, "filt", 0, 0, tiled=True)
    summed = jnp.sum(parts.astype(F32), axis=0).astype(BF16)
    summed = summed.reshape(planes, rows, cin_dev, width).transpose(2, 0, 1, 3)
    return (output, summed, weight_grad, bias_grad)


def solution(mesh):
    placed = (
        P("filt", "depth", "height", None),
        P(None, None, "filt"),
        P("filt"),
        P("filt", "depth", "height", None),
    )
    return jax.shard_map(
        per_device,
        mesh=mesh,
        in_specs=placed,
        out_specs=(
            P("filt", "depth", "height", None),
            P("filt", "depth", "height", None),
            P(None, None, "filt"),
            P("filt"),
        ),
        check_vma=False,
    )
```

```python
import functools

import jax
import jax.numpy as jnp
import numpy as np
from jax import lax
from jax.experimental import pallas as pl
from jax.experimental.pallas import tpu as pltpu
from jax.sharding import PartitionSpec as P

BF16 = jnp.bfloat16
F32 = jnp.float32
PART = 8


def spread(block, axis, groups=None):
    members = lax.axis_size(axis) if groups is None else len(groups[0])
    copies = jnp.broadcast_to(block[None], (members,) + block.shape)
    return lax.all_to_all(copies, axis, 0, 0, tiled=True, axis_index_groups=groups)


def neighbours(first, last, axis):
    ends = lax.axis_size(axis) - 1
    before = lax.ppermute(last, axis, [(i, i + 1) for i in range(ends)])
    after = lax.ppermute(first, axis, [(i + 1, i) for i in range(ends)])
    return before, after


def shifted(value, lane):
    width = value.shape[-1]
    ahead = jnp.where(lane == width - 1, 0.0, pltpu.roll(value, width - 1, 1))
    behind = jnp.where(lane == 0, 0.0, pltpu.roll(value, 1, 1))
    return jnp.concatenate([ahead, value, behind], axis=0)


def forward_kernel(planes, rows, at_ref, w_ref, bias_ref, cot, cot_before, cot_after, tiles, *refs):
    out_ref, face_ref, far_ref, kept_ref, grads, halves = refs
    cout, width = cot.shape[1:]
    sources = tiles.shape[0]
    lane = lax.broadcasted_iota(jnp.int32, (cout, width), 1)
    bias = bias_ref[...]
    sums = [None] * 3
    bias_sum = jnp.zeros((cout, width), F32)
    for d in range(planes):
        for pair in range(rows // 2 + 1):
            cells = [
                jnp.concatenate(
                    [tiles[s, d + kd, pair + t] for t in range(2) for s in range(sources)], axis=0
                )
                for kd in range(3)
            ]
            acc = jnp.dot(w_ref[0], cells[0], preferred_element_type=F32)
            for kd in range(1, 3):
                acc = acc + jnp.dot(w_ref[kd], cells[kd], preferred_element_type=F32)
            stacks = []
            for e in range(2):
                z = acc[3 * e * cout : 3 * (e + 1) * cout]
                pre = (
                    z[cout : 2 * cout]
                    + jnp.where(lane == 0, 0.0, pltpu.roll(z[:cout], 1, 1))
                    + jnp.where(lane == width - 1, 0.0, pltpu.roll(z[2 * cout :], width - 1, 1))
                    + bias
                )
                small = jnp.exp(-jnp.abs(pre))
                sigmoid = jnp.where(pre >= 0, 1.0, small) / (1.0 + small)
                row = 2 * pair + e
                if row == 0:
                    cotangent = cot_before[d]
                elif row == rows + 1:
                    cotangent = cot_after[d]
                else:
                    cotangent = cot[d * rows + row - 1]
                grad = (cotangent.astype(F32) * (0.2 + 0.8 * sigmoid)).astype(BF16)
                grads[d, row] = grad
                if row == 0 or row == rows + 1:
                    stacks.append(jnp.zeros((3 * cout, width), BF16))
                    continue
                softplus = jnp.maximum(pre, 0.0) + jnp.log1p(small)
                out_ref[d * rows + row - 1] = (0.2 * pre + 0.8 * softplus).astype(BF16)
                grad = grad.astype(F32)
                bias_sum = bias_sum + grad
                stacks.append(shifted(grad, lane).astype(BF16))
            both = jnp.concatenate(stacks, axis=0)
            for kd in range(3):
                term = lax.dot_general(
                    both, cells[kd], (((1,), (1,)), ((), ())), preferred_element_type=F32
                )
                sums[kd] = term if sums[kd] is None else sums[kd] + term

    even = (lane // PART) % 2 == 0
    blocks, last = [], []
    for kd in range(3):
        for kw in range(3):
            one = sums[kd][kw * cout : (kw + 1) * cout]
            two = sums[kd][(3 + kw) * cout : (4 + kw) * cout]
            back = pltpu.roll(two[:, width:], width - PART, 1)
            blocks.append(
                one[:, :width]
                + jnp.where(
                    even,
                    pltpu.roll(two[:, :width], width - PART, 1),
                    pltpu.roll(two[:, width:], PART, 1),
                )
            )
            last.append(one[:, width:] + back)
    last.append(jnp.broadcast_to(jnp.sum(bias_sum, axis=1, keepdims=True), (cout, width)))
    for k in range(0, len(last), 2):
        blocks.append(jnp.where(even, last[k], pltpu.roll(last[k + 1], PART, 1)))
    source = lax.broadcasted_iota(jnp.int32, (width, width), 0)
    target = (source // PART) % 2 * (width // 2) + source // (2 * PART) * PART + source % PART
    order = jnp.where(lax.broadcasted_iota(jnp.int32, (width, width), 1) == target, 1.0, 0.0).astype(BF16)
    placed = jnp.dot(jnp.concatenate(blocks, axis=0).astype(BF16), order, preferred_element_type=F32)
    count = len(blocks) // 2
    for k in range(2 * count):
        halves[k // count, k % count] = placed[k * cout : (k + 1) * cout].astype(BF16)
    core = at_ref[0]
    face_ref[: rows + 2] = grads[1 - core]
    face_ref[rows + 2 :] = halves[1 - core]
    far_ref[...] = grads[core]
    kept_ref[...] = halves[core]


def backward_kernel(planes, rows, at_ref, w_ref, face, far, face_in, far_in, kept_ref, sent_ref, stack, parts):
    cout, width = far.shape[1:]
    cin = w_ref.shape[0]
    count = 2 * parts.shape[1]
    part = cin // count
    lane = lax.broadcasted_iota(jnp.int32, (cout, width), 1)
    step = 3 * cout
    core = at_ref[0]
    for q, source in enumerate((face_in, face, far, far_in)):
        p = jnp.where(core == 1, q, planes + 1 - q)
        for r in range(rows + 2):
            stack[p, r * step : (r + 1) * step, :] = shifted(source[r].astype(F32), lane).astype(BF16)
    w = w_ref[...]
    for d in range(planes):
        for h in range(0, rows, 2):
            cells = jnp.concatenate(
                [
                    jnp.concatenate(
                        [stack[d + a, (h + e) * step : (h + e + 3) * step, :] for a in range(3)], axis=0
                    )
                    for e in range(2)
                ],
                axis=1,
            )
            acc = jnp.dot(w, cells, preferred_element_type=F32)
            pair = (d * rows + h) // 2
            for f in range(count):
                piece = acc[f * part : (f + 1) * part]
                piece = jnp.concatenate([piece[:, :width], piece[:, width:]], axis=0).astype(BF16)
                parts[(f % 2) ^ at_ref[1], (f // 2) ^ at_ref[2], pair] = piece
    kept_ref[...] = parts[0]
    sent_ref[...] = parts[1]


def placing(cin):
    ones = np.zeros((2, 3, cin, 2, cin // PART, 2, PART), np.float32)
    for e in range(2):
        for kh in range(3):
            for i in range(cin):
                ones[e, kh, i, (kh + e) // 2, i // PART, (kh + e) % 2, i % PART] = 1
    return ones.reshape(2, 3 * cin, 4 * cin)


def per_device(activations, weights, bias, cotangent):
    cin_dev, planes, rows, width = activations.shape
    taps, cin, cout = weights.shape
    cells = planes * rows
    depth, filt = lax.axis_size("depth"), lax.axis_size("filt")
    core = lax.axis_index("depth") % 2
    even = core == 0
    swap = [(i, i ^ 1) for i in range(depth)]
    cross = [(i, i - 1 if i % 2 == 0 else i + 1) for i in range(1, depth - 1)]
    groups = [[i for i in range(depth) if i % 2 == c] for c in range(2)]
    mine = lax.axis_index("filt")
    at = jnp.stack([core, mine % 2, mine // 2]).astype(jnp.int32)
    struct = jax.ShapeDtypeStruct

    grid = activations.transpose(1, 2, 0, 3)
    face_in = lax.ppermute(jnp.where(even, grid[planes - 1], grid[0]), "depth", swap)
    far_in = lax.ppermute(jnp.where(even, grid[0], grid[planes - 1]), "depth", cross)
    low, high = jnp.where(even, far_in, face_in), jnp.where(even, face_in, far_in)
    grid = jnp.concatenate([low[None], grid, high[None]], axis=0)
    before, after = neighbours(grid[:, :2], grid[:, rows - 2 :], "height")
    grid = jnp.concatenate([before, grid, after], axis=1)
    grid = grid.reshape(planes + 2, rows // 2 + 2, 2 * cin_dev, width)
    grid, late = lax.optimization_barrier((grid, cotangent))
    tiles = spread(grid, "filt")

    cot = late.transpose(1, 2, 0, 3)
    cot_before, cot_after = neighbours(cot[:, 0], cot[:, rows - 1], "height")
    cot = cot.reshape(cells, cout, width)
    split = weights.reshape(3, 3, 3, cin, cout)
    w_forward = jnp.einsum(
        "akj,ejn->aekn",
        split.transpose(0, 2, 4, 1, 3).reshape(3, 3 * cout, 3 * cin),
        jnp.asarray(placing(cin), BF16),
        preferred_element_type=F32,
    )
    w_forward = w_forward.astype(BF16).reshape(3, 6 * cout, 4 * cin)
    w_back = split[::-1, ::-1].transpose(3, 0, 1, 2, 4).reshape(cin, taps * cout)
    work = 2 * cells * width * taps * cin * cout
    count = (taps + 1) // 4
    smem, vmem = pl.BlockSpec(memory_space=pltpu.SMEM), pl.BlockSpec(memory_space=pltpu.VMEM)
    out, face, far, kept = pl.pallas_call(
        functools.partial(forward_kernel, planes, rows),
        out_shape=(
            struct((cells, cout, width), BF16),
            struct((rows + 2 + count, cout, width), BF16),
            struct((rows + 2, cout, width), BF16),
            struct((count, cout, width), BF16),
        ),
        in_specs=[smem] + [vmem] * 6,
        out_specs=(vmem,) * 4,
        scratch_shapes=[
            pltpu.VMEM((planes, rows + 2, cout, width), BF16),
            pltpu.VMEM((2, count, cout, width), BF16),
        ],
        cost_estimate=pl.CostEstimate(flops=3 * work, bytes_accessed=1 << 20, transcendentals=1 << 17),
        name="forward",
    )(at, w_forward, jnp.broadcast_to(bias[:, None], (cout, width)), cot, cot_before, cot_after, tiles)
    output = out.reshape(planes, rows, cout, width).transpose(2, 0, 1, 3)

    face_in = lax.ppermute(face, "depth", swap)
    far_in = lax.ppermute(far, "depth", cross)
    total = (kept.astype(F32) + face_in[rows + 2 :].astype(F32)).astype(BF16)
    total = jnp.sum(spread(total, "depth", groups).astype(F32), axis=0).astype(BF16)
    total = jnp.sum(spread(total, "height").astype(F32), axis=0)
    other = lax.ppermute(total, "depth", swap)
    total = jnp.concatenate([jnp.where(even, total, other), jnp.where(even, other, total)], axis=0)
    first = total[:9].reshape(3, 3, cout, 2, cin).transpose(0, 3, 1, 2, 4)
    rest = total[9:].reshape(5, cout, 2, cin).transpose(0, 2, 1, 3).reshape(10, cout, cin)
    third = rest[:9].reshape(3, 1, 3, cout, cin)
    weight_grad = jnp.concatenate([first, third], axis=1).reshape(taps, cout, cin).transpose(0, 2, 1)
    bias_grad = rest[9, :, 0]

    kept, sent = pl.pallas_call(
        functools.partial(backward_kernel, planes, rows),
        out_shape=(struct((filt // 2, cells // 2, 2 * cin_dev, width), BF16),) * 2,
        in_specs=[smem] + [vmem] * 5,
        out_specs=(vmem,) * 2,
        scratch_shapes=[
            pltpu.VMEM((planes + 2, (rows + 2) * 3 * cout, width), BF16),
            pltpu.VMEM((2, filt // 2, cells // 2, 2 * cin_dev, width), BF16),
        ],
        cost_estimate=pl.CostEstimate(flops=work, bytes_accessed=1 << 19, transcendentals=0),
        name="backward",
    )(at, w_back, face, far, face_in, far_in)
    pair = kept.astype(F32) + lax.ppermute(sent, "filt", [(i, i ^ 1) for i in range(filt)]).astype(F32)
    summed = pair[0]
    for k in range(1, filt // 2):
        moved = lax.ppermute(pair[k].astype(BF16), "filt", [(i, i ^ (2 * k)) for i in range(filt)])
        summed = summed + moved.astype(F32)
    summed = summed.astype(BF16).reshape(planes, rows, cin_dev, width).transpose(2, 0, 1, 3)
    return (output, summed, weight_grad, bias_grad)


def solution(mesh):
    placed = (
        P("filt", "depth", "height", None),
        P(None, None, "filt"),
        P("filt"),
        P("filt", "depth", "height", None),
    )
    return jax.shard_map(
        per_device,
        mesh=mesh,
        in_specs=placed,
        out_specs=(
            P("filt", "depth", "height", None),
            P("filt", "depth", "height", None),
            P(None, None, "filt"),
            P("filt"),
        ),
        check_vma=False,
    )
```

```python
import functools

import jax
import jax.numpy as jnp
import numpy as np
from jax import lax
from jax.experimental import pallas as pl
from jax.experimental.pallas import tpu as pltpu
from jax.sharding import PartitionSpec as P

BF16 = jnp.bfloat16
F32 = jnp.float32
PART = 8


def copies(block, count):
    return jnp.broadcast_to(block[None], (count,) + block.shape)


def swapped(blocks, axis):
    return lax.all_to_all(blocks, axis, 0, 0, tiled=True)


def neighbours(first, last, axis):
    ends = lax.axis_size(axis) - 1
    before = lax.ppermute(last, axis, [(i, i + 1) for i in range(ends)])
    after = lax.ppermute(first, axis, [(i + 1, i) for i in range(ends)])
    return before, after


def shifted(value, lane):
    width = value.shape[-1]
    ahead = jnp.where(lane == width - 1, 0.0, pltpu.roll(value, width - 1, 1))
    behind = jnp.where(lane == 0, 0.0, pltpu.roll(value, 1, 1))
    return jnp.concatenate([ahead, value, behind], axis=0)


def forward_kernel(planes, rows, at_ref, w_ref, bias_ref, cot, tiles, before, after, *refs):
    out_ref, face_ref, far_ref, kept_ref, grads, halves = refs
    cout, width = cot.shape[1:]
    sources = tiles.shape[0]
    edge = sources * (planes + 2)

    def tile(s, p, t):
        if t == 0:
            return before[s * (planes + 2) + p]
        if t == rows // 2 + 1:
            return after[s * (planes + 2) + p]
        return tiles[s, p, t - 1]

    lane = lax.broadcasted_iota(jnp.int32, (cout, width), 1)
    bias = bias_ref[...]
    sums = [None] * 3
    bias_sum = jnp.zeros((cout, width), F32)
    for d in range(planes):
        for pair in range(rows // 2 + 1):
            cells = [
                jnp.concatenate(
                    [tile(s, d + kd, pair + t) for t in range(2) for s in range(sources)], axis=0
                )
                for kd in range(3)
            ]
            acc = jnp.dot(w_ref[0], cells[0], preferred_element_type=F32)
            for kd in range(1, 3):
                acc = acc + jnp.dot(w_ref[kd], cells[kd], preferred_element_type=F32)
            stacks = []
            for e in range(2):
                z = acc[3 * e * cout : 3 * (e + 1) * cout]
                pre = (
                    z[cout : 2 * cout]
                    + jnp.where(lane == 0, 0.0, pltpu.roll(z[:cout], 1, 1))
                    + jnp.where(lane == width - 1, 0.0, pltpu.roll(z[2 * cout :], width - 1, 1))
                    + bias
                )
                small = jnp.exp(-jnp.abs(pre))
                sigmoid = jnp.where(pre >= 0, 1.0, small) / (1.0 + small)
                row = 2 * pair + e
                if row == 0:
                    cotangent = before[edge + d]
                elif row == rows + 1:
                    cotangent = after[edge + d]
                else:
                    cotangent = cot[d * rows + row - 1]
                grad = (cotangent.astype(F32) * (0.2 + 0.8 * sigmoid)).astype(BF16)
                grads[d, row] = grad
                if row == 0 or row == rows + 1:
                    stacks.append(jnp.zeros((3 * cout, width), BF16))
                    continue
                softplus = jnp.maximum(pre, 0.0) + jnp.log1p(small)
                out_ref[d * rows + row - 1] = (0.2 * pre + 0.8 * softplus).astype(BF16)
                grad = grad.astype(F32)
                bias_sum = bias_sum + grad
                stacks.append(shifted(grad, lane).astype(BF16))
            both = jnp.concatenate(stacks, axis=0)
            for kd in range(3):
                term = lax.dot_general(
                    both, cells[kd], (((1,), (1,)), ((), ())), preferred_element_type=F32
                )
                sums[kd] = term if sums[kd] is None else sums[kd] + term

    even = (lane // PART) % 2 == 0
    blocks, last = [], []
    for kd in range(3):
        for kw in range(3):
            one = sums[kd][kw * cout : (kw + 1) * cout]
            two = sums[kd][(3 + kw) * cout : (4 + kw) * cout]
            back = pltpu.roll(two[:, width:], width - PART, 1)
            blocks.append(
                one[:, :width]
                + jnp.where(
                    even,
                    pltpu.roll(two[:, :width], width - PART, 1),
                    pltpu.roll(two[:, width:], PART, 1),
                )
            )
            last.append(one[:, width:] + back)
    last.append(jnp.broadcast_to(jnp.sum(bias_sum, axis=1, keepdims=True), (cout, width)))
    for k in range(0, len(last), 2):
        blocks.append(jnp.where(even, last[k], pltpu.roll(last[k + 1], PART, 1)))
    source = lax.broadcasted_iota(jnp.int32, (width, width), 0)
    target = (source // PART) % 2 * (width // 2) + source // (2 * PART) * PART + source % PART
    order = jnp.where(lax.broadcasted_iota(jnp.int32, (width, width), 1) == target, 1.0, 0.0).astype(BF16)
    placed = jnp.dot(jnp.concatenate(blocks, axis=0).astype(BF16), order, preferred_element_type=F32)
    count = len(blocks) // 2
    for k in range(2 * count):
        halves[k // count, k % count] = placed[k * cout : (k + 1) * cout].astype(BF16)
    core = at_ref[0]
    face_ref[: rows + 2] = grads[1 - core]
    face_ref[rows + 2 :] = halves[1 - core]
    far_ref[...] = grads[core]
    kept_ref[...] = halves[core]


def backward_kernel(planes, rows, at_ref, w_ref, face, far, face_in, far_in, kept_ref, sent_ref, stack, parts):
    cout, width = far.shape[1:]
    cin = w_ref.shape[0]
    count = 2 * parts.shape[1]
    part = cin // count
    lane = lax.broadcasted_iota(jnp.int32, (cout, width), 1)
    step = 3 * cout
    core = at_ref[0]
    for q, source in enumerate((face_in, face, far, far_in)):
        p = jnp.where(core == 1, q, planes + 1 - q)
        for r in range(rows + 2):
            stack[p, r * step : (r + 1) * step, :] = shifted(source[r].astype(F32), lane).astype(BF16)
    w = w_ref[...]
    for d in range(planes):
        for h in range(0, rows, 2):
            cells = jnp.concatenate(
                [
                    jnp.concatenate(
                        [stack[d + a, (h + e) * step : (h + e + 3) * step, :] for a in range(3)], axis=0
                    )
                    for e in range(2)
                ],
                axis=1,
            )
            acc = jnp.dot(w, cells, preferred_element_type=F32)
            pair = (d * rows + h) // 2
            for f in range(count):
                piece = acc[f * part : (f + 1) * part]
                piece = jnp.concatenate([piece[:, :width], piece[:, width:]], axis=0).astype(BF16)
                parts[(f % 2) ^ at_ref[1], (f // 2) ^ at_ref[2], pair] = piece
    kept_ref[...] = parts[0]
    sent_ref[...] = parts[1]


def placing(cin):
    ones = np.zeros((2, 3, cin, 2, cin // PART, 2, PART), np.float32)
    for e in range(2):
        for kh in range(3):
            for i in range(cin):
                ones[e, kh, i, (kh + e) // 2, i // PART, (kh + e) % 2, i % PART] = 1
    return ones.reshape(2, 3 * cin, 4 * cin)


def per_device(activations, weights, bias, cotangent):
    cin_dev, planes, rows, width = activations.shape
    taps, cin, cout = weights.shape
    cells = planes * rows
    depth, filt = lax.axis_size("depth"), lax.axis_size("filt")
    core = lax.axis_index("depth") % 2
    even = core == 0
    swap = [(i, i ^ 1) for i in range(depth)]
    cross = [(i, i - 1 if i % 2 == 0 else i + 1) for i in range(1, depth - 1)]
    mine = lax.axis_index("filt")
    at = jnp.stack([core, mine % 2, mine // 2]).astype(jnp.int32)
    struct = jax.ShapeDtypeStruct

    grid = activations.transpose(1, 2, 0, 3)
    face_in = lax.ppermute(jnp.where(even, grid[planes - 1], grid[0]), "depth", swap)
    far_in = lax.ppermute(jnp.where(even, grid[0], grid[planes - 1]), "depth", cross)
    low, high = jnp.where(even, far_in, face_in), jnp.where(even, face_in, far_in)
    grid = jnp.concatenate([low[None], grid, high[None]], axis=0)
    grid = grid.reshape(planes + 2, rows // 2, 2 * cin_dev, width)
    tiles = swapped(copies(grid, filt), "filt")

    cot = cotangent.transpose(1, 2, 0, 3)
    split = weights.reshape(3, 3, 3, cin, cout)
    w_forward = jnp.einsum(
        "akj,ejn->aekn",
        split.transpose(0, 2, 4, 1, 3).reshape(3, 3 * cout, 3 * cin),
        jnp.asarray(placing(cin), BF16),
        preferred_element_type=F32,
    )
    w_forward = w_forward.astype(BF16).reshape(3, 6 * cout, 4 * cin)
    wide = jnp.broadcast_to(bias[:, None], (cout, width))
    w_back = split[::-1, ::-1].transpose(3, 0, 1, 2, 4).reshape(cin, taps * cout)
    first = jnp.concatenate([tiles[:, :, 0].reshape(-1, 2 * cin_dev, width), cot[:, 0]], axis=0)
    last = jnp.concatenate([tiles[:, :, -1].reshape(-1, 2 * cin_dev, width), cot[:, rows - 1]], axis=0)
    cot = cot.reshape(cells, cout, width)
    first, last, cot, w_forward, wide = lax.optimization_barrier((first, last, cot, w_forward, wide))
    before, after = neighbours(first, last, "height")
    work = 2 * cells * width * taps * cin * cout
    count = (taps + 1) // 4
    smem, vmem = pl.BlockSpec(memory_space=pltpu.SMEM), pl.BlockSpec(memory_space=pltpu.VMEM)
    out, face, far, kept = pl.pallas_call(
        functools.partial(forward_kernel, planes, rows),
        out_shape=(
            struct((cells, cout, width), BF16),
            struct((rows + 2 + count, cout, width), BF16),
            struct((rows + 2, cout, width), BF16),
            struct((count, cout, width), BF16),
        ),
        in_specs=[smem] + [vmem] * 6,
        out_specs=(vmem,) * 4,
        compiler_params=pltpu.CompilerParams(vmem_limit_bytes=12 << 20),
        scratch_shapes=[
            pltpu.VMEM((planes, rows + 2, cout, width), BF16),
            pltpu.VMEM((2, count, cout, width), BF16),
        ],
        cost_estimate=pl.CostEstimate(flops=3 * work, bytes_accessed=1 << 20, transcendentals=1 << 17),
        name="forward",
    )(at, w_forward, wide, cot, tiles, before, after)
    output = out.reshape(planes, rows, cout, width).transpose(2, 0, 1, 3)

    face_in = lax.ppermute(face, "depth", swap)
    far_in = lax.ppermute(far, "depth", cross)
    total = (kept.astype(F32) + face_in[rows + 2 :].astype(F32)).astype(BF16)
    total = copies(total, lax.axis_size("height"))
    total = jnp.sum(swapped(total, "height").astype(F32), axis=0).astype(BF16)
    total = swapped(copies(total, depth), "depth").reshape((depth // 2, 2 * count) + total.shape[1:])
    total = jnp.sum(total.astype(F32), axis=0)
    first = total[:9].reshape(3, 3, cout, 2, cin).transpose(0, 3, 1, 2, 4)
    rest = total[9:].reshape(5, cout, 2, cin).transpose(0, 2, 1, 3).reshape(10, cout, cin)
    third = rest[:9].reshape(3, 1, 3, cout, cin)
    weight_grad = jnp.concatenate([first, third], axis=1).reshape(taps, cout, cin).transpose(0, 2, 1)
    bias_grad = rest[9, :, 0]

    kept, sent = pl.pallas_call(
        functools.partial(backward_kernel, planes, rows),
        out_shape=(struct((filt // 2, cells // 2, 2 * cin_dev, width), BF16),) * 2,
        in_specs=[smem] + [vmem] * 5,
        out_specs=(vmem,) * 2,
        compiler_params=pltpu.CompilerParams(vmem_limit_bytes=12 << 20),
        scratch_shapes=[
            pltpu.VMEM((planes + 2, (rows + 2) * 3 * cout, width), BF16),
            pltpu.VMEM((2, filt // 2, cells // 2, 2 * cin_dev, width), BF16),
        ],
        cost_estimate=pl.CostEstimate(flops=work, bytes_accessed=1 << 19, transcendentals=0),
        name="backward",
    )(at, w_back, face, far, face_in, far_in)
    pair = kept.astype(F32) + lax.ppermute(sent, "filt", [(i, i ^ 1) for i in range(filt)]).astype(F32)
    summed = pair[0]
    for k in range(1, filt // 2):
        moved = lax.ppermute(pair[k].astype(BF16), "filt", [(i, i ^ (2 * k)) for i in range(filt)])
        summed = summed + moved.astype(F32)
    summed = summed.astype(BF16).reshape(planes, rows, cin_dev, width).transpose(2, 0, 1, 3)
    return (output, summed, weight_grad, bias_grad)


def solution(mesh):
    placed = (
        P("filt", "depth", "height", None),
        P(None, None, "filt"),
        P("filt"),
        P("filt", "depth", "height", None),
    )
    return jax.shard_map(
        per_device,
        mesh=mesh,
        in_specs=placed,
        out_specs=(
            P("filt", "depth", "height", None),
            P("filt", "depth", "height", None),
            P(None, None, "filt"),
            P("filt"),
        ),
        check_vma=False,
    )
```

```python
import functools

import jax
import jax.numpy as jnp
import numpy as np
from jax import lax
from jax.experimental import pallas as pl
from jax.experimental.pallas import tpu as pltpu
from jax.sharding import PartitionSpec as P

BF16 = jnp.bfloat16
F32 = jnp.float32
PART = 8


def copies(block, count):
    return jnp.broadcast_to(block[None], (count,) + block.shape)


def swapped(blocks, axis):
    return lax.all_to_all(blocks, axis, 0, 0, tiled=True)


def neighbours(first, last, axis):
    ends = lax.axis_size(axis) - 1
    before = lax.ppermute(last, axis, [(i, i + 1) for i in range(ends)])
    after = lax.ppermute(first, axis, [(i + 1, i) for i in range(ends)])
    return before, after


def shifted(value, lane):
    width = value.shape[-1]
    ahead = jnp.where(lane == width - 1, 0.0, pltpu.roll(value, width - 1, 1))
    behind = jnp.where(lane == 0, 0.0, pltpu.roll(value, 1, 1))
    return jnp.concatenate([ahead, value, behind], axis=0)


def forward_kernel(planes, rows, at_ref, w_ref, bias_ref, cot, tiles, before, after, *refs):
    out_ref, face_ref, far_ref, kept_ref, grads, halves = refs
    cout, width = cot.shape[1:]
    sources = tiles.shape[0]
    edge = sources * (planes + 2)

    def tile(s, p, t):
        if t == 0:
            return before[s * (planes + 2) + p]
        if t == rows // 2 + 1:
            return after[s * (planes + 2) + p]
        return tiles[s, p, t - 1]

    lane = lax.broadcasted_iota(jnp.int32, (cout, width), 1)
    bias = bias_ref[...]
    sums = [None] * 3
    bias_sum = jnp.zeros((cout, width), F32)
    for d in range(planes):
        for pair in range(rows // 2 + 1):
            cells = [
                jnp.concatenate(
                    [tile(s, d + kd, pair + t) for t in range(2) for s in range(sources)], axis=0
                )
                for kd in range(3)
            ]
            acc = jnp.dot(w_ref[0], cells[0], preferred_element_type=F32)
            for kd in range(1, 3):
                acc = acc + jnp.dot(w_ref[kd], cells[kd], preferred_element_type=F32)
            stacks = []
            for e in range(2):
                z = acc[3 * e * cout : 3 * (e + 1) * cout]
                pre = (
                    z[cout : 2 * cout]
                    + jnp.where(lane == 0, 0.0, pltpu.roll(z[:cout], 1, 1))
                    + jnp.where(lane == width - 1, 0.0, pltpu.roll(z[2 * cout :], width - 1, 1))
                    + bias
                )
                small = jnp.exp(-jnp.abs(pre))
                sigmoid = jnp.where(pre >= 0, 1.0, small) / (1.0 + small)
                row = 2 * pair + e
                if row == 0:
                    cotangent = before[edge + d]
                elif row == rows + 1:
                    cotangent = after[edge + d]
                else:
                    cotangent = cot[d * rows + row - 1]
                grad = (cotangent.astype(F32) * (0.2 + 0.8 * sigmoid)).astype(BF16)
                grads[d, row] = grad
                if row == 0 or row == rows + 1:
                    stacks.append(jnp.zeros((3 * cout, width), BF16))
                    continue
                softplus = jnp.maximum(pre, 0.0) + jnp.log1p(small)
                out_ref[d * rows + row - 1] = (0.2 * pre + 0.8 * softplus).astype(BF16)
                grad = grad.astype(F32)
                bias_sum = bias_sum + grad
                stacks.append(shifted(grad, lane).astype(BF16))
            both = jnp.concatenate(stacks, axis=0)
            for kd in range(3):
                term = lax.dot_general(
                    both, cells[kd], (((1,), (1,)), ((), ())), preferred_element_type=F32
                )
                sums[kd] = term if sums[kd] is None else sums[kd] + term

    even = (lane // PART) % 2 == 0
    blocks, last = [], []
    for kd in range(3):
        for kw in range(3):
            one = sums[kd][kw * cout : (kw + 1) * cout]
            two = sums[kd][(3 + kw) * cout : (4 + kw) * cout]
            back = pltpu.roll(two[:, width:], width - PART, 1)
            blocks.append(
                one[:, :width]
                + jnp.where(
                    even,
                    pltpu.roll(two[:, :width], width - PART, 1),
                    pltpu.roll(two[:, width:], PART, 1),
                )
            )
            last.append(one[:, width:] + back)
    last.append(jnp.broadcast_to(jnp.sum(bias_sum, axis=1, keepdims=True), (cout, width)))
    for k in range(0, len(last), 2):
        blocks.append(jnp.where(even, last[k], pltpu.roll(last[k + 1], PART, 1)))
    source = lax.broadcasted_iota(jnp.int32, (width, width), 0)
    target = (source // PART) % 2 * (width // 2) + source // (2 * PART) * PART + source % PART
    order = jnp.where(lax.broadcasted_iota(jnp.int32, (width, width), 1) == target, 1.0, 0.0).astype(BF16)
    placed = jnp.dot(jnp.concatenate(blocks, axis=0).astype(BF16), order, preferred_element_type=F32)
    count = len(blocks) // 2
    for k in range(2 * count):
        halves[k // count, k % count] = placed[k * cout : (k + 1) * cout].astype(BF16)
    core = at_ref[0]
    face_ref[: rows + 2] = grads[1 - core]
    face_ref[rows + 2 :] = halves[1 - core]
    far_ref[...] = grads[core]
    kept_ref[...] = halves[core]


def backward_kernel(planes, rows, at_ref, w_ref, face, far, face_in, far_in, parts, stack):
    cout, width = far.shape[1:]
    cin = w_ref.shape[0]
    count = parts.shape[0]
    part = cin // count
    lane = lax.broadcasted_iota(jnp.int32, (cout, width), 1)
    step = 3 * cout
    core = at_ref[0]
    for q, source in enumerate((face_in, face, far, far_in)):
        p = jnp.where(core == 1, q, planes + 1 - q)
        for r in range(rows + 2):
            stack[p, r * step : (r + 1) * step, :] = shifted(source[r].astype(F32), lane).astype(BF16)
    w = w_ref[...]
    for d in range(planes):
        for h in range(0, rows, 2):
            cells = jnp.concatenate(
                [
                    jnp.concatenate(
                        [stack[d + a, (h + e) * step : (h + e + 3) * step, :] for a in range(3)], axis=0
                    )
                    for e in range(2)
                ],
                axis=1,
            )
            acc = jnp.dot(w, cells, preferred_element_type=F32)
            pair = (d * rows + h) // 2
            for f in range(count):
                piece = acc[f * part : (f + 1) * part]
                piece = jnp.concatenate([piece[:, :width], piece[:, width:]], axis=0).astype(BF16)
                parts[f, pair] = piece


def placing(cin):
    ones = np.zeros((2, 3, cin, 2, cin // PART, 2, PART), np.float32)
    for e in range(2):
        for kh in range(3):
            for i in range(cin):
                ones[e, kh, i, (kh + e) // 2, i // PART, (kh + e) % 2, i % PART] = 1
    return ones.reshape(2, 3 * cin, 4 * cin)


def per_device(activations, weights, bias, cotangent):
    cin_dev, planes, rows, width = activations.shape
    taps, cin, cout = weights.shape
    cells = planes * rows
    depth, filt = lax.axis_size("depth"), lax.axis_size("filt")
    core = lax.axis_index("depth") % 2
    even = core == 0
    swap = [(i, i ^ 1) for i in range(depth)]
    cross = [(i, i - 1 if i % 2 == 0 else i + 1) for i in range(1, depth - 1)]
    at = core.astype(jnp.int32).reshape(1)
    struct = jax.ShapeDtypeStruct

    grid = activations.transpose(1, 2, 0, 3)
    face_in = lax.ppermute(jnp.where(even, grid[planes - 1], grid[0]), "depth", swap)
    far_in = lax.ppermute(jnp.where(even, grid[0], grid[planes - 1]), "depth", cross)
    low, high = jnp.where(even, far_in, face_in), jnp.where(even, face_in, far_in)
    grid = jnp.concatenate([low[None], grid, high[None]], axis=0)
    grid = grid.reshape(planes + 2, rows // 2, 2 * cin_dev, width)
    tiles = swapped(copies(grid, filt), "filt")

    cot = cotangent.transpose(1, 2, 0, 3)
    split = weights.reshape(3, 3, 3, cin, cout)
    w_forward = jnp.einsum(
        "akj,ejn->aekn",
        split.transpose(0, 2, 4, 1, 3).reshape(3, 3 * cout, 3 * cin),
        jnp.asarray(placing(cin), BF16),
        preferred_element_type=F32,
    )
    w_forward = w_forward.astype(BF16).reshape(3, 6 * cout, 4 * cin)
    wide = jnp.broadcast_to(bias[:, None], (cout, width))
    w_back = split[::-1, ::-1].transpose(3, 0, 1, 2, 4).reshape(cin, taps * cout)
    first = jnp.concatenate([tiles[:, :, 0].reshape(-1, 2 * cin_dev, width), cot[:, 0]], axis=0)
    last = jnp.concatenate([tiles[:, :, -1].reshape(-1, 2 * cin_dev, width), cot[:, rows - 1]], axis=0)
    cot = cot.reshape(cells, cout, width)
    first, last, cot, w_forward, wide = lax.optimization_barrier((first, last, cot, w_forward, wide))
    before, after = neighbours(first, last, "height")
    work = 2 * cells * width * taps * cin * cout
    count = (taps + 1) // 4
    smem, vmem = pl.BlockSpec(memory_space=pltpu.SMEM), pl.BlockSpec(memory_space=pltpu.VMEM)
    out, face, far, kept = pl.pallas_call(
        functools.partial(forward_kernel, planes, rows),
        out_shape=(
            struct((cells, cout, width), BF16),
            struct((rows + 2 + count, cout, width), BF16),
            struct((rows + 2, cout, width), BF16),
            struct((count, cout, width), BF16),
        ),
        in_specs=[smem] + [vmem] * 6,
        out_specs=(vmem,) * 4,
        compiler_params=pltpu.CompilerParams(vmem_limit_bytes=12 << 20),
        scratch_shapes=[
            pltpu.VMEM((planes, rows + 2, cout, width), BF16),
            pltpu.VMEM((2, count, cout, width), BF16),
        ],
        cost_estimate=pl.CostEstimate(flops=3 * work, bytes_accessed=1 << 20, transcendentals=1 << 17),
        name="forward",
    )(at, w_forward, wide, cot, tiles, before, after)
    output = out.reshape(planes, rows, cout, width).transpose(2, 0, 1, 3)

    face_in = lax.ppermute(face, "depth", swap)
    far_in = lax.ppermute(far, "depth", cross)
    total = (kept.astype(F32) + face_in[rows + 2 :].astype(F32)).astype(BF16)
    total = copies(total, lax.axis_size("height"))
    total = jnp.sum(swapped(total, "height").astype(F32), axis=0).astype(BF16)
    total = swapped(copies(total, depth), "depth")

    parts = pl.pallas_call(
        functools.partial(backward_kernel, planes, rows),
        out_shape=struct((filt, cells // 2, 2 * cin_dev, width), BF16),
        in_specs=[smem] + [vmem] * 5,
        out_specs=vmem,
        compiler_params=pltpu.CompilerParams(vmem_limit_bytes=12 << 20),
        scratch_shapes=[pltpu.VMEM((planes + 2, (rows + 2) * 3 * cout, width), BF16)],
        cost_estimate=pl.CostEstimate(flops=work, bytes_accessed=1 << 19, transcendentals=0),
        name="backward",
    )(at, w_back, face, far, face_in, far_in)
    parts, total = lax.optimization_barrier((parts, total))
    summed = jnp.sum(swapped(parts, "filt").astype(F32), axis=0).astype(BF16)
    summed = summed.reshape(planes, rows, cin_dev, width).transpose(2, 0, 1, 3)

    total = total.reshape(depth // 2, 2 * count, cout, width)
    total = jnp.sum(total.astype(F32), axis=0)
    first = total[:9].reshape(3, 3, cout, 2, cin).transpose(0, 3, 1, 2, 4)
    rest = total[9:].reshape(5, cout, 2, cin).transpose(0, 2, 1, 3).reshape(10, cout, cin)
    third = rest[:9].reshape(3, 1, 3, cout, cin)
    weight_grad = jnp.concatenate([first, third], axis=1).reshape(taps, cout, cin).transpose(0, 2, 1)
    bias_grad = rest[9, :, 0]

    return (output, summed, weight_grad, bias_grad)


def solution(mesh):
    placed = (
        P("filt", "depth", "height", None),
        P(None, None, "filt"),
        P("filt"),
        P("filt", "depth", "height", None),
    )
    return jax.shard_map(
        per_device,
        mesh=mesh,
        in_specs=placed,
        out_specs=(
            P("filt", "depth", "height", None),
            P("filt", "depth", "height", None),
            P(None, None, "filt"),
            P("filt"),
        ),
        check_vma=False,
    )
```

```python
import functools

import jax
import jax.numpy as jnp
import numpy as np
from jax import lax
from jax.experimental import pallas as pl
from jax.experimental.pallas import tpu as pltpu
from jax.sharding import PartitionSpec as P

BF16 = jnp.bfloat16
F32 = jnp.float32
PART = 8


def copies(block, count):
    return jnp.broadcast_to(block[None], (count,) + block.shape)


def swapped(blocks, axis):
    return lax.all_to_all(blocks, axis, 0, 0, tiled=True)


def neighbours(first, last, axis):
    ends = lax.axis_size(axis) - 1
    before = lax.ppermute(last, axis, [(i, i + 1) for i in range(ends)])
    after = lax.ppermute(first, axis, [(i + 1, i) for i in range(ends)])
    return before, after


def shifted(value, lane):
    width = value.shape[-1]
    ahead = jnp.where(lane == width - 1, 0.0, pltpu.roll(value, width - 1, 1))
    behind = jnp.where(lane == 0, 0.0, pltpu.roll(value, 1, 1))
    return jnp.concatenate([ahead, value, behind], axis=0)


def planes_kernel(planes, at_ref, tiles, face_ref, far_ref):
    core = at_ref[0]
    face_ref[...] = tiles[:, jnp.where(core == 0, planes - 1, 0)]
    far_ref[...] = tiles[:, jnp.where(core == 0, 0, planes - 1)]


def rows_kernel(planes, rows, at_ref, tiles, facing, beyond, cot, first_ref, last_ref):
    core = at_ref[0]
    sources = tiles.shape[0]
    before = jnp.where(core == 0, 0, (planes + 1) * sources)
    after = (planes + 1) * sources - before
    for ref, t, row in ((first_ref, 0, 0), (last_ref, rows // 2 - 1, rows - 1)):
        ref[pl.ds(before, sources)] = beyond[:, t]
        ref[pl.ds(after, sources)] = facing[:, t]
        for d in range(planes):
            ref[(d + 1) * sources : (d + 2) * sources] = tiles[:, d, t]
            ref[(planes + 2) * sources + d] = cot[d * rows + row]


def forward_kernel(planes, rows, at_ref, bias_ref, w_ref, cot, tiles, facing, beyond, before, after, *refs):
    out_ref, face_ref, far_ref, kept_ref, grads, halves = refs
    cout, width = cot.shape[1:]
    sources = tiles.shape[0]
    edge = sources * (planes + 2)
    core = at_ref[0]
    even = core == 0

    def tile(s, p, t):
        if t == 0:
            return before[p * sources + s]
        if t == rows // 2 + 1:
            return after[p * sources + s]
        if p == 0:
            return jnp.where(even, beyond[s, t - 1], facing[s, t - 1])
        if p == planes + 1:
            return jnp.where(even, facing[s, t - 1], beyond[s, t - 1])
        return tiles[s, p - 1, t - 1]

    lane = lax.broadcasted_iota(jnp.int32, (cout, width), 1)
    channel = lax.broadcasted_iota(jnp.int32, (cout, width), 0)
    bias = jnp.zeros((cout, width), F32)
    for o in range(cout):
        bias = jnp.where(channel == o, bias_ref[o], bias)
    sums = [None] * 3
    bias_sum = jnp.zeros((cout, width), F32)
    for d in range(planes):
        for pair in range(rows // 2 + 1):
            cells = [
                jnp.concatenate(
                    [tile(s, d + kd, pair + t) for t in range(2) for s in range(sources)], axis=0
                )
                for kd in range(3)
            ]
            acc = jnp.dot(w_ref[0], cells[0], preferred_element_type=F32)
            for kd in range(1, 3):
                acc = acc + jnp.dot(w_ref[kd], cells[kd], preferred_element_type=F32)
            stacks = []
            for e in range(2):
                z = acc[3 * e * cout : 3 * (e + 1) * cout]
                pre = (
                    z[cout : 2 * cout]
                    + jnp.where(lane == 0, 0.0, pltpu.roll(z[:cout], 1, 1))
                    + jnp.where(lane == width - 1, 0.0, pltpu.roll(z[2 * cout :], width - 1, 1))
                    + bias
                )
                small = jnp.exp(-jnp.abs(pre))
                sigmoid = jnp.where(pre >= 0, 1.0, small) / (1.0 + small)
                row = 2 * pair + e
                if row == 0:
                    cotangent = before[edge + d]
                elif row == rows + 1:
                    cotangent = after[edge + d]
                else:
                    cotangent = cot[d * rows + row - 1]
                grad = (cotangent.astype(F32) * (0.2 + 0.8 * sigmoid)).astype(BF16)
                grads[d, row] = grad
                if row == 0 or row == rows + 1:
                    stacks.append(jnp.zeros((3 * cout, width), BF16))
                    continue
                softplus = jnp.maximum(pre, 0.0) + jnp.log1p(small)
                out_ref[d * rows + row - 1] = (0.2 * pre + 0.8 * softplus).astype(BF16)
                grad = grad.astype(F32)
                bias_sum = bias_sum + grad
                stacks.append(shifted(grad, lane).astype(BF16))
            both = jnp.concatenate(stacks, axis=0)
            for kd in range(3):
                term = lax.dot_general(
                    both, cells[kd], (((1,), (1,)), ((), ())), preferred_element_type=F32
                )
                sums[kd] = term if sums[kd] is None else sums[kd] + term

    first = (lane // PART) % 2 == 0
    blocks, last = [], []
    for kd in range(3):
        for kw in range(3):
            one = sums[kd][kw * cout : (kw + 1) * cout]
            two = sums[kd][(3 + kw) * cout : (4 + kw) * cout]
            back = pltpu.roll(two[:, width:], width - PART, 1)
            blocks.append(
                one[:, :width]
                + jnp.where(
                    first,
                    pltpu.roll(two[:, :width], width - PART, 1),
                    pltpu.roll(two[:, width:], PART, 1),
                )
            )
            last.append(one[:, width:] + back)
    last.append(jnp.broadcast_to(jnp.sum(bias_sum, axis=1, keepdims=True), (cout, width)))
    for k in range(0, len(last), 2):
        blocks.append(jnp.where(first, last[k], pltpu.roll(last[k + 1], PART, 1)))
    source = lax.broadcasted_iota(jnp.int32, (width, width), 0)
    target = (source // PART) % 2 * (width // 2) + source // (2 * PART) * PART + source % PART
    order = jnp.where(lax.broadcasted_iota(jnp.int32, (width, width), 1) == target, 1.0, 0.0).astype(BF16)
    placed = jnp.dot(jnp.concatenate(blocks, axis=0).astype(BF16), order, preferred_element_type=F32)
    count = len(blocks) // 2
    for k in range(2 * count):
        halves[k // count, k % count] = placed[k * cout : (k + 1) * cout].astype(BF16)
    face_ref[: rows + 2] = grads[1 - core]
    face_ref[rows + 2 :] = halves[1 - core]
    far_ref[...] = grads[core]
    kept_ref[...] = halves[core]


def backward_kernel(planes, rows, at_ref, w_ref, face, far, face_in, far_in, parts, stack):
    cout, width = far.shape[1:]
    cin = w_ref.shape[0]
    count = parts.shape[0]
    part = cin // count
    lane = lax.broadcasted_iota(jnp.int32, (cout, width), 1)
    step = 3 * cout
    core = at_ref[0]
    for q, source in enumerate((face_in, face, far, far_in)):
        p = jnp.where(core == 1, q, planes + 1 - q)
        for r in range(rows + 2):
            stack[p, r * step : (r + 1) * step, :] = shifted(source[r].astype(F32), lane).astype(BF16)
    w = w_ref[...]
    for d in range(planes):
        for h in range(0, rows, 2):
            cells = jnp.concatenate(
                [
                    jnp.concatenate(
                        [stack[d + a, (h + e) * step : (h + e + 3) * step, :] for a in range(3)], axis=0
                    )
                    for e in range(2)
                ],
                axis=1,
            )
            acc = jnp.dot(w, cells, preferred_element_type=F32)
            pair = (d * rows + h) // 2
            for f in range(count):
                piece = acc[f * part : (f + 1) * part]
                piece = jnp.concatenate([piece[:, :width], piece[:, width:]], axis=0).astype(BF16)
                parts[f, pair] = piece


def placing(cin):
    ones = np.zeros((2, 3, cin, 2, cin // PART, 2, PART), np.float32)
    for e in range(2):
        for kh in range(3):
            for i in range(cin):
                ones[e, kh, i, (kh + e) // 2, i // PART, (kh + e) % 2, i % PART] = 1
    return ones.reshape(2, 3 * cin, 4 * cin)


def per_device(activations, weights, bias, cotangent):
    cin_dev, planes, rows, width = activations.shape
    taps, cin, cout = weights.shape
    cells = planes * rows
    depth, filt = lax.axis_size("depth"), lax.axis_size("filt")
    core = lax.axis_index("depth") % 2
    swap = [(i, i ^ 1) for i in range(depth)]
    cross = [(i, i - 1 if i % 2 == 0 else i + 1) for i in range(1, depth - 1)]
    at = core.astype(jnp.int32).reshape(1)
    struct = jax.ShapeDtypeStruct

    grid = activations.transpose(1, 2, 0, 3).reshape(planes, rows // 2, 2 * cin_dev, width)
    tiles = swapped(copies(grid, filt), "filt")
    smem, vmem = pl.BlockSpec(memory_space=pltpu.SMEM), pl.BlockSpec(memory_space=pltpu.VMEM)
    grant = pltpu.CompilerParams(vmem_limit_bytes=12 << 20)
    face, far = pl.pallas_call(
        functools.partial(planes_kernel, planes),
        out_shape=(struct((filt, rows // 2, 2 * cin_dev, width), BF16),) * 2,
        in_specs=[smem, vmem],
        out_specs=(vmem,) * 2,
        compiler_params=grant,
        cost_estimate=pl.CostEstimate(flops=0, bytes_accessed=1 << 19, transcendentals=0),
        name="planes",
    )(at, tiles)
    facing = lax.ppermute(face, "depth", swap)
    beyond = lax.ppermute(far, "depth", cross)

    cot = cotangent.transpose(1, 2, 0, 3)
    split = weights.reshape(3, 3, 3, cin, cout)
    w_forward = jnp.einsum(
        "akj,ejn->aekn",
        split.transpose(0, 2, 4, 1, 3).reshape(3, 3 * cout, 3 * cin),
        jnp.asarray(placing(cin), BF16),
        preferred_element_type=F32,
    )
    w_forward = w_forward.astype(BF16).reshape(3, 6 * cout, 4 * cin)
    w_back = split[::-1, ::-1].transpose(3, 0, 1, 2, 4).reshape(cin, taps * cout)
    cot = cot.reshape(cells, cout, width)
    first, last = pl.pallas_call(
        functools.partial(rows_kernel, planes, rows),
        out_shape=(struct(((planes + 2) * filt + planes, cout, width), BF16),) * 2,
        in_specs=[smem] + [vmem] * 4,
        out_specs=(vmem,) * 2,
        compiler_params=grant,
        cost_estimate=pl.CostEstimate(flops=0, bytes_accessed=1 << 19, transcendentals=0),
        name="rows",
    )(at, tiles, facing, beyond, cot)
    first, last, w_forward = lax.optimization_barrier((first, last, w_forward))
    before, after = neighbours(first, last, "height")
    work = 2 * cells * width * taps * cin * cout
    count = (taps + 1) // 4
    out, face, far, kept = pl.pallas_call(
        functools.partial(forward_kernel, planes, rows),
        out_shape=(
            struct((cells, cout, width), BF16),
            struct((rows + 2 + count, cout, width), BF16),
            struct((rows + 2, cout, width), BF16),
            struct((count, cout, width), BF16),
        ),
        in_specs=[smem] * 2 + [vmem] * 7,
        out_specs=(vmem,) * 4,
        compiler_params=grant,
        scratch_shapes=[
            pltpu.VMEM((planes, rows + 2, cout, width), BF16),
            pltpu.VMEM((2, count, cout, width), BF16),
        ],
        cost_estimate=pl.CostEstimate(flops=3 * work, bytes_accessed=1 << 20, transcendentals=1 << 17),
        name="forward",
    )(at, bias, w_forward, cot, tiles, facing, beyond, before, after)
    output = out.reshape(planes, rows, cout, width).transpose(2, 0, 1, 3)

    face_in = lax.ppermute(face, "depth", swap)
    far_in = lax.ppermute(far, "depth", cross)
    total = (kept.astype(F32) + face_in[rows + 2 :].astype(F32)).astype(BF16)
    total = swapped(copies(total, lax.axis_size("height")), "height")

    parts = pl.pallas_call(
        functools.partial(backward_kernel, planes, rows),
        out_shape=struct((filt, cells // 2, 2 * cin_dev, width), BF16),
        in_specs=[smem] + [vmem] * 5,
        out_specs=vmem,
        compiler_params=grant,
        scratch_shapes=[pltpu.VMEM((planes + 2, (rows + 2) * 3 * cout, width), BF16)],
        cost_estimate=pl.CostEstimate(flops=work, bytes_accessed=1 << 19, transcendentals=0),
        name="backward",
    )(at, w_back, face, far, face_in, far_in)
    parts, total = lax.optimization_barrier((parts, total))
    total = jnp.sum(total.astype(F32), axis=0).astype(BF16)
    total = swapped(copies(total, depth), "depth")
    parts, total = lax.optimization_barrier((parts, total))
    summed = jnp.sum(swapped(parts, "filt").astype(F32), axis=0).astype(BF16)
    summed = summed.reshape(planes, rows, cin_dev, width).transpose(2, 0, 1, 3)

    total = total.reshape(depth // 2, 2 * count, cout, width)
    total = jnp.sum(total.astype(F32), axis=0)
    first = total[:9].reshape(3, 3, cout, 2, cin).transpose(0, 3, 1, 2, 4)
    rest = total[9:].reshape(5, cout, 2, cin).transpose(0, 2, 1, 3).reshape(10, cout, cin)
    third = rest[:9].reshape(3, 1, 3, cout, cin)
    weight_grad = jnp.concatenate([first, third], axis=1).reshape(taps, cout, cin).transpose(0, 2, 1)
    bias_grad = rest[9, :, 0]

    return (output, summed, weight_grad, bias_grad)


def solution(mesh):
    placed = (
        P("filt", "depth", "height", None),
        P(None, None, "filt"),
        P("filt"),
        P("filt", "depth", "height", None),
    )
    return jax.shard_map(
        per_device,
        mesh=mesh,
        in_specs=placed,
        out_specs=(
            P("filt", "depth", "height", None),
            P("filt", "depth", "height", None),
            P(None, None, "filt"),
            P("filt"),
        ),
        check_vma=False,
    )
```

```python
import functools

import jax
import jax.numpy as jnp
import numpy as np
from jax import lax
from jax.experimental import pallas as pl
from jax.experimental.pallas import tpu as pltpu
from jax.sharding import PartitionSpec as P

BF16 = jnp.bfloat16
F32 = jnp.float32
PART = 8


def swapped(blocks, axis):
    return lax.all_to_all(blocks, axis, 0, 0, tiled=True)


def neighbours(first, last, axis):
    ends = lax.axis_size(axis) - 1
    before = lax.ppermute(last, axis, [(i, i + 1) for i in range(ends)])
    after = lax.ppermute(first, axis, [(i + 1, i) for i in range(ends)])
    return before, after


def shifted(value, lane):
    width = value.shape[-1]
    ahead = jnp.where(lane == width - 1, 0.0, pltpu.roll(value, width - 1, 1))
    behind = jnp.where(lane == 0, 0.0, pltpu.roll(value, 1, 1))
    return jnp.concatenate([ahead, value, behind], axis=0)


def pack_kernel(at_ref, cells, own, face_ref, far_ref, wide):
    planes, pairs = own.shape[:2]
    count, lines = cells.shape[:2]
    for c in range(count):
        wide[c * lines : (c + 1) * lines] = cells[c].astype(F32)
    for d in range(planes):
        for t in range(pairs):
            row = 2 * (d * pairs + t)
            own[d, t] = jnp.concatenate(
                [wide[pl.ds(row + e, count, stride=lines), :] for e in range(2)], axis=0
            ).astype(BF16)
    even = at_ref[0] == 0
    face_ref[...] = own[jnp.where(even, planes - 1, 0)]
    far_ref[...] = own[jnp.where(even, 0, planes - 1)]


def grid_kernel(at_ref, own, facing, beyond, out_ref):
    planes = own.shape[0]
    before = jnp.where(at_ref[0] == 0, 0, planes + 1)
    for k in range(out_ref.shape[0]):
        for d in range(planes):
            out_ref[k, d + 1] = own[d]
        out_ref[k, before] = beyond[...]
        out_ref[k, planes + 1 - before] = facing[...]


def rows_kernel(rows, tiles, cot, first_ref, last_ref):
    sources, count = tiles.shape[:2]
    for ref, t, row in ((first_ref, 0, 0), (last_ref, rows // 2 - 1, rows - 1)):
        for p in range(count):
            ref[p * sources : (p + 1) * sources] = tiles[:, p, t]
        for d in range(count - 2):
            ref[count * sources + d] = cot[d * rows + row]


def sum_kernel(blocks, out_ref):
    for r in range(blocks.shape[1]):
        total = blocks[0, r].astype(F32)
        for k in range(1, blocks.shape[0]):
            total = total + blocks[k, r].astype(F32)
        for k in range(out_ref.shape[0]):
            out_ref[k, r] = total.astype(BF16)


def add_kernel(left, right, out_ref):
    for k in range(left.shape[0]):
        out_ref[k] = (left[k].astype(F32) + right[k].astype(F32)).astype(BF16)


def unpack_kernel(parts, out_ref, wide):
    pairs, size = parts.shape[1:3]
    count, lines = out_ref.shape[:2]
    for t in range(pairs):
        total = parts[0, t].astype(F32)
        for k in range(1, parts.shape[0]):
            total = total + parts[k, t].astype(F32)
        wide[t * size : (t + 1) * size] = total
    for c in range(count):
        out_ref[c] = wide[pl.ds(c, lines, stride=count), :].astype(BF16)


def forward_kernel(planes, rows, at_ref, bias_ref, w_ref, cot, tiles, before, after, *refs):
    out_ref, face_ref, far_ref, sums_ref, grads = refs
    cout, width = cot.shape[1:]
    sources = tiles.shape[0]
    edge = sources * (planes + 2)

    def tile(s, p, t):
        if t == 0:
            return before[p * sources + s]
        if t == rows // 2 + 1:
            return after[p * sources + s]
        return tiles[s, p, t - 1]

    lane = lax.broadcasted_iota(jnp.int32, (cout, width), 1)
    channel = lax.broadcasted_iota(jnp.int32, (cout, width), 0)
    bias = jnp.zeros((cout, width), F32)
    for o in range(cout):
        bias = jnp.where(channel == o, bias_ref[o], bias)
    sums = [None] * 3
    bias_sum = jnp.zeros((cout, width), F32)
    for d in range(planes):
        for pair in range(rows // 2 + 1):
            cells = [
                jnp.concatenate(
                    [tile(s, d + kd, pair + t) for t in range(2) for s in range(sources)], axis=0
                )
                for kd in range(3)
            ]
            acc = jnp.dot(w_ref[0], cells[0], preferred_element_type=F32)
            for kd in range(1, 3):
                acc = acc + jnp.dot(w_ref[kd], cells[kd], preferred_element_type=F32)
            stacks = []
            for e in range(2):
                z = acc[3 * e * cout : 3 * (e + 1) * cout]
                pre = (
                    z[cout : 2 * cout]
                    + jnp.where(lane == 0, 0.0, pltpu.roll(z[:cout], 1, 1))
                    + jnp.where(lane == width - 1, 0.0, pltpu.roll(z[2 * cout :], width - 1, 1))
                    + bias
                )
                small = jnp.exp(-jnp.abs(pre))
                sigmoid = jnp.where(pre >= 0, 1.0, small) / (1.0 + small)
                row = 2 * pair + e
                if row == 0:
                    cotangent = before[edge + d]
                elif row == rows + 1:
                    cotangent = after[edge + d]
                else:
                    cotangent = cot[d * rows + row - 1]
                grad = (cotangent.astype(F32) * (0.2 + 0.8 * sigmoid)).astype(BF16)
                grads[d, row] = grad
                if row == 0 or row == rows + 1:
                    stacks.append(jnp.zeros((3 * cout, width), BF16))
                    continue
                softplus = jnp.maximum(pre, 0.0) + jnp.log1p(small)
                out_ref[d * rows + row - 1] = (0.2 * pre + 0.8 * softplus).astype(BF16)
                grad = grad.astype(F32)
                bias_sum = bias_sum + grad
                stacks.append(shifted(grad, lane).astype(BF16))
            both = jnp.concatenate(stacks, axis=0)
            for kd in range(3):
                term = lax.dot_general(
                    both, cells[kd], (((1,), (1,)), ((), ())), preferred_element_type=F32
                )
                sums[kd] = term if sums[kd] is None else sums[kd] + term

    first = (lane // PART) % 2 == 0
    blocks, last = [], []
    for kd in range(3):
        for kw in range(3):
            one = sums[kd][kw * cout : (kw + 1) * cout]
            two = sums[kd][(3 + kw) * cout : (4 + kw) * cout]
            back = pltpu.roll(two[:, width:], width - PART, 1)
            blocks.append(
                one[:, :width]
                + jnp.where(
                    first,
                    pltpu.roll(two[:, :width], width - PART, 1),
                    pltpu.roll(two[:, width:], PART, 1),
                )
            )
            last.append(one[:, width:] + back)
    last.append(jnp.broadcast_to(jnp.sum(bias_sum, axis=1, keepdims=True), (cout, width)))
    for k in range(0, len(last), 2):
        blocks.append(jnp.where(first, last[k], pltpu.roll(last[k + 1], PART, 1)))
    source = lax.broadcasted_iota(jnp.int32, (width, width), 0)
    target = (source // PART) % 2 * (width // 2) + source // (2 * PART) * PART + source % PART
    order = jnp.where(lax.broadcasted_iota(jnp.int32, (width, width), 1) == target, 1.0, 0.0).astype(BF16)
    placed = jnp.dot(jnp.concatenate(blocks, axis=0).astype(BF16), order, preferred_element_type=F32)
    size = sums_ref.shape[1]
    for k in range(sums_ref.shape[0] * size):
        block = placed[k * cout : (k + 1) * cout] if k < len(blocks) else jnp.zeros((cout, width), F32)
        sums_ref[k // size, k % size] = block.astype(BF16)
    core = at_ref[0]
    face_ref[...] = grads[1 - core]
    far_ref[...] = grads[core]


def backward_kernel(planes, rows, at_ref, w_ref, face, far, face_in, far_in, kept_ref, sent_ref, stack, parts):
    cout, width = far.shape[1:]
    cin = w_ref.shape[0]
    count = 2 * parts.shape[1]
    part = cin // count
    lane = lax.broadcasted_iota(jnp.int32, (cout, width), 1)
    step = 3 * cout
    core = at_ref[0]
    for q, source in enumerate((face_in, face, far, far_in)):
        p = jnp.where(core == 1, q, planes + 1 - q)
        for r in range(rows + 2):
            stack[p, r * step : (r + 1) * step, :] = shifted(source[r].astype(F32), lane).astype(BF16)
    w = w_ref[...]
    for d in range(planes):
        for h in range(0, rows, 2):
            cells = jnp.concatenate(
                [
                    jnp.concatenate(
                        [stack[d + a, (h + e) * step : (h + e + 3) * step, :] for a in range(3)], axis=0
                    )
                    for e in range(2)
                ],
                axis=1,
            )
            acc = jnp.dot(w, cells, preferred_element_type=F32)
            pair = (d * rows + h) // 2
            for f in range(count):
                piece = acc[f * part : (f + 1) * part]
                piece = jnp.concatenate([piece[:, :width], piece[:, width:]], axis=0).astype(BF16)
                parts[(f % 2) ^ at_ref[1], f // 2, pair] = piece
    kept_ref[...] = parts[0]
    sent_ref[...] = parts[1]


def placing(cin):
    ones = np.zeros((2, 3, cin, 2, cin // PART, 2, PART), np.float32)
    for e in range(2):
        for kh in range(3):
            for i in range(cin):
                ones[e, kh, i, (kh + e) // 2, i // PART, (kh + e) % 2, i % PART] = 1
    return ones.reshape(2, 3 * cin, 4 * cin)


def weights_kernel(blocks, w_ref, b_ref):
    cout, width = blocks.shape[2:]
    half = width // 2
    size = blocks.shape[1]
    for k in range(14):
        block = blocks[k // size, k % size].astype(F32)
        for e in range(2):
            piece = block[:, e * half : (e + 1) * half]
            at, kh = (k, e) if k < 9 else (2 * (k - 9) + e, 2)
            if at < 9:
                w_ref[at // 3 * 9 + kh * 3 + at % 3] = piece
    spare = blocks[13 // size, 13 % size].astype(F32)[:, half : half + cout]
    row = lax.broadcasted_iota(jnp.int32, (cout, cout), 0)
    lane = lax.broadcasted_iota(jnp.int32, (cout, cout), 1)
    b_ref[...] = jnp.sum(jnp.where(row == lane, spare, 0.0), axis=0, keepdims=True)


def call(body, name, *args, out, scratch=(), dtype=BF16, flops=0, moved=1 << 18, waves=0, scalars=0):
    smem, vmem = pl.BlockSpec(memory_space=pltpu.SMEM), pl.BlockSpec(memory_space=pltpu.VMEM)
    outs = tuple(jax.ShapeDtypeStruct(shape, dtype) for shape in out)
    results = pl.pallas_call(
        body,
        out_shape=outs,
        in_specs=[smem] * scalars + [vmem] * (len(args) - scalars),
        out_specs=(vmem,) * len(outs),
        scratch_shapes=[pltpu.VMEM(shape, kind) for shape, kind in scratch],
        compiler_params=pltpu.CompilerParams(vmem_limit_bytes=12 << 20),
        cost_estimate=pl.CostEstimate(flops=flops, bytes_accessed=moved, transcendentals=waves),
        name=name,
    )(*args)
    return results[0] if len(outs) == 1 else results


def per_device(activations, weights, bias, cotangent):
    cin_dev, planes, rows, width = activations.shape
    taps, cin, cout = weights.shape
    cells = planes * rows
    depth, height, filt = (lax.axis_size(axis) for axis in ("depth", "height", "filt"))
    swap = [(i, i ^ 1) for i in range(depth)]
    cross = [(i, i - 1 if i % 2 == 0 else i + 1) for i in range(1, depth - 1)]
    at = jnp.stack([lax.axis_index("depth") % 2, lax.axis_index("filt") % 2]).astype(jnp.int32)
    pairs, double = rows // 2, 2 * cin_dev

    own, face, far = call(
        pack_kernel,
        "pack",
        at,
        activations.reshape(cin_dev, cells, width),
        out=[(planes, pairs, double, width)] + [(pairs, double, width)] * 2,
        scratch=[((cin_dev * cells, width), F32)],
        scalars=1,
    )
    facing = lax.ppermute(face, "depth", swap)
    beyond = lax.ppermute(far, "depth", cross)
    grid = call(
        grid_kernel,
        "grid",
        at,
        own,
        facing,
        beyond,
        out=[(filt, planes + 2, pairs, double, width)],
        scalars=1,
    )
    tiles = swapped(grid, "filt")

    cot = cotangent.transpose(1, 2, 0, 3).reshape(cells, cout, width)
    split = weights.reshape(3, 3, 3, cin, cout)
    w_forward = jnp.einsum(
        "akj,ejn->aekn",
        split.transpose(0, 2, 4, 1, 3).reshape(3, 3 * cout, 3 * cin),
        jnp.asarray(placing(cin), BF16),
        preferred_element_type=F32,
    )
    w_forward = w_forward.astype(BF16).reshape(3, 6 * cout, 4 * cin)
    w_back = split[::-1, ::-1].transpose(3, 0, 1, 2, 4).reshape(cin, taps * cout)
    first, last = call(
        functools.partial(rows_kernel, rows),
        "rows",
        tiles,
        cot,
        out=[((planes + 2) * filt + planes, cout, width)] * 2,
    )
    first, last, w_forward = lax.optimization_barrier((first, last, w_forward))
    before, after = neighbours(first, last, "height")

    work = 2 * cells * width * taps * cin * cout
    out, face, far, sums = call(
        functools.partial(forward_kernel, planes, rows),
        "forward",
        at,
        bias,
        w_forward,
        cot,
        tiles,
        before,
        after,
        out=[(cells, cout, width)] + [(rows + 2, cout, width)] * 2 + [(height, 16 // height, cout, width)],
        scratch=[((planes, rows + 2, cout, width), BF16)],
        flops=3 * work,
        waves=1 << 17,
        scalars=2,
    )
    output = out.reshape(planes, rows, cout, width).transpose(2, 0, 1, 3)

    size = sums.shape[1:]
    face_in = lax.ppermute(face, "depth", swap)
    far_in = lax.ppermute(far, "depth", cross)
    sums = swapped(sums, "height")
    sums, face_in, far_in = lax.optimization_barrier((sums, face_in, far_in))
    sums = swapped(call(sum_kernel, "sums", sums, out=[(depth,) + size]), "depth")
    kept, sent = call(
        functools.partial(backward_kernel, planes, rows),
        "backward",
        at,
        w_back,
        face,
        far,
        face_in,
        far_in,
        out=[(filt // 2, cells // 2, double, width)] * 2,
        scratch=[
            ((planes + 2, (rows + 2) * 3 * cout, width), BF16),
            ((2, filt // 2, cells // 2, double, width), BF16),
        ],
        flops=work,
        scalars=1,
    )
    sums, kept, sent = lax.optimization_barrier((sums, kept, sent))
    sums = swapped(call(sum_kernel, "sums", sums, out=[(height,) + size]), "height")
    sent = lax.ppermute(sent, "filt", [(i, i ^ 1) for i in range(filt)])
    parts = call(add_kernel, "add", kept, sent, out=[kept.shape])
    sums, parts = lax.optimization_barrier((sums, parts))
    groups = [[i for i in range(filt) if i % 2 == k] for k in range(2)]
    parts = lax.all_to_all(parts, "filt", 0, 0, tiled=True, axis_index_groups=groups)
    summed = call(
        unpack_kernel,
        "unpack",
        parts,
        out=[(cin_dev, cells, width)],
        scratch=[((cin_dev * cells, width), F32)],
    ).reshape(activations.shape)

    weight_grad, bias_grad = call(
        weights_kernel, "weights", sums, out=[(taps, cout, cin), (1, cout)], dtype=F32
    )
    return (output, summed, weight_grad.transpose(0, 2, 1), bias_grad.reshape(cout))


def solution(mesh):
    placed = (
        P("filt", "depth", "height", None),
        P(None, None, "filt"),
        P("filt"),
        P("filt", "depth", "height", None),
    )
    return jax.shard_map(
        per_device,
        mesh=mesh,
        in_specs=placed,
        out_specs=(
            P("filt", "depth", "height", None),
            P("filt", "depth", "height", None),
            P(None, None, "filt"),
            P("filt"),
        ),
        check_vma=False,
    )
```

```python
import functools

import jax
import jax.numpy as jnp
import numpy as np
from jax import lax
from jax.experimental import pallas as pl
from jax.experimental.pallas import tpu as pltpu
from jax.sharding import PartitionSpec as P

BF16 = jnp.bfloat16
F32 = jnp.float32
PART = 8


def swapped(blocks, axis, groups=None):
    return lax.all_to_all(blocks, axis, 0, 0, tiled=True, axis_index_groups=groups)


def neighbours(first, last, axis):
    ends = lax.axis_size(axis) - 1
    before = lax.ppermute(last, axis, [(i, i + 1) for i in range(ends)])
    after = lax.ppermute(first, axis, [(i + 1, i) for i in range(ends)])
    return before, after


def shifted(value, lane):
    width = value.shape[-1]
    ahead = jnp.where(lane == width - 1, 0.0, pltpu.roll(value, width - 1, 1))
    behind = jnp.where(lane == 0, 0.0, pltpu.roll(value, 1, 1))
    return jnp.concatenate([ahead, value, behind], axis=0)


def pack_kernel(at_ref, cells, own, face_ref, far_ref, wide):
    planes, pairs = own.shape[:2]
    count, lines = cells.shape[:2]
    for c in range(count):
        wide[c * lines : (c + 1) * lines] = cells[c].astype(F32)
    for d in range(planes):
        for t in range(pairs):
            row = 2 * (d * pairs + t)
            own[d, t] = jnp.concatenate(
                [wide[pl.ds(row + e, count, stride=lines), :] for e in range(2)], axis=0
            ).astype(BF16)
    even = at_ref[0] == 0
    face_ref[...] = own[jnp.where(even, planes - 1, 0)]
    far_ref[...] = own[jnp.where(even, 0, planes - 1)]


def grid_kernel(at_ref, own, facing, beyond, out_ref):
    planes = own.shape[0]
    before = jnp.where(at_ref[0] == 0, 0, planes + 1)
    for k in range(out_ref.shape[0]):
        for d in range(planes):
            out_ref[k, d + 1] = own[d]
        out_ref[k, before] = beyond[...]
        out_ref[k, planes + 1 - before] = facing[...]


def rows_kernel(rows, tiles, cot, first_ref, last_ref):
    sources, count = tiles.shape[:2]
    for ref, t, row in ((first_ref, 0, 0), (last_ref, rows // 2 - 1, rows - 1)):
        for p in range(count):
            ref[p * sources : (p + 1) * sources] = tiles[:, p, t]
        for d in range(count - 2):
            ref[count * sources + d] = cot[d * rows + row]


def sum_kernel(blocks, out_ref):
    for r in range(blocks.shape[1]):
        total = blocks[0, r].astype(F32)
        for k in range(1, blocks.shape[0]):
            total = total + blocks[k, r].astype(F32)
        for k in range(out_ref.shape[0]):
            out_ref[k, r] = total.astype(BF16)


def pair_kernel(kept, other, out_ref):
    first = other.shape[0] - kept.shape[0]
    for r in range(kept.shape[0]):
        total = (kept[r].astype(F32) + other[first + r].astype(F32)).astype(BF16)
        for k in range(out_ref.shape[0]):
            out_ref[k, r] = total


def add_kernel(left, right, out_ref):
    for k in range(left.shape[0]):
        out_ref[k] = (left[k].astype(F32) + right[k].astype(F32)).astype(BF16)


def unpack_kernel(parts, out_ref, wide):
    pairs, size = parts.shape[1:3]
    count, lines = out_ref.shape[:2]
    for t in range(pairs):
        total = parts[0, t].astype(F32)
        for k in range(1, parts.shape[0]):
            total = total + parts[k, t].astype(F32)
        wide[t * size : (t + 1) * size] = total
    for c in range(count):
        out_ref[c] = wide[pl.ds(c, lines, stride=count), :].astype(BF16)


def forward_kernel(planes, rows, at_ref, bias_ref, w_ref, cot, tiles, before, after, *refs):
    out_ref, face_ref, far_ref, kept_ref, grads, halves = refs
    cout, width = cot.shape[1:]
    sources = tiles.shape[0]
    edge = sources * (planes + 2)

    def tile(s, p, t):
        if t == 0:
            return before[p * sources + s]
        if t == rows // 2 + 1:
            return after[p * sources + s]
        return tiles[s, p, t - 1]

    lane = lax.broadcasted_iota(jnp.int32, (cout, width), 1)
    channel = lax.broadcasted_iota(jnp.int32, (cout, width), 0)
    bias = jnp.zeros((cout, width), F32)
    for o in range(cout):
        bias = jnp.where(channel == o, bias_ref[o], bias)
    sums = [None] * 3
    bias_sum = jnp.zeros((cout, width), F32)
    for d in range(planes):
        for pair in range(rows // 2 + 1):
            cells = [
                jnp.concatenate(
                    [tile(s, d + kd, pair + t) for t in range(2) for s in range(sources)], axis=0
                )
                for kd in range(3)
            ]
            acc = jnp.dot(w_ref[0], cells[0], preferred_element_type=F32)
            for kd in range(1, 3):
                acc = acc + jnp.dot(w_ref[kd], cells[kd], preferred_element_type=F32)
            stacks = []
            for e in range(2):
                z = acc[3 * e * cout : 3 * (e + 1) * cout]
                pre = (
                    z[cout : 2 * cout]
                    + jnp.where(lane == 0, 0.0, pltpu.roll(z[:cout], 1, 1))
                    + jnp.where(lane == width - 1, 0.0, pltpu.roll(z[2 * cout :], width - 1, 1))
                    + bias
                )
                small = jnp.exp(-jnp.abs(pre))
                sigmoid = jnp.where(pre >= 0, 1.0, small) / (1.0 + small)
                row = 2 * pair + e
                if row == 0:
                    cotangent = before[edge + d]
                elif row == rows + 1:
                    cotangent = after[edge + d]
                else:
                    cotangent = cot[d * rows + row - 1]
                grad = (cotangent.astype(F32) * (0.2 + 0.8 * sigmoid)).astype(BF16)
                grads[d, row] = grad
                if row == 0 or row == rows + 1:
                    stacks.append(jnp.zeros((3 * cout, width), BF16))
                    continue
                softplus = jnp.maximum(pre, 0.0) + jnp.log1p(small)
                out_ref[d * rows + row - 1] = (0.2 * pre + 0.8 * softplus).astype(BF16)
                grad = grad.astype(F32)
                bias_sum = bias_sum + grad
                stacks.append(shifted(grad, lane).astype(BF16))
            both = jnp.concatenate(stacks, axis=0)
            for kd in range(3):
                term = lax.dot_general(
                    both, cells[kd], (((1,), (1,)), ((), ())), preferred_element_type=F32
                )
                sums[kd] = term if sums[kd] is None else sums[kd] + term

    first = (lane // PART) % 2 == 0
    blocks, last = [], []
    for kd in range(3):
        for kw in range(3):
            one = sums[kd][kw * cout : (kw + 1) * cout]
            two = sums[kd][(3 + kw) * cout : (4 + kw) * cout]
            back = pltpu.roll(two[:, width:], width - PART, 1)
            blocks.append(
                one[:, :width]
                + jnp.where(
                    first,
                    pltpu.roll(two[:, :width], width - PART, 1),
                    pltpu.roll(two[:, width:], PART, 1),
                )
            )
            last.append(one[:, width:] + back)
    last.append(jnp.broadcast_to(jnp.sum(bias_sum, axis=1, keepdims=True), (cout, width)))
    for k in range(0, len(last), 2):
        blocks.append(jnp.where(first, last[k], pltpu.roll(last[k + 1], PART, 1)))
    source = lax.broadcasted_iota(jnp.int32, (width, width), 0)
    target = (source // PART) % 2 * (width // 2) + source // (2 * PART) * PART + source % PART
    order = jnp.where(lax.broadcasted_iota(jnp.int32, (width, width), 1) == target, 1.0, 0.0).astype(BF16)
    placed = jnp.dot(jnp.concatenate(blocks, axis=0).astype(BF16), order, preferred_element_type=F32)
    count = len(blocks) // 2
    for k in range(2 * count):
        halves[k // count, k % count] = placed[k * cout : (k + 1) * cout].astype(BF16)
    core = at_ref[0]
    face_ref[: rows + 2] = grads[1 - core]
    face_ref[rows + 2 :] = halves[1 - core]
    far_ref[...] = grads[core]
    kept_ref[...] = halves[core]


def backward_kernel(planes, rows, at_ref, w_ref, face, far, face_in, far_in, kept_ref, sent_ref, stack, parts):
    cout, width = far.shape[1:]
    cin = w_ref.shape[0]
    count = 2 * parts.shape[1]
    part = cin // count
    lane = lax.broadcasted_iota(jnp.int32, (cout, width), 1)
    step = 3 * cout
    core = at_ref[0]
    for q, source in enumerate((face_in, face, far, far_in)):
        p = jnp.where(core == 1, q, planes + 1 - q)
        for r in range(rows + 2):
            stack[p, r * step : (r + 1) * step, :] = shifted(source[r].astype(F32), lane).astype(BF16)
    w = w_ref[...]
    for d in range(planes):
        for h in range(0, rows, 2):
            cells = jnp.concatenate(
                [
                    jnp.concatenate(
                        [stack[d + a, (h + e) * step : (h + e + 3) * step, :] for a in range(3)], axis=0
                    )
                    for e in range(2)
                ],
                axis=1,
            )
            acc = jnp.dot(w, cells, preferred_element_type=F32)
            pair = (d * rows + h) // 2
            for f in range(count):
                piece = acc[f * part : (f + 1) * part]
                piece = jnp.concatenate([piece[:, :width], piece[:, width:]], axis=0).astype(BF16)
                parts[(f % 2) ^ at_ref[1], f // 2, pair] = piece
    kept_ref[...] = parts[0]
    sent_ref[...] = parts[1]


def placing(cin):
    ones = np.zeros((2, 3, cin, 2, cin // PART, 2, PART), np.float32)
    for e in range(2):
        for kh in range(3):
            for i in range(cin):
                ones[e, kh, i, (kh + e) // 2, i // PART, (kh + e) % 2, i % PART] = 1
    return ones.reshape(2, 3 * cin, 4 * cin)


def weights_kernel(at_ref, mine, other, w_ref, b_ref):
    count, cout, width = mine.shape
    half = width // 2
    for k in range(2 * count):
        own = at_ref[0] == k // count
        block = jnp.where(own, mine[k % count].astype(F32), other[k % count].astype(F32))
        for e in range(2):
            piece = block[:, e * half : (e + 1) * half]
            at, kh = (k, e) if k < 9 else (2 * (k - 9) + e, 2)
            if at < 9:
                w_ref[at // 3 * 9 + kh * 3 + at % 3] = piece
    spare = block[:, half : half + cout]
    row = lax.broadcasted_iota(jnp.int32, (cout, cout), 0)
    lane = lax.broadcasted_iota(jnp.int32, (cout, cout), 1)
    b_ref[...] = jnp.sum(jnp.where(row == lane, spare, 0.0), axis=0, keepdims=True)


def call(body, name, *args, out, scratch=(), dtype=BF16, flops=0, moved=1 << 18, waves=0, scalars=0):
    smem, vmem = pl.BlockSpec(memory_space=pltpu.SMEM), pl.BlockSpec(memory_space=pltpu.VMEM)
    outs = tuple(jax.ShapeDtypeStruct(shape, dtype) for shape in out)
    results = pl.pallas_call(
        body,
        out_shape=outs,
        in_specs=[smem] * scalars + [vmem] * (len(args) - scalars),
        out_specs=(vmem,) * len(outs),
        scratch_shapes=[pltpu.VMEM(shape, kind) for shape, kind in scratch],
        compiler_params=pltpu.CompilerParams(vmem_limit_bytes=12 << 20),
        cost_estimate=pl.CostEstimate(flops=flops, bytes_accessed=moved, transcendentals=waves),
        name=name,
    )(*args)
    return results[0] if len(outs) == 1 else results


def per_device(activations, weights, bias, cotangent):
    cin_dev, planes, rows, width = activations.shape
    taps, cin, cout = weights.shape
    cells = planes * rows
    depth, height, filt = (lax.axis_size(axis) for axis in ("depth", "height", "filt"))
    swap = [(i, i ^ 1) for i in range(depth)]
    cross = [(i, i - 1 if i % 2 == 0 else i + 1) for i in range(1, depth - 1)]
    at = jnp.stack([lax.axis_index("depth") % 2, lax.axis_index("filt") % 2]).astype(jnp.int32)
    pairs, double = rows // 2, 2 * cin_dev

    own, face, far = call(
        pack_kernel,
        "pack",
        at,
        activations.reshape(cin_dev, cells, width),
        out=[(planes, pairs, double, width)] + [(pairs, double, width)] * 2,
        scratch=[((cin_dev * cells, width), F32)],
        scalars=1,
    )
    facing = lax.ppermute(face, "depth", swap)
    beyond = lax.ppermute(far, "depth", cross)
    grid = call(
        grid_kernel,
        "grid",
        at,
        own,
        facing,
        beyond,
        out=[(filt, planes + 2, pairs, double, width)],
        scalars=1,
    )
    tiles = swapped(grid, "filt")

    cot = cotangent.transpose(1, 2, 0, 3).reshape(cells, cout, width)
    split = weights.reshape(3, 3, 3, cin, cout)
    w_forward = jnp.einsum(
        "akj,ejn->aekn",
        split.transpose(0, 2, 4, 1, 3).reshape(3, 3 * cout, 3 * cin),
        jnp.asarray(placing(cin), BF16),
        preferred_element_type=F32,
    )
    w_forward = w_forward.astype(BF16).reshape(3, 6 * cout, 4 * cin)
    w_back = split[::-1, ::-1].transpose(3, 0, 1, 2, 4).reshape(cin, taps * cout)
    first, last = call(
        functools.partial(rows_kernel, rows),
        "rows",
        tiles,
        cot,
        out=[((planes + 2) * filt + planes, cout, width)] * 2,
    )
    first, last, w_forward = lax.optimization_barrier((first, last, w_forward))
    before, after = neighbours(first, last, "height")

    work = 2 * cells * width * taps * cin * cout
    count = (taps + 1) // 4
    out, face, far, kept_sums = call(
        functools.partial(forward_kernel, planes, rows),
        "forward",
        at,
        bias,
        w_forward,
        cot,
        tiles,
        before,
        after,
        out=[(k, cout, width) for k in (cells, rows + 2 + count, rows + 2, count)],
        scratch=[((planes, rows + 2, cout, width), BF16), ((2, count, cout, width), BF16)],
        flops=3 * work,
        waves=1 << 17,
        scalars=2,
    )
    output = out.reshape(planes, rows, cout, width).transpose(2, 0, 1, 3)

    size = kept_sums.shape
    face_in = lax.ppermute(face, "depth", swap)
    sums = call(pair_kernel, "pair", kept_sums, face_in, out=[(height,) + size])
    sums, far = lax.optimization_barrier((sums, far))
    far_in = lax.ppermute(far, "depth", cross)
    sums = swapped(sums, "height")
    kept, sent = call(
        functools.partial(backward_kernel, planes, rows),
        "backward",
        at,
        w_back,
        face,
        far,
        face_in,
        far_in,
        out=[(filt // 2, cells // 2, double, width)] * 2,
        scratch=[
            ((planes + 2, (rows + 2) * 3 * cout, width), BF16),
            ((2, filt // 2, cells // 2, double, width), BF16),
        ],
        flops=work,
        scalars=1,
    )
    sums, kept, sent = lax.optimization_barrier((sums, kept, sent))
    groups = [[i for i in range(depth) if i % 2 == k] for k in range(2)]
    sums = swapped(call(sum_kernel, "sums", sums, out=[(depth // 2,) + size]), "depth", groups)
    sent = lax.ppermute(sent, "filt", [(i, i ^ 1) for i in range(filt)])
    parts = call(add_kernel, "add", kept, sent, out=[kept.shape])
    sums, parts = lax.optimization_barrier((sums, parts))
    groups = [[i for i in range(filt) if i % 2 == k] for k in range(2)]
    parts = swapped(parts, "filt", groups)
    summed = call(
        unpack_kernel,
        "unpack",
        parts,
        out=[(cin_dev, cells, width)],
        scratch=[((cin_dev * cells, width), F32)],
    ).reshape(activations.shape)

    mine = call(sum_kernel, "sums", sums, out=[(1,) + size])[0]
    other = lax.ppermute(mine, "depth", swap)
    weight_grad, bias_grad = call(
        weights_kernel,
        "weights",
        at,
        mine,
        other,
        out=[(taps, cout, cin), (1, cout)],
        dtype=F32,
        scalars=1,
    )
    return (output, summed, weight_grad.transpose(0, 2, 1), bias_grad.reshape(cout))


def solution(mesh):
    placed = (
        P("filt", "depth", "height", None),
        P(None, None, "filt"),
        P("filt"),
        P("filt", "depth", "height", None),
    )
    return jax.shard_map(
        per_device,
        mesh=mesh,
        in_specs=placed,
        out_specs=(
            P("filt", "depth", "height", None),
            P("filt", "depth", "height", None),
            P(None, None, "filt"),
            P("filt"),
        ),
        check_vma=False,
    )
```

```python
import functools

import jax
import jax.numpy as jnp
import numpy as np
from jax import lax
from jax.experimental import pallas as pl
from jax.experimental.pallas import tpu as pltpu
from jax.sharding import PartitionSpec as P

BF16 = jnp.bfloat16
F32 = jnp.float32
PART = 8


def swapped(blocks, axis, groups=None):
    return lax.all_to_all(blocks, axis, 0, 0, tiled=True, axis_index_groups=groups)


def neighbours(first, last, axis):
    ends = lax.axis_size(axis) - 1
    before = lax.ppermute(last, axis, [(i, i + 1) for i in range(ends)])
    after = lax.ppermute(first, axis, [(i + 1, i) for i in range(ends)])
    return before, after


def shifted(value, lane):
    width = value.shape[-1]
    ahead = jnp.where(lane == width - 1, 0.0, pltpu.roll(value, width - 1, 1))
    behind = jnp.where(lane == 0, 0.0, pltpu.roll(value, 1, 1))
    return jnp.concatenate([ahead, value, behind], axis=0)


def pack_kernel(at_ref, cells, own, face_ref, far_ref, wide):
    planes, pairs = own.shape[:2]
    count, lines = cells.shape[:2]
    for c in range(count):
        wide[c * lines : (c + 1) * lines] = cells[c].astype(F32)
    for d in range(planes):
        for t in range(pairs):
            row = 2 * (d * pairs + t)
            own[d, t] = jnp.concatenate(
                [wide[pl.ds(row + e, count, stride=lines), :] for e in range(2)], axis=0
            ).astype(BF16)
    even = at_ref[0] == 0
    face_ref[...] = own[jnp.where(even, planes - 1, 0)]
    far_ref[...] = own[jnp.where(even, 0, planes - 1)]


def grid_kernel(at_ref, own, facing, beyond, out_ref):
    planes = own.shape[0]
    before = jnp.where(at_ref[0] == 0, 0, planes + 1)
    for k in range(out_ref.shape[0]):
        for d in range(planes):
            out_ref[k, d + 1] = own[d]
        out_ref[k, before] = beyond[...]
        out_ref[k, planes + 1 - before] = facing[...]


def rows_kernel(rows, tiles, cot, first_ref, last_ref):
    sources, count = tiles.shape[:2]
    for ref, t, row in ((first_ref, 0, 0), (last_ref, rows // 2 - 1, rows - 1)):
        for p in range(count):
            ref[p * sources : (p + 1) * sources] = tiles[:, p, t]
        for d in range(count - 2):
            ref[count * sources + d] = cot[d * rows + row]


def sum_kernel(blocks, out_ref):
    for r in range(blocks.shape[1]):
        total = blocks[0, r].astype(F32)
        for k in range(1, blocks.shape[0]):
            total = total + blocks[k, r].astype(F32)
        for k in range(out_ref.shape[0]):
            out_ref[k, r] = total.astype(BF16)


def pair_kernel(kept, other, out_ref):
    first = other.shape[0] - kept.shape[0]
    for r in range(kept.shape[0]):
        total = (kept[r].astype(F32) + other[first + r].astype(F32)).astype(BF16)
        for k in range(out_ref.shape[0]):
            out_ref[k, r] = total


def unpack_kernel(parts, out_ref, wide):
    pairs, size = parts.shape[1:3]
    count, lines = out_ref.shape[:2]
    for t in range(pairs):
        total = parts[0, t].astype(F32)
        for k in range(1, parts.shape[0]):
            total = total + parts[k, t].astype(F32)
        wide[t * size : (t + 1) * size] = total
    for c in range(count):
        out_ref[c] = wide[pl.ds(c, lines, stride=count), :].astype(BF16)


def forward_kernel(planes, rows, at_ref, bias_ref, w_ref, cot, tiles, before, after, *refs):
    out_ref, face_ref, far_ref, kept_ref, grads, halves = refs
    cout, width = cot.shape[1:]
    sources = tiles.shape[0]
    edge = sources * (planes + 2)

    def tile(s, p, t):
        if t == 0:
            return before[p * sources + s]
        if t == rows // 2 + 1:
            return after[p * sources + s]
        return tiles[s, p, t - 1]

    lane = lax.broadcasted_iota(jnp.int32, (cout, width), 1)
    channel = lax.broadcasted_iota(jnp.int32, (cout, width), 0)
    bias = jnp.zeros((cout, width), F32)
    for o in range(cout):
        bias = jnp.where(channel == o, bias_ref[o], bias)
    sums = [None] * 3
    bias_sum = jnp.zeros((cout, width), F32)
    for d in range(planes):
        for pair in range(rows // 2 + 1):
            cells = [
                jnp.concatenate(
                    [tile(s, d + kd, pair + t) for t in range(2) for s in range(sources)], axis=0
                )
                for kd in range(3)
            ]
            acc = jnp.dot(w_ref[0], cells[0], preferred_element_type=F32)
            for kd in range(1, 3):
                acc = acc + jnp.dot(w_ref[kd], cells[kd], preferred_element_type=F32)
            stacks = []
            for e in range(2):
                z = acc[3 * e * cout : 3 * (e + 1) * cout]
                pre = (
                    z[cout : 2 * cout]
                    + jnp.where(lane == 0, 0.0, pltpu.roll(z[:cout], 1, 1))
                    + jnp.where(lane == width - 1, 0.0, pltpu.roll(z[2 * cout :], width - 1, 1))
                    + bias
                )
                small = jnp.exp(-jnp.abs(pre))
                sigmoid = jnp.where(pre >= 0, 1.0, small) / (1.0 + small)
                row = 2 * pair + e
                if row == 0:
                    cotangent = before[edge + d]
                elif row == rows + 1:
                    cotangent = after[edge + d]
                else:
                    cotangent = cot[d * rows + row - 1]
                grad = (cotangent.astype(F32) * (0.2 + 0.8 * sigmoid)).astype(BF16)
                grads[d, row] = grad
                if row == 0 or row == rows + 1:
                    stacks.append(jnp.zeros((3 * cout, width), BF16))
                    continue
                softplus = jnp.maximum(pre, 0.0) + jnp.log1p(small)
                out_ref[d * rows + row - 1] = (0.2 * pre + 0.8 * softplus).astype(BF16)
                grad = grad.astype(F32)
                bias_sum = bias_sum + grad
                stacks.append(shifted(grad, lane).astype(BF16))
            both = jnp.concatenate(stacks, axis=0)
            for kd in range(3):
                term = lax.dot_general(
                    both, cells[kd], (((1,), (1,)), ((), ())), preferred_element_type=F32
                )
                sums[kd] = term if sums[kd] is None else sums[kd] + term

    first = (lane // PART) % 2 == 0
    blocks, last = [], []
    for kd in range(3):
        for kw in range(3):
            one = sums[kd][kw * cout : (kw + 1) * cout]
            two = sums[kd][(3 + kw) * cout : (4 + kw) * cout]
            back = pltpu.roll(two[:, width:], width - PART, 1)
            blocks.append(
                one[:, :width]
                + jnp.where(
                    first,
                    pltpu.roll(two[:, :width], width - PART, 1),
                    pltpu.roll(two[:, width:], PART, 1),
                )
            )
            last.append(one[:, width:] + back)
    last.append(jnp.broadcast_to(jnp.sum(bias_sum, axis=1, keepdims=True), (cout, width)))
    for k in range(0, len(last), 2):
        blocks.append(jnp.where(first, last[k], pltpu.roll(last[k + 1], PART, 1)))
    source = lax.broadcasted_iota(jnp.int32, (width, width), 0)
    target = (source // PART) % 2 * (width // 2) + source // (2 * PART) * PART + source % PART
    order = jnp.where(lax.broadcasted_iota(jnp.int32, (width, width), 1) == target, 1.0, 0.0).astype(BF16)
    placed = jnp.dot(jnp.concatenate(blocks, axis=0).astype(BF16), order, preferred_element_type=F32)
    count = len(blocks) // 2
    for k in range(2 * count):
        halves[k // count, k % count] = placed[k * cout : (k + 1) * cout].astype(BF16)
    core = at_ref[0]
    face_ref[: rows + 2] = grads[1 - core]
    face_ref[rows + 2 :] = halves[1 - core]
    far_ref[...] = grads[core]
    kept_ref[...] = halves[core]


def backward_kernel(planes, rows, at_ref, w_ref, face, far, face_in, far_in, parts, stack):
    cout, width = far.shape[1:]
    cin = w_ref.shape[0]
    count = parts.shape[0]
    part = cin // count
    lane = lax.broadcasted_iota(jnp.int32, (cout, width), 1)
    step = 3 * cout
    core = at_ref[0]
    for q, source in enumerate((face_in, face, far, far_in)):
        p = jnp.where(core == 1, q, planes + 1 - q)
        for r in range(rows + 2):
            stack[p, r * step : (r + 1) * step, :] = shifted(source[r].astype(F32), lane).astype(BF16)
    w = w_ref[...]
    for d in range(planes):
        for h in range(0, rows, 2):
            cells = jnp.concatenate(
                [
                    jnp.concatenate(
                        [stack[d + a, (h + e) * step : (h + e + 3) * step, :] for a in range(3)], axis=0
                    )
                    for e in range(2)
                ],
                axis=1,
            )
            acc = jnp.dot(w, cells, preferred_element_type=F32)
            pair = (d * rows + h) // 2
            for f in range(count):
                piece = acc[f * part : (f + 1) * part]
                piece = jnp.concatenate([piece[:, :width], piece[:, width:]], axis=0).astype(BF16)
                parts[f, pair] = piece


def placing(cin):
    ones = np.zeros((2, 3, cin, 2, cin // PART, 2, PART), np.float32)
    for e in range(2):
        for kh in range(3):
            for i in range(cin):
                ones[e, kh, i, (kh + e) // 2, i // PART, (kh + e) % 2, i % PART] = 1
    return ones.reshape(2, 3 * cin, 4 * cin)


def weights_kernel(at_ref, mine, other, w_ref, b_ref):
    count, cout, width = mine.shape
    half = width // 2
    for k in range(2 * count):
        own = at_ref[0] == k // count
        block = jnp.where(own, mine[k % count].astype(F32), other[k % count].astype(F32))
        for e in range(2):
            piece = block[:, e * half : (e + 1) * half]
            at, kh = (k, e) if k < 9 else (2 * (k - 9) + e, 2)
            if at < 9:
                w_ref[at // 3 * 9 + kh * 3 + at % 3] = piece
    spare = block[:, half : half + cout]
    row = lax.broadcasted_iota(jnp.int32, (cout, cout), 0)
    lane = lax.broadcasted_iota(jnp.int32, (cout, cout), 1)
    b_ref[...] = jnp.sum(jnp.where(row == lane, spare, 0.0), axis=0, keepdims=True)


def call(body, name, *args, out, scratch=(), dtype=BF16, flops=0, moved=1 << 18, waves=0, scalars=0):
    smem, vmem = pl.BlockSpec(memory_space=pltpu.SMEM), pl.BlockSpec(memory_space=pltpu.VMEM)
    outs = tuple(jax.ShapeDtypeStruct(shape, dtype) for shape in out)
    results = pl.pallas_call(
        body,
        out_shape=outs,
        in_specs=[smem] * scalars + [vmem] * (len(args) - scalars),
        out_specs=(vmem,) * len(outs),
        scratch_shapes=[pltpu.VMEM(shape, kind) for shape, kind in scratch],
        compiler_params=pltpu.CompilerParams(vmem_limit_bytes=12 << 20),
        cost_estimate=pl.CostEstimate(flops=flops, bytes_accessed=moved, transcendentals=waves),
        name=name,
    )(*args)
    return results[0] if len(outs) == 1 else results


def per_device(activations, weights, bias, cotangent):
    cin_dev, planes, rows, width = activations.shape
    taps, cin, cout = weights.shape
    cells = planes * rows
    depth, height, filt = (lax.axis_size(axis) for axis in ("depth", "height", "filt"))
    swap = [(i, i ^ 1) for i in range(depth)]
    cross = [(i, i - 1 if i % 2 == 0 else i + 1) for i in range(1, depth - 1)]
    at = (lax.axis_index("depth") % 2).astype(jnp.int32).reshape(1)
    pairs, double = rows // 2, 2 * cin_dev

    own, face, far = call(
        pack_kernel,
        "pack",
        at,
        activations.reshape(cin_dev, cells, width),
        out=[(planes, pairs, double, width)] + [(pairs, double, width)] * 2,
        scratch=[((cin_dev * cells, width), F32)],
        scalars=1,
    )
    facing = lax.ppermute(face, "depth", swap)
    beyond = lax.ppermute(far, "depth", cross)
    grid = call(
        grid_kernel,
        "grid",
        at,
        own,
        facing,
        beyond,
        out=[(filt, planes + 2, pairs, double, width)],
        scalars=1,
    )
    tiles = swapped(grid, "filt")

    cot = cotangent.transpose(1, 2, 0, 3).reshape(cells, cout, width)
    split = weights.reshape(3, 3, 3, cin, cout)
    w_forward = jnp.einsum(
        "akj,ejn->aekn",
        split.transpose(0, 2, 4, 1, 3).reshape(3, 3 * cout, 3 * cin),
        jnp.asarray(placing(cin), BF16),
        preferred_element_type=F32,
    )
    w_forward = w_forward.astype(BF16).reshape(3, 6 * cout, 4 * cin)
    w_back = split[::-1, ::-1].transpose(3, 0, 1, 2, 4).reshape(cin, taps * cout)
    first, last = call(
        functools.partial(rows_kernel, rows),
        "rows",
        tiles,
        cot,
        out=[((planes + 2) * filt + planes, cout, width)] * 2,
    )
    first, last, w_forward, w_back = lax.optimization_barrier((first, last, w_forward, w_back))
    before, after = neighbours(first, last, "height")

    work = 2 * cells * width * taps * cin * cout
    count = (taps + 1) // 4
    out, face, far, kept_sums = call(
        functools.partial(forward_kernel, planes, rows),
        "forward",
        at,
        bias,
        w_forward,
        cot,
        tiles,
        before,
        after,
        out=[(k, cout, width) for k in (cells, rows + 2 + count, rows + 2, count)],
        scratch=[((planes, rows + 2, cout, width), BF16), ((2, count, cout, width), BF16)],
        flops=3 * work,
        waves=1 << 17,
        scalars=2,
    )
    output = out.reshape(planes, rows, cout, width).transpose(2, 0, 1, 3)

    size = kept_sums.shape
    face_in = lax.ppermute(face, "depth", swap)
    far_in = lax.ppermute(far, "depth", cross)
    sums = swapped(call(pair_kernel, "pair", kept_sums, face_in, out=[(height,) + size]), "height")
    parts = call(
        functools.partial(backward_kernel, planes, rows),
        "backward",
        at,
        w_back,
        face,
        far,
        face_in,
        far_in,
        out=[(filt, cells // 2, double, width)],
        scratch=[((planes + 2, (rows + 2) * 3 * cout, width), BF16)],
        flops=64 * work,
        scalars=1,
    )
    sums, parts = lax.optimization_barrier((sums, parts))
    groups = [[i for i in range(depth) if i % 2 == k] for k in range(2)]
    sums = swapped(call(sum_kernel, "sums", sums, out=[(depth // 2,) + size]), "depth", groups)
    sums, parts = lax.optimization_barrier((sums, parts))
    parts = swapped(parts, "filt")
    summed = call(
        unpack_kernel,
        "unpack",
        parts,
        out=[(cin_dev, cells, width)],
        scratch=[((cin_dev * cells, width), F32)],
    ).reshape(activations.shape)

    mine = call(sum_kernel, "sums", sums, out=[(1,) + size])[0]
    other = lax.ppermute(mine, "depth", swap)
    weight_grad, bias_grad = call(
        weights_kernel,
        "weights",
        at,
        mine,
        other,
        out=[(taps, cout, cin), (1, cout)],
        dtype=F32,
        scalars=1,
    )
    return (output, summed, weight_grad.transpose(0, 2, 1), bias_grad.reshape(cout))


def solution(mesh):
    placed = (
        P("filt", "depth", "height", None),
        P(None, None, "filt"),
        P("filt"),
        P("filt", "depth", "height", None),
    )
    return jax.shard_map(
        per_device,
        mesh=mesh,
        in_specs=placed,
        out_specs=(
            P("filt", "depth", "height", None),
            P("filt", "depth", "height", None),
            P(None, None, "filt"),
            P("filt"),
        ),
        check_vma=False,
    )
```

```python
import functools

import jax
import jax.numpy as jnp
import numpy as np
from jax import lax
from jax.experimental import pallas as pl
from jax.experimental.pallas import tpu as pltpu
from jax.sharding import PartitionSpec as P

BF16 = jnp.bfloat16
F32 = jnp.float32
PART = 8


def swapped(blocks, axis, groups=None):
    return lax.all_to_all(blocks, axis, 0, 0, tiled=True, axis_index_groups=groups)


def neighbours(first, last, axis):
    ends = lax.axis_size(axis) - 1
    before = lax.ppermute(last, axis, [(i, i + 1) for i in range(ends)])
    after = lax.ppermute(first, axis, [(i + 1, i) for i in range(ends)])
    return before, after


def shifted(value, lane):
    width = value.shape[-1]
    ahead = jnp.where(lane == width - 1, 0.0, pltpu.roll(value, width - 1, 1))
    behind = jnp.where(lane == 0, 0.0, pltpu.roll(value, 1, 1))
    return jnp.concatenate([ahead, value, behind], axis=0)


def pack_kernel(at_ref, cells, own, face_ref, wide):
    planes, pairs = own.shape[:2]
    count, lines = cells.shape[:2]
    for c in range(count):
        wide[c * lines : (c + 1) * lines] = cells[c].astype(F32)
    for d in range(planes):
        for t in range(pairs):
            row = 2 * (d * pairs + t)
            own[d, t] = jnp.concatenate(
                [wide[pl.ds(row + e, count, stride=lines), :] for e in range(2)], axis=0
            ).astype(BF16)
    face_ref[...] = own[jnp.where(at_ref[0] == 0, planes - 1, 0)]


def grid_kernel(at_ref, own, facing, out_ref):
    planes = own.shape[0]
    core = at_ref[0]
    for k in range(out_ref.shape[0]):
        for d in range(planes):
            out_ref[k, d + core] = own[d]
        out_ref[k, (1 - core) * planes] = facing[...]


def rows_kernel(rows, at_ref, tiles, cot, far_ref, far_first, far_last, first_ref, last_ref):
    sources, count, pairs = tiles.shape[:3]
    plane = at_ref[0] * (count - 1)
    far_ref[...] = tiles[:, plane]
    far_first[...] = tiles[:, plane, 0]
    far_last[...] = tiles[:, plane, pairs - 1]
    for ref, t, row in ((first_ref, 0, 0), (last_ref, pairs - 1, rows - 1)):
        for p in range(count):
            ref[p * sources : (p + 1) * sources] = tiles[:, p, t]
        for d in range(count - 1):
            ref[count * sources + d] = cot[d * rows + row]


def sum_kernel(blocks, out_ref):
    for r in range(blocks.shape[1]):
        total = blocks[0, r].astype(F32)
        for k in range(1, blocks.shape[0]):
            total = total + blocks[k, r].astype(F32)
        for k in range(out_ref.shape[0]):
            out_ref[k, r] = total.astype(BF16)


def pair_kernel(kept, other, out_ref):
    first = other.shape[0] - kept.shape[0]
    for r in range(kept.shape[0]):
        total = (kept[r].astype(F32) + other[first + r].astype(F32)).astype(BF16)
        for k in range(out_ref.shape[0]):
            out_ref[k, r] = total


def unpack_kernel(parts, out_ref, wide):
    pairs, size = parts.shape[1:3]
    count, lines = out_ref.shape[:2]
    for t in range(pairs):
        total = parts[0, t].astype(F32)
        for k in range(1, parts.shape[0]):
            total = total + parts[k, t].astype(F32)
        wide[t * size : (t + 1) * size] = total
    for c in range(count):
        out_ref[c] = wide[pl.ds(c, lines, stride=count), :].astype(BF16)


def forward_kernel(planes, rows, at_ref, bias_ref, w_ref, cot, tiles, before, after, far, far_before, far_after, *refs):
    out_ref, face_ref, far_ref, kept_ref, grads, halves = refs
    cout, width = cot.shape[1:]
    sources = tiles.shape[0]
    edge = sources * (planes + 1)
    core = at_ref[0]

    def tile(s, p, t):
        def near(q):
            if t == 0:
                return before[q * sources + s]
            if t == rows // 2 + 1:
                return after[q * sources + s]
            return tiles[s, q, t - 1]

        if 0 < p < planes + 1:
            return near(p - 1 + core)
        if t == 0:
            beyond = far_before[s]
        elif t == rows // 2 + 1:
            beyond = far_after[s]
        else:
            beyond = far[s, t - 1]
        if p == 0:
            return jnp.where(core == 0, beyond, near(0))
        return jnp.where(core == 1, beyond, near(planes))

    lane = lax.broadcasted_iota(jnp.int32, (cout, width), 1)
    channel = lax.broadcasted_iota(jnp.int32, (cout, width), 0)
    bias = jnp.zeros((cout, width), F32)
    for o in range(cout):
        bias = jnp.where(channel == o, bias_ref[o], bias)
    sums = [None] * 3
    bias_sum = jnp.zeros((cout, width), F32)
    for d in range(planes):
        for pair in range(rows // 2 + 1):
            cells = [
                jnp.concatenate(
                    [tile(s, d + kd, pair + t) for t in range(2) for s in range(sources)], axis=0
                )
                for kd in range(3)
            ]
            acc = jnp.dot(w_ref[0], cells[0], preferred_element_type=F32)
            for kd in range(1, 3):
                acc = acc + jnp.dot(w_ref[kd], cells[kd], preferred_element_type=F32)
            stacks = []
            for e in range(2):
                z = acc[3 * e * cout : 3 * (e + 1) * cout]
                pre = (
                    z[cout : 2 * cout]
                    + jnp.where(lane == 0, 0.0, pltpu.roll(z[:cout], 1, 1))
                    + jnp.where(lane == width - 1, 0.0, pltpu.roll(z[2 * cout :], width - 1, 1))
                    + bias
                )
                small = jnp.exp(-jnp.abs(pre))
                sigmoid = jnp.where(pre >= 0, 1.0, small) / (1.0 + small)
                row = 2 * pair + e
                if row == 0:
                    cotangent = before[edge + d]
                elif row == rows + 1:
                    cotangent = after[edge + d]
                else:
                    cotangent = cot[d * rows + row - 1]
                grad = (cotangent.astype(F32) * (0.2 + 0.8 * sigmoid)).astype(BF16)
                grads[d, row] = grad
                if row == 0 or row == rows + 1:
                    stacks.append(jnp.zeros((3 * cout, width), BF16))
                    continue
                softplus = jnp.maximum(pre, 0.0) + jnp.log1p(small)
                out_ref[d * rows + row - 1] = (0.2 * pre + 0.8 * softplus).astype(BF16)
                grad = grad.astype(F32)
                bias_sum = bias_sum + grad
                stacks.append(shifted(grad, lane).astype(BF16))
            both = jnp.concatenate(stacks, axis=0)
            for kd in range(3):
                term = lax.dot_general(
                    both, cells[kd], (((1,), (1,)), ((), ())), preferred_element_type=F32
                )
                sums[kd] = term if sums[kd] is None else sums[kd] + term

    first = (lane // PART) % 2 == 0
    blocks, last = [], []
    for kd in range(3):
        for kw in range(3):
            one = sums[kd][kw * cout : (kw + 1) * cout]
            two = sums[kd][(3 + kw) * cout : (4 + kw) * cout]
            back = pltpu.roll(two[:, width:], width - PART, 1)
            blocks.append(
                one[:, :width]
                + jnp.where(
                    first,
                    pltpu.roll(two[:, :width], width - PART, 1),
                    pltpu.roll(two[:, width:], PART, 1),
                )
            )
            last.append(one[:, width:] + back)
    last.append(jnp.broadcast_to(jnp.sum(bias_sum, axis=1, keepdims=True), (cout, width)))
    for k in range(0, len(last), 2):
        blocks.append(jnp.where(first, last[k], pltpu.roll(last[k + 1], PART, 1)))
    source = lax.broadcasted_iota(jnp.int32, (width, width), 0)
    target = (source // PART) % 2 * (width // 2) + source // (2 * PART) * PART + source % PART
    order = jnp.where(lax.broadcasted_iota(jnp.int32, (width, width), 1) == target, 1.0, 0.0).astype(BF16)
    placed = jnp.dot(jnp.concatenate(blocks, axis=0).astype(BF16), order, preferred_element_type=F32)
    count = len(blocks) // 2
    for k in range(2 * count):
        halves[k // count, k % count] = placed[k * cout : (k + 1) * cout].astype(BF16)
    face_ref[: rows + 2] = grads[1 - core]
    face_ref[rows + 2 :] = halves[1 - core]
    far_ref[...] = grads[core]
    kept_ref[...] = halves[core]


def backward_kernel(planes, rows, at_ref, w_ref, face, far, face_in, far_in, parts, stack):
    cout, width = far.shape[1:]
    cin = w_ref.shape[0]
    count = parts.shape[0]
    part = cin // count
    lane = lax.broadcasted_iota(jnp.int32, (cout, width), 1)
    step = 3 * cout
    core = at_ref[0]
    for q, source in enumerate((face_in, face, far, far_in)):
        p = jnp.where(core == 1, q, planes + 1 - q)
        for r in range(rows + 2):
            stack[p, r * step : (r + 1) * step, :] = shifted(source[r].astype(F32), lane).astype(BF16)
    w = w_ref[...]
    for d in range(planes):
        for h in range(0, rows, 2):
            cells = jnp.concatenate(
                [
                    jnp.concatenate(
                        [stack[d + a, (h + e) * step : (h + e + 3) * step, :] for a in range(3)], axis=0
                    )
                    for e in range(2)
                ],
                axis=1,
            )
            acc = jnp.dot(w, cells, preferred_element_type=F32)
            pair = (d * rows + h) // 2
            for f in range(count):
                piece = acc[f * part : (f + 1) * part]
                piece = jnp.concatenate([piece[:, :width], piece[:, width:]], axis=0).astype(BF16)
                parts[f, pair] = piece


def placing(cin):
    ones = np.zeros((2, 3, cin, 2, cin // PART, 2, PART), np.float32)
    for e in range(2):
        for kh in range(3):
            for i in range(cin):
                ones[e, kh, i, (kh + e) // 2, i // PART, (kh + e) % 2, i % PART] = 1
    return ones.reshape(2, 3 * cin, 4 * cin)


def weights_kernel(at_ref, mine, other, w_ref, b_ref):
    count, cout, width = mine.shape
    half = width // 2
    for k in range(2 * count):
        own = at_ref[0] == k // count
        block = jnp.where(own, mine[k % count].astype(F32), other[k % count].astype(F32))
        for e in range(2):
            piece = block[:, e * half : (e + 1) * half]
            at, kh = (k, e) if k < 9 else (2 * (k - 9) + e, 2)
            if at < 9:
                w_ref[at // 3 * 9 + kh * 3 + at % 3] = piece
    spare = block[:, half : half + cout]
    row = lax.broadcasted_iota(jnp.int32, (cout, cout), 0)
    lane = lax.broadcasted_iota(jnp.int32, (cout, cout), 1)
    b_ref[...] = jnp.sum(jnp.where(row == lane, spare, 0.0), axis=0, keepdims=True)


def call(body, name, *args, out, scratch=(), dtype=BF16, flops=0, moved=1 << 18, waves=0, scalars=0):
    smem, vmem = pl.BlockSpec(memory_space=pltpu.SMEM), pl.BlockSpec(memory_space=pltpu.VMEM)
    outs = tuple(jax.ShapeDtypeStruct(shape, dtype) for shape in out)
    results = pl.pallas_call(
        body,
        out_shape=outs,
        in_specs=[smem] * scalars + [vmem] * (len(args) - scalars),
        out_specs=(vmem,) * len(outs),
        scratch_shapes=[pltpu.VMEM(shape, kind) for shape, kind in scratch],
        compiler_params=pltpu.CompilerParams(vmem_limit_bytes=12 << 20),
        cost_estimate=pl.CostEstimate(flops=flops, bytes_accessed=moved, transcendentals=waves),
        name=name,
    )(*args)
    return results[0] if len(outs) == 1 else results


def per_device(activations, weights, bias, cotangent):
    cin_dev, planes, rows, width = activations.shape
    taps, cin, cout = weights.shape
    cells = planes * rows
    depth, height, filt = (lax.axis_size(axis) for axis in ("depth", "height", "filt"))
    swap = [(i, i ^ 1) for i in range(depth)]
    cross = [(i, i - 1 if i % 2 == 0 else i + 1) for i in range(1, depth - 1)]
    at = (lax.axis_index("depth") % 2).astype(jnp.int32).reshape(1)
    pairs, double = rows // 2, 2 * cin_dev

    own, face = call(
        pack_kernel,
        "pack",
        at,
        activations.reshape(cin_dev, cells, width),
        out=[(planes, pairs, double, width), (pairs, double, width)],
        scratch=[((cin_dev * cells, width), F32)],
        scalars=1,
    )
    facing = lax.ppermute(face, "depth", swap)
    grid = call(
        grid_kernel,
        "grid",
        at,
        own,
        facing,
        out=[(filt, planes + 1, pairs, double, width)],
        scalars=1,
    )
    tiles = swapped(grid, "filt")

    cot = cotangent.transpose(1, 2, 0, 3).reshape(cells, cout, width)
    split = weights.reshape(3, 3, 3, cin, cout)
    w_forward = jnp.einsum(
        "akj,ejn->aekn",
        split.transpose(0, 2, 4, 1, 3).reshape(3, 3 * cout, 3 * cin),
        jnp.asarray(placing(cin), BF16),
        preferred_element_type=F32,
    )
    w_forward = w_forward.astype(BF16).reshape(3, 6 * cout, 4 * cin)
    w_back = split[::-1, ::-1].transpose(3, 0, 1, 2, 4).reshape(cin, taps * cout)
    sends = call(
        functools.partial(rows_kernel, rows),
        "rows",
        at,
        tiles,
        cot,
        out=[(filt, pairs, double, width)]
        + [(filt, double, width)] * 2
        + [((planes + 1) * filt + planes, cout, width)] * 2,
        scalars=1,
    )
    sends, w_forward, w_back = lax.optimization_barrier((sends, w_forward, w_back))
    far, far_first, far_last, first, last = sends
    corner = ("depth", "height")
    up = [(i * height + k, j * height + k + 1) for i, j in cross for k in range(height - 1)]
    down = [(i * height + k + 1, j * height + k) for i, j in cross for k in range(height - 1)]
    far_plane = lax.ppermute(far, "depth", cross)
    far_before = lax.ppermute(far_last, corner, up)
    far_after = lax.ppermute(far_first, corner, down)
    before, after = neighbours(first, last, "height")

    work = 2 * cells * width * taps * cin * cout
    count = (taps + 1) // 4
    out, face, far, kept_sums = call(
        functools.partial(forward_kernel, planes, rows),
        "forward",
        at,
        bias,
        w_forward,
        cot,
        tiles,
        before,
        after,
        far_plane,
        far_before,
        far_after,
        out=[(k, cout, width) for k in (cells, rows + 2 + count, rows + 2, count)],
        scratch=[((planes, rows + 2, cout, width), BF16), ((2, count, cout, width), BF16)],
        flops=3 * work,
        waves=1 << 17,
        scalars=2,
    )
    output = out.reshape(planes, rows, cout, width).transpose(2, 0, 1, 3)

    size = kept_sums.shape
    face_in = lax.ppermute(face, "depth", swap)
    far_in = lax.ppermute(far, "depth", cross)
    sums = swapped(call(pair_kernel, "pair", kept_sums, face_in, out=[(height,) + size]), "height")
    parts = call(
        functools.partial(backward_kernel, planes, rows),
        "backward",
        at,
        w_back,
        face,
        far,
        face_in,
        far_in,
        out=[(filt, cells // 2, double, width)],
        scratch=[((planes + 2, (rows + 2) * 3 * cout, width), BF16)],
        flops=64 * work,
        scalars=1,
    )
    sums, parts = lax.optimization_barrier((sums, parts))
    groups = [[i for i in range(depth) if i % 2 == k] for k in range(2)]
    sums = swapped(call(sum_kernel, "sums", sums, out=[(depth // 2,) + size]), "depth", groups)
    sums, parts = lax.optimization_barrier((sums, parts))
    parts = swapped(parts, "filt")
    summed = call(
        unpack_kernel,
        "unpack",
        parts,
        out=[(cin_dev, cells, width)],
        scratch=[((cin_dev * cells, width), F32)],
    ).reshape(activations.shape)

    mine = call(sum_kernel, "sums", sums, out=[(1,) + size])[0]
    other = lax.ppermute(mine, "depth", swap)
    weight_grad, bias_grad = call(
        weights_kernel,
        "weights",
        at,
        mine,
        other,
        out=[(taps, cout, cin), (1, cout)],
        dtype=F32,
        scalars=1,
    )
    return (output, summed, weight_grad.transpose(0, 2, 1), bias_grad.reshape(cout))


def solution(mesh):
    placed = (
        P("filt", "depth", "height", None),
        P(None, None, "filt"),
        P("filt"),
        P("filt", "depth", "height", None),
    )
    return jax.shard_map(
        per_device,
        mesh=mesh,
        in_specs=placed,
        out_specs=(
            P("filt", "depth", "height", None),
            P("filt", "depth", "height", None),
            P(None, None, "filt"),
            P("filt"),
        ),
        check_vma=False,
    )
```

```python
import functools

import jax
import jax.numpy as jnp
import numpy as np
from jax import lax
from jax.experimental import pallas as pl
from jax.experimental.pallas import tpu as pltpu
from jax.sharding import PartitionSpec as P

BF16 = jnp.bfloat16
F32 = jnp.float32
PART = 8


def swapped(blocks, axis, groups=None):
    return lax.all_to_all(blocks, axis, 0, 0, tiled=True, axis_index_groups=groups)


def neighbours(first, last, axis):
    ends = lax.axis_size(axis) - 1
    before = lax.ppermute(last, axis, [(i, i + 1) for i in range(ends)])
    after = lax.ppermute(first, axis, [(i + 1, i) for i in range(ends)])
    return before, after


def shifted(value, lane):
    width = value.shape[-1]
    ahead = jnp.where(lane == width - 1, 0.0, pltpu.roll(value, width - 1, 1))
    behind = jnp.where(lane == 0, 0.0, pltpu.roll(value, 1, 1))
    return jnp.concatenate([ahead, value, behind], axis=0)


def pack_kernel(cells, out_ref, wide):
    planes, pairs = out_ref.shape[1:3]
    count, lines = cells.shape[:2]
    for c in range(count):
        wide[c * lines : (c + 1) * lines] = cells[c].astype(F32)
    for d in range(planes):
        for t in range(pairs):
            row = 2 * (d * pairs + t)
            tile = jnp.concatenate(
                [wide[pl.ds(row + e, count, stride=lines), :] for e in range(2)], axis=0
            ).astype(BF16)
            for k in range(out_ref.shape[0]):
                out_ref[k, d, t] = tile


def plane_kernel(even, odd, at_ref, tiles, out_ref):
    out_ref[...] = tiles[:, jnp.where(at_ref[0] == 0, even, odd)]


def rows_kernel(planes, rows, at_ref, tiles, facing, beyond, cot, first_ref, last_ref):
    core = at_ref[0]
    sources = tiles.shape[0]
    before = jnp.where(core == 0, 0, (planes + 1) * sources)
    after = (planes + 1) * sources - before
    for ref, t, row in ((first_ref, 0, 0), (last_ref, rows // 2 - 1, rows - 1)):
        ref[pl.ds(before, sources)] = beyond[:, t]
        ref[pl.ds(after, sources)] = facing[:, t]
        for d in range(planes):
            ref[(d + 1) * sources : (d + 2) * sources] = tiles[:, d, t]
            ref[(planes + 2) * sources + d] = cot[d * rows + row]


def sum_kernel(blocks, out_ref):
    for r in range(blocks.shape[1]):
        total = blocks[0, r].astype(F32)
        for k in range(1, blocks.shape[0]):
            total = total + blocks[k, r].astype(F32)
        for k in range(out_ref.shape[0]):
            out_ref[k, r] = total.astype(BF16)


def pair_kernel(kept, other, out_ref):
    first = other.shape[0] - kept.shape[0]
    for r in range(kept.shape[0]):
        total = (kept[r].astype(F32) + other[first + r].astype(F32)).astype(BF16)
        for k in range(out_ref.shape[0]):
            out_ref[k, r] = total


def unpack_kernel(parts, out_ref, wide):
    pairs, size = parts.shape[1:3]
    count, lines = out_ref.shape[:2]
    for t in range(pairs):
        total = parts[0, t].astype(F32)
        for k in range(1, parts.shape[0]):
            total = total + parts[k, t].astype(F32)
        wide[t * size : (t + 1) * size] = total
    for c in range(count):
        out_ref[c] = wide[pl.ds(c, lines, stride=count), :].astype(BF16)


def forward_kernel(planes, rows, at_ref, bias_ref, w_ref, cot, tiles, facing, beyond, before, after, *refs):
    out_ref, face_ref, far_ref, kept_ref, grads, halves = refs
    cout, width = cot.shape[1:]
    sources = tiles.shape[0]
    edge = sources * (planes + 2)
    core = at_ref[0]
    even = core == 0

    def tile(s, p, t):
        if t == 0:
            return before[p * sources + s]
        if t == rows // 2 + 1:
            return after[p * sources + s]
        if p == 0:
            return jnp.where(even, beyond[s, t - 1], facing[s, t - 1])
        if p == planes + 1:
            return jnp.where(even, facing[s, t - 1], beyond[s, t - 1])
        return tiles[s, p - 1, t - 1]

    lane = lax.broadcasted_iota(jnp.int32, (cout, width), 1)
    channel = lax.broadcasted_iota(jnp.int32, (cout, width), 0)
    bias = jnp.zeros((cout, width), F32)
    for o in range(cout):
        bias = jnp.where(channel == o, bias_ref[o], bias)
    sums = [None] * 3
    bias_sum = jnp.zeros((cout, width), F32)
    for d in range(planes):
        for pair in range(rows // 2 + 1):
            cells = [
                jnp.concatenate(
                    [tile(s, d + kd, pair + t) for t in range(2) for s in range(sources)], axis=0
                )
                for kd in range(3)
            ]
            acc = jnp.dot(w_ref[0], cells[0], preferred_element_type=F32)
            for kd in range(1, 3):
                acc = acc + jnp.dot(w_ref[kd], cells[kd], preferred_element_type=F32)
            stacks = []
            for e in range(2):
                z = acc[3 * e * cout : 3 * (e + 1) * cout]
                pre = (
                    z[cout : 2 * cout]
                    + jnp.where(lane == 0, 0.0, pltpu.roll(z[:cout], 1, 1))
                    + jnp.where(lane == width - 1, 0.0, pltpu.roll(z[2 * cout :], width - 1, 1))
                    + bias
                )
                small = jnp.exp(-jnp.abs(pre))
                sigmoid = jnp.where(pre >= 0, 1.0, small) / (1.0 + small)
                row = 2 * pair + e
                if row == 0:
                    cotangent = before[edge + d]
                elif row == rows + 1:
                    cotangent = after[edge + d]
                else:
                    cotangent = cot[d * rows + row - 1]
                grad = (cotangent.astype(F32) * (0.2 + 0.8 * sigmoid)).astype(BF16)
                grads[d, row] = grad
                if row == 0 or row == rows + 1:
                    stacks.append(jnp.zeros((3 * cout, width), BF16))
                    continue
                softplus = jnp.maximum(pre, 0.0) + jnp.log1p(small)
                out_ref[d * rows + row - 1] = (0.2 * pre + 0.8 * softplus).astype(BF16)
                grad = grad.astype(F32)
                bias_sum = bias_sum + grad
                stacks.append(shifted(grad, lane).astype(BF16))
            both = jnp.concatenate(stacks, axis=0)
            for kd in range(3):
                term = lax.dot_general(
                    both, cells[kd], (((1,), (1,)), ((), ())), preferred_element_type=F32
                )
                sums[kd] = term if sums[kd] is None else sums[kd] + term

    first = (lane // PART) % 2 == 0
    blocks, last = [], []
    for kd in range(3):
        for kw in range(3):
            one = sums[kd][kw * cout : (kw + 1) * cout]
            two = sums[kd][(3 + kw) * cout : (4 + kw) * cout]
            back = pltpu.roll(two[:, width:], width - PART, 1)
            blocks.append(
                one[:, :width]
                + jnp.where(
                    first,
                    pltpu.roll(two[:, :width], width - PART, 1),
                    pltpu.roll(two[:, width:], PART, 1),
                )
            )
            last.append(one[:, width:] + back)
    last.append(jnp.broadcast_to(jnp.sum(bias_sum, axis=1, keepdims=True), (cout, width)))
    for k in range(0, len(last), 2):
        blocks.append(jnp.where(first, last[k], pltpu.roll(last[k + 1], PART, 1)))
    source = lax.broadcasted_iota(jnp.int32, (width, width), 0)
    target = (source // PART) % 2 * (width // 2) + source // (2 * PART) * PART + source % PART
    order = jnp.where(lax.broadcasted_iota(jnp.int32, (width, width), 1) == target, 1.0, 0.0).astype(BF16)
    placed = jnp.dot(jnp.concatenate(blocks, axis=0).astype(BF16), order, preferred_element_type=F32)
    count = len(blocks) // 2
    for k in range(2 * count):
        halves[k // count, k % count] = placed[k * cout : (k + 1) * cout].astype(BF16)
    face_ref[: rows + 2] = grads[1 - core]
    face_ref[rows + 2 :] = halves[1 - core]
    far_ref[...] = grads[core]
    kept_ref[...] = halves[core]


def backward_kernel(planes, rows, at_ref, w_ref, face, far, face_in, far_in, parts, stack):
    cout, width = far.shape[1:]
    cin = w_ref.shape[1]
    count = parts.shape[0]
    part = cin // count
    lane = lax.broadcasted_iota(jnp.int32, (cout, width), 1)
    step = 3 * cout
    core = at_ref[0]
    for q, source in enumerate((face_in, face, far, far_in)):
        p = jnp.where(core == 1, q, planes + 1 - q)
        for r in range(rows + 2):
            stack[p, r * step : (r + 1) * step, :] = shifted(source[r].astype(F32), lane).astype(BF16)
    w = jnp.transpose(w_ref[...].astype(F32)).astype(BF16)
    for d in range(planes):
        for h in range(0, rows, 2):
            cells = jnp.concatenate(
                [
                    jnp.concatenate(
                        [
                            stack[d + 2 - kd, (h + e + 2 - kh) * step : (h + e + 3 - kh) * step, :]
                            for kd in range(3)
                            for kh in range(3)
                        ],
                        axis=0,
                    )
                    for e in range(2)
                ],
                axis=1,
            )
            acc = jnp.dot(w, cells, preferred_element_type=F32)
            pair = (d * rows + h) // 2
            for f in range(count):
                piece = acc[f * part : (f + 1) * part]
                piece = jnp.concatenate([piece[:, :width], piece[:, width:]], axis=0).astype(BF16)
                parts[f, pair] = piece


def placing(cin):
    ones = np.zeros((2, 3, cin, 2, cin // PART, 2, PART), np.float32)
    for e in range(2):
        for kh in range(3):
            for i in range(cin):
                ones[e, kh, i, (kh + e) // 2, i // PART, (kh + e) % 2, i % PART] = 1
    return ones.reshape(2, 3 * cin, 4 * cin)


def weights_kernel(at_ref, mine, other, w_ref, b_ref):
    count, cout, width = mine.shape
    half = width // 2
    for k in range(2 * count):
        own = at_ref[0] == k // count
        block = jnp.where(own, mine[k % count].astype(F32), other[k % count].astype(F32))
        for e in range(2):
            piece = block[:, e * half : (e + 1) * half]
            at, kh = (k, e) if k < 9 else (2 * (k - 9) + e, 2)
            if at < 9:
                w_ref[at // 3 * 9 + kh * 3 + at % 3] = piece
    spare = block[:, half : half + cout]
    row = lax.broadcasted_iota(jnp.int32, (cout, cout), 0)
    lane = lax.broadcasted_iota(jnp.int32, (cout, cout), 1)
    b_ref[...] = jnp.sum(jnp.where(row == lane, spare, 0.0), axis=0, keepdims=True)


def call(body, name, *args, out, scratch=(), dtype=BF16, flops=0, moved=1 << 18, waves=0, scalars=0):
    smem, vmem = pl.BlockSpec(memory_space=pltpu.SMEM), pl.BlockSpec(memory_space=pltpu.VMEM)
    outs = tuple(jax.ShapeDtypeStruct(shape, dtype) for shape in out)
    results = pl.pallas_call(
        body,
        out_shape=outs,
        in_specs=[smem] * scalars + [vmem] * (len(args) - scalars),
        out_specs=(vmem,) * len(outs),
        scratch_shapes=[pltpu.VMEM(shape, kind) for shape, kind in scratch],
        compiler_params=pltpu.CompilerParams(vmem_limit_bytes=12 << 20),
        cost_estimate=pl.CostEstimate(flops=flops, bytes_accessed=moved, transcendentals=waves),
        name=name,
    )(*args)
    return results[0] if len(outs) == 1 else results


def per_device(activations, weights, bias, cotangent):
    cin_dev, planes, rows, width = activations.shape
    taps, cin, cout = weights.shape
    cells = planes * rows
    depth, height, filt = (lax.axis_size(axis) for axis in ("depth", "height", "filt"))
    swap = [(i, i ^ 1) for i in range(depth)]
    cross = [(i, i - 1 if i % 2 == 0 else i + 1) for i in range(1, depth - 1)]
    at = (lax.axis_index("depth") % 2).astype(jnp.int32).reshape(1)
    pairs, double = rows // 2, 2 * cin_dev

    grid = call(
        pack_kernel,
        "pack",
        activations.reshape(cin_dev, cells, width),
        out=[(filt, planes, pairs, double, width)],
        scratch=[((cin_dev * cells, width), F32)],
    )
    tiles = swapped(grid, "filt")
    work = 2 * cells * width * taps * cin * cout
    far, face = (
        call(
            functools.partial(plane_kernel, *order),
            "plane",
            at,
            tiles,
            out=[(filt, pairs, double, width)],
            flops=cost,
            scalars=1,
        )
        for order, cost in (((0, planes - 1), 0), ((planes - 1, 0), 64 * work))
    )
    beyond = lax.ppermute(far, "depth", cross)
    facing = lax.ppermute(face, "depth", swap)

    cot = cotangent.transpose(1, 2, 0, 3).reshape(cells, cout, width)
    split = weights.reshape(3, 3, 3, cin, cout)
    w_forward = jnp.einsum(
        "akj,ejn->aekn",
        split.transpose(0, 2, 4, 1, 3).reshape(3, 3 * cout, 3 * cin),
        jnp.asarray(placing(cin), BF16),
        preferred_element_type=F32,
    )
    w_forward = w_forward.astype(BF16).reshape(3, 6 * cout, 4 * cin)
    w_back = weights.transpose(0, 2, 1).reshape(taps * cout, cin)
    first, last = call(
        functools.partial(rows_kernel, planes, rows),
        "rows",
        at,
        tiles,
        facing,
        beyond,
        cot,
        out=[((planes + 2) * filt + planes, cout, width)] * 2,
        scalars=1,
    )
    first, last, w_forward = lax.optimization_barrier((first, last, w_forward))
    before, after = neighbours(first, last, "height")

    count = (taps + 1) // 4
    out, face, far, kept_sums = call(
        functools.partial(forward_kernel, planes, rows),
        "forward",
        at,
        bias,
        w_forward,
        cot,
        tiles,
        facing,
        beyond,
        before,
        after,
        out=[(k, cout, width) for k in (cells, rows + 2 + count, rows + 2, count)],
        scratch=[((planes, rows + 2, cout, width), BF16), ((2, count, cout, width), BF16)],
        flops=3 * work,
        waves=1 << 17,
        scalars=2,
    )
    output = out.reshape(planes, rows, cout, width).transpose(2, 0, 1, 3)

    size = kept_sums.shape
    face_in = lax.ppermute(face, "depth", swap)
    far_in = lax.ppermute(far, "depth", cross)
    sums = swapped(call(pair_kernel, "pair", kept_sums, face_in, out=[(height,) + size]), "height")
    parts = call(
        functools.partial(backward_kernel, planes, rows),
        "backward",
        at,
        w_back,
        face,
        far,
        face_in,
        far_in,
        out=[(filt, cells // 2, double, width)],
        scratch=[((planes + 2, (rows + 2) * 3 * cout, width), BF16)],
        flops=64 * work,
        scalars=1,
    )
    sums, parts = lax.optimization_barrier((sums, parts))
    groups = [[i for i in range(depth) if i % 2 == k] for k in range(2)]
    sums = swapped(call(sum_kernel, "sums", sums, out=[(depth // 2,) + size]), "depth", groups)
    sums, parts = lax.optimization_barrier((sums, parts))
    parts = swapped(parts, "filt")
    summed = call(
        unpack_kernel,
        "unpack",
        parts,
        out=[(cin_dev, cells, width)],
        scratch=[((cin_dev * cells, width), F32)],
    ).reshape(activations.shape)

    mine = call(sum_kernel, "sums", sums, out=[(1,) + size])[0]
    other = lax.ppermute(mine, "depth", swap)
    weight_grad, bias_grad = call(
        weights_kernel,
        "weights",
        at,
        mine,
        other,
        out=[(taps, cout, cin), (1, cout)],
        dtype=F32,
        scalars=1,
    )
    return (output, summed, weight_grad.transpose(0, 2, 1), bias_grad.reshape(cout))


def solution(mesh):
    placed = (
        P("filt", "depth", "height", None),
        P(None, None, "filt"),
        P("filt"),
        P("filt", "depth", "height", None),
    )
    return jax.shard_map(
        per_device,
        mesh=mesh,
        in_specs=placed,
        out_specs=(
            P("filt", "depth", "height", None),
            P("filt", "depth", "height", None),
            P(None, None, "filt"),
            P("filt"),
        ),
        check_vma=False,
    )
```

```python
import functools

import jax
import jax.numpy as jnp
import numpy as np
from jax import lax
from jax.experimental import pallas as pl
from jax.experimental.pallas import tpu as pltpu
from jax.sharding import PartitionSpec as P

BF16 = jnp.bfloat16
F32 = jnp.float32
PART = 8


def swapped(blocks, axis, groups=None):
    return lax.all_to_all(blocks, axis, 0, 0, tiled=True, axis_index_groups=groups)


def neighbours(first, last, axis):
    ends = lax.axis_size(axis) - 1
    before = lax.ppermute(last, axis, [(i, i + 1) for i in range(ends)])
    after = lax.ppermute(first, axis, [(i + 1, i) for i in range(ends)])
    return before, after


def shifted(value, lane):
    width = value.shape[-1]
    ahead = jnp.where(lane == width - 1, 0.0, pltpu.roll(value, width - 1, 1))
    behind = jnp.where(lane == 0, 0.0, pltpu.roll(value, 1, 1))
    return jnp.concatenate([ahead, value, behind], axis=0)


def pack_kernel(cells, out_ref, wide):
    planes, pairs = out_ref.shape[1:3]
    count, lines = cells.shape[:2]
    for c in range(count):
        wide[c * lines : (c + 1) * lines] = cells[c].astype(F32)
    for d in range(planes):
        for t in range(pairs):
            row = 2 * (d * pairs + t)
            tile = jnp.concatenate(
                [wide[pl.ds(row + e, count, stride=lines), :] for e in range(2)], axis=0
            ).astype(BF16)
            for k in range(out_ref.shape[0]):
                out_ref[k, d, t] = tile


def plane_kernel(even, odd, at_ref, tiles, out_ref):
    out_ref[...] = tiles[:, jnp.where(at_ref[0] == 0, even, odd)]


def rows_kernel(planes, rows, at_ref, tiles, facing, beyond, cot, first_ref, last_ref):
    core = at_ref[0]
    sources = tiles.shape[0]
    before = jnp.where(core == 0, 0, (planes + 1) * sources)
    after = (planes + 1) * sources - before
    for ref, t, row in ((first_ref, 0, 0), (last_ref, rows // 2 - 1, rows - 1)):
        ref[pl.ds(before, sources)] = beyond[:, t]
        ref[pl.ds(after, sources)] = facing[:, t]
        for d in range(planes):
            ref[(d + 1) * sources : (d + 2) * sources] = tiles[:, d, t]
            ref[(planes + 2) * sources + d] = cot[d * rows + row]


def sum_kernel(blocks, out_ref):
    for r in range(blocks.shape[1]):
        total = blocks[0, r].astype(F32)
        for k in range(1, blocks.shape[0]):
            total = total + blocks[k, r].astype(F32)
        for k in range(out_ref.shape[0]):
            out_ref[k, r] = total.astype(BF16)


def pair_kernel(kept, other, out_ref):
    first = other.shape[0] - kept.shape[0]
    for r in range(kept.shape[0]):
        total = (kept[r].astype(F32) + other[first + r].astype(F32)).astype(BF16)
        for k in range(out_ref.shape[0]):
            out_ref[k, r] = total


def unpack_kernel(parts, out_ref, wide):
    pairs, size = parts.shape[1:3]
    count, lines = out_ref.shape[:2]
    for t in range(pairs):
        total = parts[0, t].astype(F32)
        for k in range(1, parts.shape[0]):
            total = total + parts[k, t].astype(F32)
        wide[t * size : (t + 1) * size] = total
    for c in range(count):
        out_ref[c] = wide[pl.ds(c, lines, stride=count), :].astype(BF16)


def forward_kernel(planes, rows, at_ref, bias_ref, w_ref, cot, tiles, facing, beyond, before, after, *refs):
    out_ref, face_ref, far_ref, kept_ref, grads, halves = refs
    cout, width = cot.shape[1:]
    sources = tiles.shape[0]
    edge = sources * (planes + 2)
    core = at_ref[0]
    even = core == 0

    def tile(s, p, t):
        if t == 0:
            return before[p * sources + s]
        if t == rows // 2 + 1:
            return after[p * sources + s]
        if p == 0:
            return jnp.where(even, beyond[s, t - 1], facing[s, t - 1])
        if p == planes + 1:
            return jnp.where(even, facing[s, t - 1], beyond[s, t - 1])
        return tiles[s, p - 1, t - 1]

    lane = lax.broadcasted_iota(jnp.int32, (cout, width), 1)
    channel = lax.broadcasted_iota(jnp.int32, (cout, width), 0)
    bias = jnp.zeros((cout, width), F32)
    for o in range(cout):
        bias = jnp.where(channel == o, bias_ref[o], bias)
    lefts, rights = [], []
    bias_sum = jnp.zeros((cout, width), F32)
    for d in range(planes):
        for pair in range(rows // 2 + 1):
            cells = [
                jnp.concatenate(
                    [tile(s, d + kd, pair + t) for t in range(2) for s in range(sources)], axis=0
                )
                for kd in range(3)
            ]
            acc = jnp.dot(w_ref[0], cells[0], preferred_element_type=F32)
            for kd in range(1, 3):
                acc = acc + jnp.dot(w_ref[kd], cells[kd], preferred_element_type=F32)
            stacks = []
            for e in range(2):
                z = acc[3 * e * cout : 3 * (e + 1) * cout]
                pre = (
                    z[cout : 2 * cout]
                    + jnp.where(lane == 0, 0.0, pltpu.roll(z[:cout], 1, 1))
                    + jnp.where(lane == width - 1, 0.0, pltpu.roll(z[2 * cout :], width - 1, 1))
                    + bias
                )
                small = jnp.exp(-jnp.abs(pre))
                sigmoid = jnp.where(pre >= 0, 1.0, small) / (1.0 + small)
                row = 2 * pair + e
                if row == 0:
                    cotangent = before[edge + d]
                elif row == rows + 1:
                    cotangent = after[edge + d]
                else:
                    cotangent = cot[d * rows + row - 1]
                grad = (cotangent.astype(F32) * (0.2 + 0.8 * sigmoid)).astype(BF16)
                grads[d, row] = grad
                if row == 0 or row == rows + 1:
                    stacks.append(jnp.zeros((3 * cout, width), BF16))
                    continue
                softplus = jnp.maximum(pre, 0.0) + jnp.log1p(small)
                out_ref[d * rows + row - 1] = (0.2 * pre + 0.8 * softplus).astype(BF16)
                grad = grad.astype(F32)
                bias_sum = bias_sum + grad
                stacks.append(shifted(grad, lane).astype(BF16))
            lefts.append(jnp.concatenate(stacks, axis=0))
            rights.append(cells)
    left = jnp.concatenate(lefts, axis=1)
    sums = [
        lax.dot_general(
            left,
            jnp.concatenate([cells[kd] for cells in rights], axis=1),
            (((1,), (1,)), ((), ())),
            preferred_element_type=F32,
        )
        for kd in range(3)
    ]

    first = (lane // PART) % 2 == 0
    blocks, last = [], []
    for kd in range(3):
        for kw in range(3):
            one = sums[kd][kw * cout : (kw + 1) * cout]
            two = sums[kd][(3 + kw) * cout : (4 + kw) * cout]
            back = pltpu.roll(two[:, width:], width - PART, 1)
            blocks.append(
                one[:, :width]
                + jnp.where(
                    first,
                    pltpu.roll(two[:, :width], width - PART, 1),
                    pltpu.roll(two[:, width:], PART, 1),
                )
            )
            last.append(one[:, width:] + back)
    last.append(jnp.broadcast_to(jnp.sum(bias_sum, axis=1, keepdims=True), (cout, width)))
    for k in range(0, len(last), 2):
        blocks.append(jnp.where(first, last[k], pltpu.roll(last[k + 1], PART, 1)))
    source = lax.broadcasted_iota(jnp.int32, (width, width), 0)
    target = (source // PART) % 2 * (width // 2) + source // (2 * PART) * PART + source % PART
    order = jnp.where(lax.broadcasted_iota(jnp.int32, (width, width), 1) == target, 1.0, 0.0).astype(BF16)
    placed = jnp.dot(jnp.concatenate(blocks, axis=0).astype(BF16), order, preferred_element_type=F32)
    count = len(blocks) // 2
    for k in range(2 * count):
        halves[k // count, k % count] = placed[k * cout : (k + 1) * cout].astype(BF16)
    face_ref[: rows + 2] = grads[1 - core]
    face_ref[rows + 2 :] = halves[1 - core]
    far_ref[...] = grads[core]
    kept_ref[...] = halves[core]


def backward_kernel(planes, rows, at_ref, w_ref, face, far, face_in, far_in, parts, stack):
    cout, width = far.shape[1:]
    cin = w_ref.shape[1]
    count = parts.shape[0]
    part = cin // count
    lane = lax.broadcasted_iota(jnp.int32, (cout, width), 1)
    step = 3 * cout
    core = at_ref[0]
    for q, source in enumerate((face_in, face, far, far_in)):
        p = jnp.where(core == 1, q, planes + 1 - q)
        for r in range(rows + 2):
            stack[p, r * step : (r + 1) * step, :] = shifted(source[r].astype(F32), lane).astype(BF16)
    w = jnp.transpose(w_ref[...].astype(F32)).astype(BF16)
    for d in range(planes):
        for h in range(0, rows, 2):
            cells = jnp.concatenate(
                [
                    jnp.concatenate(
                        [
                            stack[d + 2 - kd, (h + e + 2 - kh) * step : (h + e + 3 - kh) * step, :]
                            for kd in range(3)
                            for kh in range(3)
                        ],
                        axis=0,
                    )
                    for e in range(2)
                ],
                axis=1,
            )
            acc = jnp.dot(w, cells, preferred_element_type=F32)
            pair = (d * rows + h) // 2
            for f in range(count):
                piece = acc[f * part : (f + 1) * part]
                piece = jnp.concatenate([piece[:, :width], piece[:, width:]], axis=0).astype(BF16)
                parts[f, pair] = piece


def placing(cin):
    ones = np.zeros((2, 3, cin, 2, cin // PART, 2, PART), np.float32)
    for e in range(2):
        for kh in range(3):
            for i in range(cin):
                ones[e, kh, i, (kh + e) // 2, i // PART, (kh + e) % 2, i % PART] = 1
    return ones.reshape(2, 3 * cin, 4 * cin)


def weights_kernel(at_ref, mine, other, w_ref, b_ref):
    count, cout, width = mine.shape
    half = width // 2
    for k in range(2 * count):
        own = at_ref[0] == k // count
        block = jnp.where(own, mine[k % count].astype(F32), other[k % count].astype(F32))
        for e in range(2):
            piece = block[:, e * half : (e + 1) * half]
            at, kh = (k, e) if k < 9 else (2 * (k - 9) + e, 2)
            if at < 9:
                w_ref[at // 3 * 9 + kh * 3 + at % 3] = piece
    spare = block[:, half : half + cout]
    row = lax.broadcasted_iota(jnp.int32, (cout, cout), 0)
    lane = lax.broadcasted_iota(jnp.int32, (cout, cout), 1)
    b_ref[...] = jnp.sum(jnp.where(row == lane, spare, 0.0), axis=0, keepdims=True)


def call(body, name, *args, out, scratch=(), dtype=BF16, flops=0, moved=1 << 18, waves=0, scalars=0):
    smem, vmem = pl.BlockSpec(memory_space=pltpu.SMEM), pl.BlockSpec(memory_space=pltpu.VMEM)
    outs = tuple(jax.ShapeDtypeStruct(shape, dtype) for shape in out)
    results = pl.pallas_call(
        body,
        out_shape=outs,
        in_specs=[smem] * scalars + [vmem] * (len(args) - scalars),
        out_specs=(vmem,) * len(outs),
        scratch_shapes=[pltpu.VMEM(shape, kind) for shape, kind in scratch],
        compiler_params=pltpu.CompilerParams(vmem_limit_bytes=12 << 20),
        cost_estimate=pl.CostEstimate(flops=flops, bytes_accessed=moved, transcendentals=waves),
        name=name,
    )(*args)
    return results[0] if len(outs) == 1 else results


def per_device(activations, weights, bias, cotangent):
    cin_dev, planes, rows, width = activations.shape
    taps, cin, cout = weights.shape
    cells = planes * rows
    depth, height, filt = (lax.axis_size(axis) for axis in ("depth", "height", "filt"))
    swap = [(i, i ^ 1) for i in range(depth)]
    cross = [(i, i - 1 if i % 2 == 0 else i + 1) for i in range(1, depth - 1)]
    at = (lax.axis_index("depth") % 2).astype(jnp.int32).reshape(1)
    pairs, double = rows // 2, 2 * cin_dev

    grid = call(
        pack_kernel,
        "pack",
        activations.reshape(cin_dev, cells, width),
        out=[(filt, planes, pairs, double, width)],
        scratch=[((cin_dev * cells, width), F32)],
    )
    tiles = swapped(grid, "filt")
    work = 2 * cells * width * taps * cin * cout
    far, face = (
        call(
            functools.partial(plane_kernel, *order),
            "plane",
            at,
            tiles,
            out=[(filt, pairs, double, width)],
            flops=cost,
            scalars=1,
        )
        for order, cost in (((0, planes - 1), 0), ((planes - 1, 0), 64 * work))
    )
    beyond = lax.ppermute(far, "depth", cross)
    facing = lax.ppermute(face, "depth", swap)

    cot = cotangent.transpose(1, 2, 0, 3).reshape(cells, cout, width)
    split = weights.reshape(3, 3, 3, cin, cout)
    w_forward = jnp.einsum(
        "akj,ejn->aekn",
        split.transpose(0, 2, 4, 1, 3).reshape(3, 3 * cout, 3 * cin),
        jnp.asarray(placing(cin), BF16),
        preferred_element_type=F32,
    )
    w_forward = w_forward.astype(BF16).reshape(3, 6 * cout, 4 * cin)
    w_back = weights.transpose(0, 2, 1).reshape(taps * cout, cin)
    first, last = call(
        functools.partial(rows_kernel, planes, rows),
        "rows",
        at,
        tiles,
        facing,
        beyond,
        cot,
        out=[((planes + 2) * filt + planes, cout, width)] * 2,
        scalars=1,
    )
    first, last, w_forward = lax.optimization_barrier((first, last, w_forward))
    before, after = neighbours(first, last, "height")

    count = (taps + 1) // 4
    out, face, far, kept_sums = call(
        functools.partial(forward_kernel, planes, rows),
        "forward",
        at,
        bias,
        w_forward,
        cot,
        tiles,
        facing,
        beyond,
        before,
        after,
        out=[(k, cout, width) for k in (cells, rows + 2 + count, rows + 2, count)],
        scratch=[((planes, rows + 2, cout, width), BF16), ((2, count, cout, width), BF16)],
        flops=3 * work,
        waves=1 << 17,
        scalars=2,
    )
    output = out.reshape(planes, rows, cout, width).transpose(2, 0, 1, 3)

    size = kept_sums.shape
    face_in = lax.ppermute(face, "depth", swap)
    far_in = lax.ppermute(far, "depth", cross)
    sums = swapped(call(pair_kernel, "pair", kept_sums, face_in, out=[(height,) + size]), "height")
    parts = call(
        functools.partial(backward_kernel, planes, rows),
        "backward",
        at,
        w_back,
        face,
        far,
        face_in,
        far_in,
        out=[(filt, cells // 2, double, width)],
        scratch=[((planes + 2, (rows + 2) * 3 * cout, width), BF16)],
        flops=64 * work,
        scalars=1,
    )
    sums, parts = lax.optimization_barrier((sums, parts))
    groups = [[i for i in range(depth) if i % 2 == k] for k in range(2)]
    sums = swapped(call(sum_kernel, "sums", sums, out=[(depth // 2,) + size]), "depth", groups)
    sums, parts = lax.optimization_barrier((sums, parts))
    parts = swapped(parts, "filt")
    summed = call(
        unpack_kernel,
        "unpack",
        parts,
        out=[(cin_dev, cells, width)],
        scratch=[((cin_dev * cells, width), F32)],
    ).reshape(activations.shape)

    mine = call(sum_kernel, "sums", sums, out=[(1,) + size])[0]
    other = lax.ppermute(mine, "depth", swap)
    weight_grad, bias_grad = call(
        weights_kernel,
        "weights",
        at,
        mine,
        other,
        out=[(taps, cout, cin), (1, cout)],
        dtype=F32,
        scalars=1,
    )
    return (output, summed, weight_grad.transpose(0, 2, 1), bias_grad.reshape(cout))


def solution(mesh):
    placed = (
        P("filt", "depth", "height", None),
        P(None, None, "filt"),
        P("filt"),
        P("filt", "depth", "height", None),
    )
    return jax.shard_map(
        per_device,
        mesh=mesh,
        in_specs=placed,
        out_specs=(
            P("filt", "depth", "height", None),
            P("filt", "depth", "height", None),
            P(None, None, "filt"),
            P("filt"),
        ),
        check_vma=False,
    )
```

```python
import functools

import jax
import jax.numpy as jnp
import numpy as np
from jax import lax
from jax.experimental import pallas as pl
from jax.experimental.pallas import tpu as pltpu
from jax.sharding import PartitionSpec as P

BF16 = jnp.bfloat16
F32 = jnp.float32
PART = 8


def swapped(blocks, axis, groups=None):
    return lax.all_to_all(blocks, axis, 0, 0, tiled=True, axis_index_groups=groups)


def neighbours(first, last, axis):
    ends = lax.axis_size(axis) - 1
    before = lax.ppermute(last, axis, [(i, i + 1) for i in range(ends)])
    after = lax.ppermute(first, axis, [(i + 1, i) for i in range(ends)])
    return before, after


def shifted(value, lane):
    width = value.shape[-1]
    ahead = jnp.where(lane == width - 1, 0.0, pltpu.roll(value, width - 1, 1))
    behind = jnp.where(lane == 0, 0.0, pltpu.roll(value, 1, 1))
    return jnp.concatenate([ahead, value, behind], axis=0)


def pack_kernel(at_ref, cells, own, far_ref, wide):
    planes, pairs = own.shape[:2]
    count, lines = cells.shape[:2]
    for c in range(count):
        wide[c * lines : (c + 1) * lines] = cells[c].astype(F32)
    for d in range(planes):
        for t in range(pairs):
            row = 2 * (d * pairs + t)
            own[d, t] = jnp.concatenate(
                [wide[pl.ds(row + e, count, stride=lines), :] for e in range(2)], axis=0
            ).astype(BF16)
    far_ref[...] = own[jnp.where(at_ref[0] == 0, 0, planes - 1)]


def face_kernel(at_ref, own, face_ref):
    face_ref[...] = own[jnp.where(at_ref[0] == 0, own.shape[0] - 1, 0)]


def grid_kernel(at_ref, own, facing, beyond, out_ref):
    planes = own.shape[0]
    before = jnp.where(at_ref[0] == 0, 0, planes + 1)
    for k in range(out_ref.shape[0]):
        for d in range(planes):
            out_ref[k, d + 1] = own[d]
        out_ref[k, before] = beyond[...]
        out_ref[k, planes + 1 - before] = facing[...]


def rows_kernel(rows, tiles, cot, first_ref, last_ref):
    sources, count = tiles.shape[:2]
    for ref, t, row in ((first_ref, 0, 0), (last_ref, rows // 2 - 1, rows - 1)):
        for p in range(count):
            ref[p * sources : (p + 1) * sources] = tiles[:, p, t]
        for d in range(count - 2):
            ref[count * sources + d] = cot[d * rows + row]


def sum_kernel(blocks, out_ref):
    for r in range(blocks.shape[1]):
        total = blocks[0, r].astype(F32)
        for k in range(1, blocks.shape[0]):
            total = total + blocks[k, r].astype(F32)
        for k in range(out_ref.shape[0]):
            out_ref[k, r] = total.astype(BF16)


def pair_kernel(kept, other, out_ref):
    first = other.shape[0] - kept.shape[0]
    for r in range(kept.shape[0]):
        total = (kept[r].astype(F32) + other[first + r].astype(F32)).astype(BF16)
        for k in range(out_ref.shape[0]):
            out_ref[k, r] = total


def unpack_kernel(parts, out_ref, wide):
    pairs, size = parts.shape[1:3]
    count, lines = out_ref.shape[:2]
    for t in range(pairs):
        total = parts[0, t].astype(F32)
        for k in range(1, parts.shape[0]):
            total = total + parts[k, t].astype(F32)
        wide[t * size : (t + 1) * size] = total
    for c in range(count):
        out_ref[c] = wide[pl.ds(c, lines, stride=count), :].astype(BF16)


def forward_kernel(planes, rows, at_ref, bias_ref, w_ref, cot, tiles, before, after, *refs):
    out_ref, face_ref, far_ref, kept_ref, grads, halves = refs
    cout, width = cot.shape[1:]
    sources = tiles.shape[0]
    edge = sources * (planes + 2)
    core = at_ref[0]

    def tile(s, p, t):
        if t == 0:
            return before[p * sources + s]
        if t == rows // 2 + 1:
            return after[p * sources + s]
        return tiles[s, p, t - 1]

    lane = lax.broadcasted_iota(jnp.int32, (cout, width), 1)
    channel = lax.broadcasted_iota(jnp.int32, (cout, width), 0)
    bias = jnp.zeros((cout, width), F32)
    for o in range(cout):
        bias = jnp.where(channel == o, bias_ref[o], bias)
    lefts, rights = [], []
    bias_sum = jnp.zeros((cout, width), F32)
    for d in range(planes):
        for pair in range(rows // 2 + 1):
            cells = [
                jnp.concatenate(
                    [tile(s, d + kd, pair + t) for t in range(2) for s in range(sources)], axis=0
                )
                for kd in range(3)
            ]
            acc = jnp.dot(w_ref[0], cells[0], preferred_element_type=F32)
            for kd in range(1, 3):
                acc = acc + jnp.dot(w_ref[kd], cells[kd], preferred_element_type=F32)
            stacks = []
            for e in range(2):
                z = acc[3 * e * cout : 3 * (e + 1) * cout]
                pre = (
                    z[cout : 2 * cout]
                    + jnp.where(lane == 0, 0.0, pltpu.roll(z[:cout], 1, 1))
                    + jnp.where(lane == width - 1, 0.0, pltpu.roll(z[2 * cout :], width - 1, 1))
                    + bias
                )
                small = jnp.exp(-jnp.abs(pre))
                sigmoid = jnp.where(pre >= 0, 1.0, small) / (1.0 + small)
                row = 2 * pair + e
                if row == 0:
                    cotangent = before[edge + d]
                elif row == rows + 1:
                    cotangent = after[edge + d]
                else:
                    cotangent = cot[d * rows + row - 1]
                grad = (cotangent.astype(F32) * (0.2 + 0.8 * sigmoid)).astype(BF16)
                grads[d, row] = grad
                if row == 0 or row == rows + 1:
                    stacks.append(jnp.zeros((3 * cout, width), BF16))
                    continue
                softplus = jnp.maximum(pre, 0.0) + jnp.log1p(small)
                out_ref[d * rows + row - 1] = (0.2 * pre + 0.8 * softplus).astype(BF16)
                grad = grad.astype(F32)
                bias_sum = bias_sum + grad
                stacks.append(shifted(grad, lane).astype(BF16))
            lefts.append(jnp.concatenate(stacks, axis=0))
            rights.append(cells)
    left = jnp.concatenate(lefts, axis=1)
    sums = [
        lax.dot_general(
            left,
            jnp.concatenate([cells[kd] for cells in rights], axis=1),
            (((1,), (1,)), ((), ())),
            preferred_element_type=F32,
        )
        for kd in range(3)
    ]

    first = (lane // PART) % 2 == 0
    blocks, last = [], []
    for kd in range(3):
        for kw in range(3):
            one = sums[kd][kw * cout : (kw + 1) * cout]
            two = sums[kd][(3 + kw) * cout : (4 + kw) * cout]
            back = pltpu.roll(two[:, width:], width - PART, 1)
            blocks.append(
                one[:, :width]
                + jnp.where(
                    first,
                    pltpu.roll(two[:, :width], width - PART, 1),
                    pltpu.roll(two[:, width:], PART, 1),
                )
            )
            last.append(one[:, width:] + back)
    last.append(jnp.broadcast_to(jnp.sum(bias_sum, axis=1, keepdims=True), (cout, width)))
    for k in range(0, len(last), 2):
        blocks.append(jnp.where(first, last[k], pltpu.roll(last[k + 1], PART, 1)))
    source = lax.broadcasted_iota(jnp.int32, (width, width), 0)
    target = (source // PART) % 2 * (width // 2) + source // (2 * PART) * PART + source % PART
    order = jnp.where(lax.broadcasted_iota(jnp.int32, (width, width), 1) == target, 1.0, 0.0).astype(BF16)
    placed = jnp.dot(jnp.concatenate(blocks, axis=0).astype(BF16), order, preferred_element_type=F32)
    count = len(blocks) // 2
    for k in range(2 * count):
        halves[k // count, k % count] = placed[k * cout : (k + 1) * cout].astype(BF16)
    face_ref[: rows + 2] = grads[1 - core]
    face_ref[rows + 2 :] = halves[1 - core]
    far_ref[...] = grads[core]
    kept_ref[...] = halves[core]


def backward_kernel(planes, rows, at_ref, w_ref, face, far, face_in, far_in, parts, stack):
    cout, width = far.shape[1:]
    cin = w_ref.shape[1]
    count = parts.shape[0]
    part = cin // count
    lane = lax.broadcasted_iota(jnp.int32, (cout, width), 1)
    step = 3 * cout
    core = at_ref[0]
    for q, source in enumerate((face_in, face, far, far_in)):
        p = jnp.where(core == 1, q, planes + 1 - q)
        for r in range(rows + 2):
            stack[p, r * step : (r + 1) * step, :] = shifted(source[r].astype(F32), lane).astype(BF16)
    w = jnp.transpose(w_ref[...].astype(F32)).astype(BF16)
    for d in range(planes):
        for h in range(0, rows, 2):
            cells = jnp.concatenate(
                [
                    jnp.concatenate(
                        [
                            stack[d + 2 - kd, (h + e + 2 - kh) * step : (h + e + 3 - kh) * step, :]
                            for kd in range(3)
                            for kh in range(3)
                        ],
                        axis=0,
                    )
                    for e in range(2)
                ],
                axis=1,
            )
            acc = jnp.dot(w, cells, preferred_element_type=F32)
            pair = (d * rows + h) // 2
            for f in range(count):
                piece = acc[f * part : (f + 1) * part]
                piece = jnp.concatenate([piece[:, :width], piece[:, width:]], axis=0).astype(BF16)
                parts[f, pair] = piece


def placing(cin):
    ones = np.zeros((2, 3, cin, 2, cin // PART, 2, PART), np.float32)
    for e in range(2):
        for kh in range(3):
            for i in range(cin):
                ones[e, kh, i, (kh + e) // 2, i // PART, (kh + e) % 2, i % PART] = 1
    return ones.reshape(2, 3 * cin, 4 * cin)


def weights_kernel(at_ref, mine, other, w_ref, b_ref):
    count, cout, width = mine.shape
    half = width // 2
    for k in range(2 * count):
        own = at_ref[0] == k // count
        block = jnp.where(own, mine[k % count].astype(F32), other[k % count].astype(F32))
        for e in range(2):
            piece = block[:, e * half : (e + 1) * half]
            at, kh = (k, e) if k < 9 else (2 * (k - 9) + e, 2)
            if at < 9:
                w_ref[at // 3 * 9 + kh * 3 + at % 3] = piece
    spare = block[:, half : half + cout]
    row = lax.broadcasted_iota(jnp.int32, (cout, cout), 0)
    lane = lax.broadcasted_iota(jnp.int32, (cout, cout), 1)
    b_ref[...] = jnp.sum(jnp.where(row == lane, spare, 0.0), axis=0, keepdims=True)


def call(body, name, *args, out, scratch=(), dtype=BF16, flops=0, moved=1 << 18, waves=0, scalars=0):
    smem, vmem = pl.BlockSpec(memory_space=pltpu.SMEM), pl.BlockSpec(memory_space=pltpu.VMEM)
    outs = tuple(jax.ShapeDtypeStruct(shape, dtype) for shape in out)
    results = pl.pallas_call(
        body,
        out_shape=outs,
        in_specs=[smem] * scalars + [vmem] * (len(args) - scalars),
        out_specs=(vmem,) * len(outs),
        scratch_shapes=[pltpu.VMEM(shape, kind) for shape, kind in scratch],
        compiler_params=pltpu.CompilerParams(vmem_limit_bytes=12 << 20),
        cost_estimate=pl.CostEstimate(flops=flops, bytes_accessed=moved, transcendentals=waves),
        name=name,
    )(*args)
    return results[0] if len(outs) == 1 else results


def per_device(activations, weights, bias, cotangent):
    cin_dev, planes, rows, width = activations.shape
    taps, cin, cout = weights.shape
    cells = planes * rows
    depth, height, filt = (lax.axis_size(axis) for axis in ("depth", "height", "filt"))
    swap = [(i, i ^ 1) for i in range(depth)]
    cross = [(i, i - 1 if i % 2 == 0 else i + 1) for i in range(1, depth - 1)]
    at = (lax.axis_index("depth") % 2).astype(jnp.int32).reshape(1)
    pairs, double = rows // 2, 2 * cin_dev

    work = 2 * cells * width * taps * cin * cout
    own, far = call(
        pack_kernel,
        "pack",
        at,
        activations.reshape(cin_dev, cells, width),
        out=[(planes, pairs, double, width), (pairs, double, width)],
        scratch=[((cin_dev * cells, width), F32)],
        scalars=1,
    )
    beyond = lax.ppermute(far, "depth", cross)
    face = call(face_kernel, "face", at, own, out=[far.shape], flops=64 * work, scalars=1)
    facing = lax.ppermute(face, "depth", swap)
    grid = call(
        grid_kernel,
        "grid",
        at,
        own,
        facing,
        beyond,
        out=[(filt, planes + 2, pairs, double, width)],
        scalars=1,
    )
    tiles = swapped(grid, "filt")

    cot = cotangent.transpose(1, 2, 0, 3).reshape(cells, cout, width)
    split = weights.reshape(3, 3, 3, cin, cout)
    w_forward = jnp.einsum(
        "akj,ejn->aekn",
        split.transpose(0, 2, 4, 1, 3).reshape(3, 3 * cout, 3 * cin),
        jnp.asarray(placing(cin), BF16),
        preferred_element_type=F32,
    )
    w_forward = w_forward.astype(BF16).reshape(3, 6 * cout, 4 * cin)
    w_back = weights.transpose(0, 2, 1).reshape(taps * cout, cin)
    first, last = call(
        functools.partial(rows_kernel, rows),
        "rows",
        tiles,
        cot,
        out=[((planes + 2) * filt + planes, cout, width)] * 2,
    )
    first, last, w_forward = lax.optimization_barrier((first, last, w_forward))
    before, after = neighbours(first, last, "height")

    count = (taps + 1) // 4
    out, face, far, kept_sums = call(
        functools.partial(forward_kernel, planes, rows),
        "forward",
        at,
        bias,
        w_forward,
        cot,
        tiles,
        before,
        after,
        out=[(k, cout, width) for k in (cells, rows + 2 + count, rows + 2, count)],
        scratch=[((planes, rows + 2, cout, width), BF16), ((2, count, cout, width), BF16)],
        flops=3 * work,
        waves=1 << 17,
        scalars=2,
    )
    output = out.reshape(planes, rows, cout, width).transpose(2, 0, 1, 3)

    size = kept_sums.shape
    face_in = lax.ppermute(face, "depth", swap)
    far_in = lax.ppermute(far, "depth", cross)
    sums = swapped(call(pair_kernel, "pair", kept_sums, face_in, out=[(height,) + size]), "height")
    parts = call(
        functools.partial(backward_kernel, planes, rows),
        "backward",
        at,
        w_back,
        face,
        far,
        face_in,
        far_in,
        out=[(filt, cells // 2, double, width)],
        scratch=[((planes + 2, (rows + 2) * 3 * cout, width), BF16)],
        flops=64 * work,
        scalars=1,
    )
    sums, parts = lax.optimization_barrier((sums, parts))
    groups = [[i for i in range(depth) if i % 2 == k] for k in range(2)]
    sums = swapped(call(sum_kernel, "sums", sums, out=[(depth // 2,) + size]), "depth", groups)
    sums, parts = lax.optimization_barrier((sums, parts))
    parts = swapped(parts, "filt")
    summed = call(
        unpack_kernel,
        "unpack",
        parts,
        out=[(cin_dev, cells, width)],
        scratch=[((cin_dev * cells, width), F32)],
    ).reshape(activations.shape)

    mine = call(sum_kernel, "sums", sums, out=[(1,) + size])[0]
    other = lax.ppermute(mine, "depth", swap)
    weight_grad, bias_grad = call(
        weights_kernel,
        "weights",
        at,
        mine,
        other,
        out=[(taps, cout, cin), (1, cout)],
        dtype=F32,
        scalars=1,
    )
    return (output, summed, weight_grad.transpose(0, 2, 1), bias_grad.reshape(cout))


def solution(mesh):
    placed = (
        P("filt", "depth", "height", None),
        P(None, None, "filt"),
        P("filt"),
        P("filt", "depth", "height", None),
    )
    return jax.shard_map(
        per_device,
        mesh=mesh,
        in_specs=placed,
        out_specs=(
            P("filt", "depth", "height", None),
            P("filt", "depth", "height", None),
            P(None, None, "filt"),
            P("filt"),
        ),
        check_vma=False,
    )
```

```python
import functools

import jax
import jax.numpy as jnp
import numpy as np
from jax import lax
from jax.experimental import pallas as pl
from jax.experimental.pallas import tpu as pltpu
from jax.sharding import PartitionSpec as P

BF16 = jnp.bfloat16
F32 = jnp.float32
PART = 8


def swapped(blocks, axis, groups=None):
    return lax.all_to_all(blocks, axis, 0, 0, tiled=True, axis_index_groups=groups)


def neighbours(first, last, axis):
    ends = lax.axis_size(axis) - 1
    before = lax.ppermute(last, axis, [(i, i + 1) for i in range(ends)])
    after = lax.ppermute(first, axis, [(i + 1, i) for i in range(ends)])
    return before, after


def shifted(value, lane):
    width = value.shape[-1]
    ahead = jnp.where(lane == width - 1, 0.0, pltpu.roll(value, width - 1, 1))
    behind = jnp.where(lane == 0, 0.0, pltpu.roll(value, 1, 1))
    return jnp.concatenate([ahead, value, behind], axis=0)


def pack_kernel(at_ref, cells, own, face_ref, wide):
    planes, pairs = own.shape[:2]
    count, lines = cells.shape[:2]
    for c in range(count):
        wide[c * lines : (c + 1) * lines] = cells[c].astype(F32)
    for d in range(planes):
        for t in range(pairs):
            row = 2 * (d * pairs + t)
            own[d, t] = jnp.concatenate(
                [wide[pl.ds(row + e, count, stride=lines), :] for e in range(2)], axis=0
            ).astype(BF16)
    face_ref[...] = own[jnp.where(at_ref[0] == 0, planes - 1, 0)]


def far_kernel(at_ref, own, far_ref):
    far_ref[...] = own[jnp.where(at_ref[0] == 0, 0, own.shape[0] - 1)]


def grid_kernel(at_ref, own, facing, beyond, out_ref):
    planes = own.shape[0]
    before = jnp.where(at_ref[0] == 0, 0, planes + 1)
    for k in range(out_ref.shape[0]):
        for d in range(planes):
            out_ref[k, d + 1] = own[d]
        out_ref[k, before] = beyond[...]
        out_ref[k, planes + 1 - before] = facing[...]


def rows_kernel(rows, tiles, cot, first_ref, last_ref):
    sources, count = tiles.shape[:2]
    for ref, t, row in ((first_ref, 0, 0), (last_ref, rows // 2 - 1, rows - 1)):
        for p in range(count):
            ref[p * sources : (p + 1) * sources] = tiles[:, p, t]
        for d in range(count - 2):
            ref[count * sources + d] = cot[d * rows + row]


def sum_kernel(blocks, out_ref):
    for r in range(blocks.shape[1]):
        total = blocks[0, r].astype(F32)
        for k in range(1, blocks.shape[0]):
            total = total + blocks[k, r].astype(F32)
        for k in range(out_ref.shape[0]):
            out_ref[k, r] = total.astype(BF16)


def pair_kernel(kept, other, out_ref):
    first = other.shape[0] - kept.shape[0]
    for r in range(kept.shape[0]):
        total = (kept[r].astype(F32) + other[first + r].astype(F32)).astype(BF16)
        for k in range(out_ref.shape[0]):
            out_ref[k, r] = total


def unpack_kernel(parts, out_ref, wide):
    pairs, size = parts.shape[1:3]
    count, lines = out_ref.shape[:2]
    for t in range(pairs):
        total = parts[0, t].astype(F32)
        for k in range(1, parts.shape[0]):
            total = total + parts[k, t].astype(F32)
        wide[t * size : (t + 1) * size] = total
    for c in range(count):
        out_ref[c] = wide[pl.ds(c, lines, stride=count), :].astype(BF16)


def forward_kernel(planes, rows, at_ref, bias_ref, w_ref, cot, tiles, before, after, *refs):
    out_ref, face_ref, far_ref, kept_ref, grads, halves = refs
    cout, width = cot.shape[1:]
    sources = tiles.shape[0]
    edge = sources * (planes + 2)
    core = at_ref[0]

    def tile(s, p, t):
        if t == 0:
            return before[p * sources + s]
        if t == rows // 2 + 1:
            return after[p * sources + s]
        return tiles[s, p, t - 1]

    lane = lax.broadcasted_iota(jnp.int32, (cout, width), 1)
    channel = lax.broadcasted_iota(jnp.int32, (cout, width), 0)
    bias = jnp.zeros((cout, width), F32)
    for o in range(cout):
        bias = jnp.where(channel == o, bias_ref[o], bias)
    lefts, rights = [], []
    bias_sum = jnp.zeros((cout, width), F32)
    for d in range(planes):
        for pair in range(rows // 2 + 1):
            cells = [
                jnp.concatenate(
                    [tile(s, d + kd, pair + t) for t in range(2) for s in range(sources)], axis=0
                )
                for kd in range(3)
            ]
            acc = jnp.dot(w_ref[0], cells[0], preferred_element_type=F32)
            for kd in range(1, 3):
                acc = acc + jnp.dot(w_ref[kd], cells[kd], preferred_element_type=F32)
            stacks = []
            for e in range(2):
                z = acc[3 * e * cout : 3 * (e + 1) * cout]
                pre = (
                    z[cout : 2 * cout]
                    + jnp.where(lane == 0, 0.0, pltpu.roll(z[:cout], 1, 1))
                    + jnp.where(lane == width - 1, 0.0, pltpu.roll(z[2 * cout :], width - 1, 1))
                    + bias
                )
                small = jnp.exp(-jnp.abs(pre))
                sigmoid = jnp.where(pre >= 0, 1.0, small) / (1.0 + small)
                row = 2 * pair + e
                if row == 0:
                    cotangent = before[edge + d]
                elif row == rows + 1:
                    cotangent = after[edge + d]
                else:
                    cotangent = cot[d * rows + row - 1]
                grad = (cotangent.astype(F32) * (0.2 + 0.8 * sigmoid)).astype(BF16)
                grads[d, row] = grad
                if row == 0 or row == rows + 1:
                    stacks.append(jnp.zeros((3 * cout, width), BF16))
                    continue
                softplus = jnp.maximum(pre, 0.0) + jnp.log1p(small)
                out_ref[d * rows + row - 1] = (0.2 * pre + 0.8 * softplus).astype(BF16)
                grad = grad.astype(F32)
                bias_sum = bias_sum + grad
                stacks.append(shifted(grad, lane).astype(BF16))
            lefts.append(jnp.concatenate(stacks, axis=0))
            rights.append(cells)
    left = jnp.concatenate(lefts, axis=1)
    sums = [
        lax.dot_general(
            left,
            jnp.concatenate([cells[kd] for cells in rights], axis=1),
            (((1,), (1,)), ((), ())),
            preferred_element_type=F32,
        )
        for kd in range(3)
    ]

    first = (lane // PART) % 2 == 0
    blocks, last = [], []
    for kd in range(3):
        for kw in range(3):
            one = sums[kd][kw * cout : (kw + 1) * cout]
            two = sums[kd][(3 + kw) * cout : (4 + kw) * cout]
            back = pltpu.roll(two[:, width:], width - PART, 1)
            blocks.append(
                one[:, :width]
                + jnp.where(
                    first,
                    pltpu.roll(two[:, :width], width - PART, 1),
                    pltpu.roll(two[:, width:], PART, 1),
                )
            )
            last.append(one[:, width:] + back)
    last.append(jnp.broadcast_to(jnp.sum(bias_sum, axis=1, keepdims=True), (cout, width)))
    for k in range(0, len(last), 2):
        blocks.append(jnp.where(first, last[k], pltpu.roll(last[k + 1], PART, 1)))
    source = lax.broadcasted_iota(jnp.int32, (width, width), 0)
    target = (source // PART) % 2 * (width // 2) + source // (2 * PART) * PART + source % PART
    order = jnp.where(lax.broadcasted_iota(jnp.int32, (width, width), 1) == target, 1.0, 0.0).astype(BF16)
    placed = jnp.dot(jnp.concatenate(blocks, axis=0).astype(BF16), order, preferred_element_type=F32)
    count = len(blocks) // 2
    for k in range(2 * count):
        halves[k // count, k % count] = placed[k * cout : (k + 1) * cout].astype(BF16)
    face_ref[: rows + 2] = grads[1 - core]
    face_ref[rows + 2 :] = halves[1 - core]
    far_ref[...] = grads[core]
    kept_ref[...] = halves[core]


def backward_kernel(planes, rows, at_ref, w_ref, face, far, face_in, far_in, parts, stack):
    cout, width = far.shape[1:]
    cin = w_ref.shape[1]
    count = parts.shape[0]
    part = cin // count
    lane = lax.broadcasted_iota(jnp.int32, (cout, width), 1)
    step = 3 * cout
    core = at_ref[0]
    for q, source in enumerate((face_in, face, far, far_in)):
        p = jnp.where(core == 1, q, planes + 1 - q)
        for r in range(rows + 2):
            stack[p, r * step : (r + 1) * step, :] = shifted(source[r].astype(F32), lane).astype(BF16)
    w = jnp.transpose(w_ref[...].astype(F32)).astype(BF16)
    for d in range(planes):
        for h in range(0, rows, 2):
            cells = jnp.concatenate(
                [
                    jnp.concatenate(
                        [
                            stack[d + 2 - kd, (h + e + 2 - kh) * step : (h + e + 3 - kh) * step, :]
                            for kd in range(3)
                            for kh in range(3)
                        ],
                        axis=0,
                    )
                    for e in range(2)
                ],
                axis=1,
            )
            acc = jnp.dot(w, cells, preferred_element_type=F32)
            pair = (d * rows + h) // 2
            for f in range(count):
                piece = acc[f * part : (f + 1) * part]
                piece = jnp.concatenate([piece[:, :width], piece[:, width:]], axis=0).astype(BF16)
                parts[f, pair] = piece


def placing(cin):
    ones = np.zeros((2, 3, cin, 2, cin // PART, 2, PART), np.float32)
    for e in range(2):
        for kh in range(3):
            for i in range(cin):
                ones[e, kh, i, (kh + e) // 2, i // PART, (kh + e) % 2, i % PART] = 1
    return ones.reshape(2, 3 * cin, 4 * cin)


def weights_kernel(at_ref, mine, other, w_ref, b_ref):
    count, cout, width = mine.shape
    half = width // 2
    for k in range(2 * count):
        own = at_ref[0] == k // count
        block = jnp.where(own, mine[k % count].astype(F32), other[k % count].astype(F32))
        for e in range(2):
            piece = block[:, e * half : (e + 1) * half]
            at, kh = (k, e) if k < 9 else (2 * (k - 9) + e, 2)
            if at < 9:
                w_ref[at // 3 * 9 + kh * 3 + at % 3] = piece
    spare = block[:, half : half + cout]
    row = lax.broadcasted_iota(jnp.int32, (cout, cout), 0)
    lane = lax.broadcasted_iota(jnp.int32, (cout, cout), 1)
    b_ref[...] = jnp.sum(jnp.where(row == lane, spare, 0.0), axis=0, keepdims=True)


def call(body, name, *args, out, scratch=(), dtype=BF16, flops=0, moved=1 << 18, waves=0, scalars=0):
    smem, vmem = pl.BlockSpec(memory_space=pltpu.SMEM), pl.BlockSpec(memory_space=pltpu.VMEM)
    outs = tuple(jax.ShapeDtypeStruct(shape, dtype) for shape in out)
    results = pl.pallas_call(
        body,
        out_shape=outs,
        in_specs=[smem] * scalars + [vmem] * (len(args) - scalars),
        out_specs=(vmem,) * len(outs),
        scratch_shapes=[pltpu.VMEM(shape, kind) for shape, kind in scratch],
        compiler_params=pltpu.CompilerParams(vmem_limit_bytes=12 << 20),
        cost_estimate=pl.CostEstimate(flops=flops, bytes_accessed=moved, transcendentals=waves),
        name=name,
    )(*args)
    return results[0] if len(outs) == 1 else results


def per_device(activations, weights, bias, cotangent):
    cin_dev, planes, rows, width = activations.shape
    taps, cin, cout = weights.shape
    cells = planes * rows
    depth, height, filt = (lax.axis_size(axis) for axis in ("depth", "height", "filt"))
    swap = [(i, i ^ 1) for i in range(depth)]
    cross = [(i, i - 1 if i % 2 == 0 else i + 1) for i in range(1, depth - 1)]
    at = (lax.axis_index("depth") % 2).astype(jnp.int32).reshape(1)
    pairs, double = rows // 2, 2 * cin_dev

    work = 2 * cells * width * taps * cin * cout
    own, face = call(
        pack_kernel,
        "pack",
        at,
        activations.reshape(cin_dev, cells, width),
        out=[(planes, pairs, double, width), (pairs, double, width)],
        scratch=[((cin_dev * cells, width), F32)],
        scalars=1,
    )
    facing = lax.ppermute(face, "depth", swap)
    far = call(far_kernel, "far", at, own, out=[face.shape], flops=64 * work, scalars=1)
    beyond = lax.ppermute(far, "depth", cross)
    grid = call(
        grid_kernel,
        "grid",
        at,
        own,
        facing,
        beyond,
        out=[(filt, planes + 2, pairs, double, width)],
        scalars=1,
    )
    tiles = swapped(grid, "filt")

    cot = cotangent.transpose(1, 2, 0, 3).reshape(cells, cout, width)
    split = weights.reshape(3, 3, 3, cin, cout)
    w_forward = jnp.einsum(
        "akj,ejn->aekn",
        split.transpose(0, 2, 4, 1, 3).reshape(3, 3 * cout, 3 * cin),
        jnp.asarray(placing(cin), BF16),
        preferred_element_type=F32,
    )
    w_forward = w_forward.astype(BF16).reshape(3, 6 * cout, 4 * cin)
    w_back = weights.transpose(0, 2, 1).reshape(taps * cout, cin)
    first, last = call(
        functools.partial(rows_kernel, rows),
        "rows",
        tiles,
        cot,
        out=[((planes + 2) * filt + planes, cout, width)] * 2,
    )
    first, last, w_forward = lax.optimization_barrier((first, last, w_forward))
    before, after = neighbours(first, last, "height")

    count = (taps + 1) // 4
    out, face, far, kept_sums = call(
        functools.partial(forward_kernel, planes, rows),
        "forward",
        at,
        bias,
        w_forward,
        cot,
        tiles,
        before,
        after,
        out=[(k, cout, width) for k in (cells, rows + 2 + count, rows + 2, count)],
        scratch=[((planes, rows + 2, cout, width), BF16), ((2, count, cout, width), BF16)],
        flops=3 * work,
        waves=1 << 17,
        scalars=2,
    )
    output = out.reshape(planes, rows, cout, width).transpose(2, 0, 1, 3)

    size = kept_sums.shape
    face_in = lax.ppermute(face, "depth", swap)
    far_in = lax.ppermute(far, "depth", cross)
    sums = swapped(call(pair_kernel, "pair", kept_sums, face_in, out=[(height,) + size]), "height")
    parts = call(
        functools.partial(backward_kernel, planes, rows),
        "backward",
        at,
        w_back,
        face,
        far,
        face_in,
        far_in,
        out=[(filt, cells // 2, double, width)],
        scratch=[((planes + 2, (rows + 2) * 3 * cout, width), BF16)],
        flops=64 * work,
        scalars=1,
    )
    sums, parts = lax.optimization_barrier((sums, parts))
    groups = [[i for i in range(depth) if i % 2 == k] for k in range(2)]
    sums = swapped(call(sum_kernel, "sums", sums, out=[(depth // 2,) + size]), "depth", groups)
    sums, parts = lax.optimization_barrier((sums, parts))
    parts = swapped(parts, "filt")
    summed = call(
        unpack_kernel,
        "unpack",
        parts,
        out=[(cin_dev, cells, width)],
        scratch=[((cin_dev * cells, width), F32)],
    ).reshape(activations.shape)

    mine = call(sum_kernel, "sums", sums, out=[(1,) + size])[0]
    other = lax.ppermute(mine, "depth", swap)
    weight_grad, bias_grad = call(
        weights_kernel,
        "weights",
        at,
        mine,
        other,
        out=[(taps, cout, cin), (1, cout)],
        dtype=F32,
        scalars=1,
    )
    return (output, summed, weight_grad.transpose(0, 2, 1), bias_grad.reshape(cout))


def solution(mesh):
    placed = (
        P("filt", "depth", "height", None),
        P(None, None, "filt"),
        P("filt"),
        P("filt", "depth", "height", None),
    )
    return jax.shard_map(
        per_device,
        mesh=mesh,
        in_specs=placed,
        out_specs=(
            P("filt", "depth", "height", None),
            P("filt", "depth", "height", None),
            P(None, None, "filt"),
            P("filt"),
        ),
        check_vma=False,
    )
```

```python
import functools

import jax
import jax.numpy as jnp
import numpy as np
from jax import lax
from jax.experimental import pallas as pl
from jax.experimental.pallas import tpu as pltpu
from jax.sharding import PartitionSpec as P

BF16 = jnp.bfloat16
F32 = jnp.float32
PART = 8


def swapped(blocks, axis, groups=None):
    return lax.all_to_all(blocks, axis, 0, 0, tiled=True, axis_index_groups=groups)


def neighbours(first, last, axis):
    ends = lax.axis_size(axis) - 1
    before = lax.ppermute(last, axis, [(i, i + 1) for i in range(ends)])
    after = lax.ppermute(first, axis, [(i + 1, i) for i in range(ends)])
    return before, after


def shifted(value, lane):
    width = value.shape[-1]
    ahead = jnp.where(lane == width - 1, 0.0, pltpu.roll(value, width - 1, 1))
    behind = jnp.where(lane == 0, 0.0, pltpu.roll(value, 1, 1))
    return jnp.concatenate([ahead, value, behind], axis=0)


def pack_kernel(at_ref, cells, own, face_ref, wide):
    planes, pairs = own.shape[:2]
    count, lines = cells.shape[:2]
    for c in range(count):
        wide[c * lines : (c + 1) * lines] = cells[c].astype(F32)
    for d in range(planes):
        for t in range(pairs):
            row = 2 * (d * pairs + t)
            own[d, t] = jnp.concatenate(
                [wide[pl.ds(row + e, count, stride=lines), :] for e in range(2)], axis=0
            ).astype(BF16)
    face_ref[...] = own[jnp.where(at_ref[0] == 0, planes - 1, 0)]


def far_kernel(at_ref, own, far_ref):
    far_ref[...] = own[jnp.where(at_ref[0] == 0, 0, own.shape[0] - 1)]


def grid_kernel(at_ref, own, facing, beyond, out_ref):
    planes = own.shape[0]
    before = jnp.where(at_ref[0] == 0, 0, planes + 1)
    for k in range(out_ref.shape[0]):
        for d in range(planes):
            out_ref[k, d + 1] = own[d]
        out_ref[k, before] = beyond[...]
        out_ref[k, planes + 1 - before] = facing[...]


def rows_kernel(rows, tiles, cot, first_ref, last_ref):
    sources, count = tiles.shape[:2]
    for ref, t, row in ((first_ref, 0, 0), (last_ref, rows // 2 - 1, rows - 1)):
        for p in range(count):
            ref[p * sources : (p + 1) * sources] = tiles[:, p, t]
        for d in range(count - 2):
            ref[count * sources + d] = cot[d * rows + row]


def sum_kernel(blocks, out_ref):
    for r in range(blocks.shape[1]):
        total = blocks[0, r].astype(F32)
        for k in range(1, blocks.shape[0]):
            total = total + blocks[k, r].astype(F32)
        for k in range(out_ref.shape[0]):
            out_ref[k, r] = total.astype(BF16)


def pair_kernel(kept, other, out_ref):
    first = other.shape[0] - kept.shape[0]
    for r in range(kept.shape[0]):
        total = (kept[r].astype(F32) + other[first + r].astype(F32)).astype(BF16)
        for k in range(out_ref.shape[0]):
            out_ref[k, r] = total


def unpack_kernel(parts, out_ref, wide):
    pairs, size = parts.shape[1:3]
    count, lines = out_ref.shape[:2]
    for t in range(pairs):
        total = parts[0, t].astype(F32)
        for k in range(1, parts.shape[0]):
            total = total + parts[k, t].astype(F32)
        wide[t * size : (t + 1) * size] = total
    for c in range(count):
        out_ref[c] = wide[pl.ds(c, lines, stride=count), :].astype(BF16)


def forward_kernel(planes, rows, at_ref, bias_ref, w_ref, cot, tiles, before, after, *refs):
    out_ref, face_ref, far_ref, kept_ref, grads, halves = refs
    cout, width = cot.shape[1:]
    sources = tiles.shape[0]
    edge = sources * (planes + 2)
    core = at_ref[0]

    def tile(s, p, t):
        if t == 0:
            return before[p * sources + s]
        if t == rows // 2 + 1:
            return after[p * sources + s]
        return tiles[s, p, t - 1]

    lane = lax.broadcasted_iota(jnp.int32, (cout, width), 1)
    channel = lax.broadcasted_iota(jnp.int32, (cout, width), 0)
    bias = jnp.zeros((cout, width), F32)
    for o in range(cout):
        bias = jnp.where(channel == o, bias_ref[o], bias)
    lefts, rights = [], []
    bias_sum = jnp.zeros((cout, width), F32)
    for d in range(planes):
        for pair in range(rows // 2 + 1):
            cells = [
                jnp.concatenate(
                    [tile(s, d + kd, pair + t) for t in range(2) for s in range(sources)], axis=0
                )
                for kd in range(3)
            ]
            acc = jnp.dot(w_ref[0], cells[0], preferred_element_type=F32)
            for kd in range(1, 3):
                acc = acc + jnp.dot(w_ref[kd], cells[kd], preferred_element_type=F32)
            stacks = []
            for e in range(2):
                z = acc[3 * e * cout : 3 * (e + 1) * cout]
                pre = (
                    z[cout : 2 * cout]
                    + jnp.where(lane == 0, 0.0, pltpu.roll(z[:cout], 1, 1))
                    + jnp.where(lane == width - 1, 0.0, pltpu.roll(z[2 * cout :], width - 1, 1))
                    + bias
                )
                small = jnp.exp(-jnp.abs(pre))
                sigmoid = jnp.where(pre >= 0, 1.0, small) / (1.0 + small)
                row = 2 * pair + e
                if row == 0:
                    cotangent = before[edge + d]
                elif row == rows + 1:
                    cotangent = after[edge + d]
                else:
                    cotangent = cot[d * rows + row - 1]
                grad = (cotangent.astype(F32) * (0.2 + 0.8 * sigmoid)).astype(BF16)
                grads[d, row] = grad
                if row == 0 or row == rows + 1:
                    stacks.append(jnp.zeros((3 * cout, width), BF16))
                    continue
                softplus = jnp.maximum(pre, 0.0) + jnp.log1p(small)
                out_ref[d * rows + row - 1] = (0.2 * pre + 0.8 * softplus).astype(BF16)
                grad = grad.astype(F32)
                bias_sum = bias_sum + grad
                stacks.append(shifted(grad, lane).astype(BF16))
            lefts.append(jnp.concatenate(stacks, axis=0))
            rights.append(cells)
    left = jnp.concatenate(lefts, axis=1)
    sums = [
        lax.dot_general(
            left,
            jnp.concatenate([cells[kd] for cells in rights], axis=1),
            (((1,), (1,)), ((), ())),
            preferred_element_type=F32,
        )
        for kd in range(3)
    ]

    first = (lane // PART) % 2 == 0
    blocks, last = [], []
    for kd in range(3):
        for kw in range(3):
            one = sums[kd][kw * cout : (kw + 1) * cout]
            two = sums[kd][(3 + kw) * cout : (4 + kw) * cout]
            back = pltpu.roll(two[:, width:], width - PART, 1)
            blocks.append(
                one[:, :width]
                + jnp.where(
                    first,
                    pltpu.roll(two[:, :width], width - PART, 1),
                    pltpu.roll(two[:, width:], PART, 1),
                )
            )
            last.append(one[:, width:] + back)
    last.append(jnp.broadcast_to(jnp.sum(bias_sum, axis=1, keepdims=True), (cout, width)))
    for k in range(0, len(last), 2):
        blocks.append(jnp.where(first, last[k], pltpu.roll(last[k + 1], PART, 1)))
    source = lax.broadcasted_iota(jnp.int32, (width, width), 0)
    target = (source // PART) % 2 * (width // 2) + source // (2 * PART) * PART + source % PART
    order = jnp.where(lax.broadcasted_iota(jnp.int32, (width, width), 1) == target, 1.0, 0.0).astype(BF16)
    placed = jnp.dot(jnp.concatenate(blocks, axis=0).astype(BF16), order, preferred_element_type=F32)
    count = len(blocks) // 2
    for k in range(2 * count):
        halves[k // count, k % count] = placed[k * cout : (k + 1) * cout].astype(BF16)
    face_ref[: rows + 2] = grads[1 - core]
    face_ref[rows + 2 :] = halves[1 - core]
    far_ref[...] = grads[core]
    kept_ref[...] = halves[core]


def backward_kernel(planes, rows, at_ref, w_ref, face, far, face_in, far_in, parts, stack):
    cout, width = far.shape[1:]
    cin = w_ref.shape[1]
    count = parts.shape[0]
    part = cin // count
    lane = lax.broadcasted_iota(jnp.int32, (cout, width), 1)
    step = 3 * cout
    core = at_ref[0]
    for q, source in enumerate((face_in, face, far, far_in)):
        p = jnp.where(core == 1, q, planes + 1 - q)
        for r in range(rows + 2):
            stack[p, r * step : (r + 1) * step, :] = shifted(source[r].astype(F32), lane).astype(BF16)
    w = jnp.transpose(w_ref[...].astype(F32)).astype(BF16)
    for d in range(planes):
        for h in range(0, rows, 2):
            cells = jnp.concatenate(
                [
                    jnp.concatenate(
                        [
                            stack[d + 2 - kd, (h + e + 2 - kh) * step : (h + e + 3 - kh) * step, :]
                            for kd in range(3)
                            for kh in range(3)
                        ],
                        axis=0,
                    )
                    for e in range(2)
                ],
                axis=1,
            )
            acc = jnp.dot(w, cells, preferred_element_type=F32)
            pair = (d * rows + h) // 2
            for f in range(count):
                piece = acc[f * part : (f + 1) * part]
                piece = jnp.concatenate([piece[:, :width], piece[:, width:]], axis=0).astype(BF16)
                parts[f, pair] = piece


def placing(cin):
    ones = np.zeros((2, 3, cin, 2, cin // PART, 2, PART), np.float32)
    for e in range(2):
        for kh in range(3):
            for i in range(cin):
                ones[e, kh, i, (kh + e) // 2, i // PART, (kh + e) % 2, i % PART] = 1
    return ones.reshape(2, 3 * cin, 4 * cin)


def weights_kernel(at_ref, mine, other, w_ref, b_ref):
    count, cout, width = mine.shape
    half = width // 2
    for k in range(2 * count):
        own = at_ref[0] == k // count
        block = jnp.where(own, mine[k % count].astype(F32), other[k % count].astype(F32))
        for e in range(2):
            piece = block[:, e * half : (e + 1) * half]
            at, kh = (k, e) if k < 9 else (2 * (k - 9) + e, 2)
            if at < 9:
                w_ref[at // 3 * 9 + kh * 3 + at % 3] = piece
    spare = block[:, half : half + cout]
    row = lax.broadcasted_iota(jnp.int32, (cout, cout), 0)
    lane = lax.broadcasted_iota(jnp.int32, (cout, cout), 1)
    b_ref[...] = jnp.sum(jnp.where(row == lane, spare, 0.0), axis=0, keepdims=True)


def call(body, name, *args, out, scratch=(), dtype=BF16, flops=0, moved=1 << 18, waves=0, scalars=0):
    smem, vmem = pl.BlockSpec(memory_space=pltpu.SMEM), pl.BlockSpec(memory_space=pltpu.VMEM)
    outs = tuple(jax.ShapeDtypeStruct(shape, dtype) for shape in out)
    results = pl.pallas_call(
        body,
        out_shape=outs,
        in_specs=[smem] * scalars + [vmem] * (len(args) - scalars),
        out_specs=(vmem,) * len(outs),
        scratch_shapes=[pltpu.VMEM(shape, kind) for shape, kind in scratch],
        compiler_params=pltpu.CompilerParams(vmem_limit_bytes=12 << 20),
        cost_estimate=pl.CostEstimate(flops=flops, bytes_accessed=moved, transcendentals=waves),
        name=name,
    )(*args)
    return results[0] if len(outs) == 1 else results


def per_device(activations, weights, bias, cotangent):
    cin_dev, planes, rows, width = activations.shape
    taps, cin, cout = weights.shape
    cells = planes * rows
    depth, height, filt = (lax.axis_size(axis) for axis in ("depth", "height", "filt"))
    swap = [(i, i ^ 1) for i in range(depth)]
    cross = [(i, i - 1 if i % 2 == 0 else i + 1) for i in range(1, depth - 1)]
    at = (lax.axis_index("depth") % 2).astype(jnp.int32).reshape(1)
    pairs, double = rows // 2, 2 * cin_dev

    work = 2 * cells * width * taps * cin * cout
    own, face = call(
        pack_kernel,
        "pack",
        at,
        activations.reshape(cin_dev, cells, width),
        out=[(planes, pairs, double, width), (pairs, double, width)],
        scratch=[((cin_dev * cells, width), F32)],
        scalars=1,
    )
    facing = lax.ppermute(face, "depth", swap)
    far = call(far_kernel, "far", at, own, out=[face.shape], flops=64 * work, scalars=1)
    beyond = lax.ppermute(far, "depth", cross)
    grid = call(
        grid_kernel,
        "grid",
        at,
        own,
        facing,
        beyond,
        out=[(filt, planes + 2, pairs, double, width)],
        scalars=1,
    )
    tiles = swapped(grid, "filt")

    cot = cotangent.transpose(1, 2, 0, 3).reshape(cells, cout, width)
    split = weights.reshape(3, 3, 3, cin, cout)
    w_forward = jnp.einsum(
        "akj,ejn->aekn",
        split.transpose(0, 2, 4, 1, 3).reshape(3, 3 * cout, 3 * cin),
        jnp.asarray(placing(cin), BF16),
        preferred_element_type=F32,
    )
    w_forward = w_forward.astype(BF16).reshape(3, 6 * cout, 4 * cin)
    w_back = weights.transpose(0, 2, 1).reshape(taps * cout, cin)
    first, last = call(
        functools.partial(rows_kernel, rows),
        "rows",
        tiles,
        cot,
        out=[((planes + 2) * filt + planes, cout, width)] * 2,
    )
    first, last, w_forward = lax.optimization_barrier((first, last, w_forward))
    before, after = neighbours(first, last, "height")

    count = (taps + 1) // 4
    out, face, far, kept_sums = call(
        functools.partial(forward_kernel, planes, rows),
        "forward",
        at,
        bias,
        w_forward,
        cot,
        tiles,
        before,
        after,
        out=[(k, cout, width) for k in (cells, rows + 2 + count, rows + 2, count)],
        scratch=[((planes, rows + 2, cout, width), BF16), ((2, count, cout, width), BF16)],
        flops=3 * work,
        waves=1 << 17,
        scalars=2,
    )
    output = out.reshape(planes, rows, cout, width).transpose(2, 0, 1, 3)

    size = kept_sums.shape
    face_in = lax.ppermute(face, "depth", swap)
    far_in = lax.ppermute(far, "depth", cross)
    sums = swapped(call(pair_kernel, "pair", kept_sums, face_in, out=[(height,) + size]), "height")
    parts = call(
        functools.partial(backward_kernel, planes, rows),
        "backward",
        at,
        w_back,
        face,
        far,
        face_in,
        far_in,
        out=[(filt, cells // 2, double, width)],
        scratch=[((planes + 2, (rows + 2) * 3 * cout, width), BF16)],
        flops=work,
        scalars=1,
    )
    sums, parts = lax.optimization_barrier((sums, parts))
    groups = [[i for i in range(depth) if i % 2 == k] for k in range(2)]
    sums = swapped(call(sum_kernel, "sums", sums, out=[(depth // 2,) + size]), "depth", groups)
    sums, parts = lax.optimization_barrier((sums, parts))
    parts = swapped(parts, "filt")
    summed = call(
        unpack_kernel,
        "unpack",
        parts,
        out=[(cin_dev, cells, width)],
        scratch=[((cin_dev * cells, width), F32)],
    ).reshape(activations.shape)

    mine = call(sum_kernel, "sums", sums, out=[(1,) + size])[0]
    other = lax.ppermute(mine, "depth", swap)
    weight_grad, bias_grad = call(
        weights_kernel,
        "weights",
        at,
        mine,
        other,
        out=[(taps, cout, cin), (1, cout)],
        dtype=F32,
        scalars=1,
    )
    return (output, summed, weight_grad.transpose(0, 2, 1), bias_grad.reshape(cout))


def solution(mesh):
    placed = (
        P("filt", "depth", "height", None),
        P(None, None, "filt"),
        P("filt"),
        P("filt", "depth", "height", None),
    )
    return jax.shard_map(
        per_device,
        mesh=mesh,
        in_specs=placed,
        out_specs=(
            P("filt", "depth", "height", None),
            P("filt", "depth", "height", None),
            P(None, None, "filt"),
            P("filt"),
        ),
        check_vma=False,
    )
```

```python
import functools

import jax
import jax.numpy as jnp
import numpy as np
from jax import lax
from jax.experimental import pallas as pl
from jax.experimental.pallas import tpu as pltpu
from jax.sharding import PartitionSpec as P

BF16 = jnp.bfloat16
F32 = jnp.float32
PART = 8


def swapped(blocks, axis, groups=None):
    return lax.all_to_all(blocks, axis, 0, 0, tiled=True, axis_index_groups=groups)


def neighbours(first, last, axis):
    ends = lax.axis_size(axis) - 1
    before = lax.ppermute(last, axis, [(i, i + 1) for i in range(ends)])
    after = lax.ppermute(first, axis, [(i + 1, i) for i in range(ends)])
    return before, after


def shifted(value, lane):
    width = value.shape[-1]
    ahead = jnp.where(lane == width - 1, 0.0, pltpu.roll(value, width - 1, 1))
    behind = jnp.where(lane == 0, 0.0, pltpu.roll(value, 1, 1))
    return jnp.concatenate([ahead, value, behind], axis=0)


def pack_kernel(at_ref, cells, own, face_ref, wide):
    planes, pairs = own.shape[:2]
    count, lines = cells.shape[:2]
    for c in range(count):
        wide[c * lines : (c + 1) * lines] = cells[c].astype(F32)
    for d in range(planes):
        for t in range(pairs):
            row = 2 * (d * pairs + t)
            own[d, t] = jnp.concatenate(
                [wide[pl.ds(row + e, count, stride=lines), :] for e in range(2)], axis=0
            ).astype(BF16)
    face_ref[...] = own[jnp.where(at_ref[0] == 0, planes - 1, 0)]


def far_kernel(at_ref, own, far_ref):
    far_ref[...] = own[jnp.where(at_ref[0] == 0, 0, own.shape[0] - 1)]


def grid_kernel(at_ref, own, facing, beyond, out_ref):
    planes = own.shape[0]
    before = jnp.where(at_ref[0] == 0, 0, planes + 1)
    for k in range(out_ref.shape[0]):
        for d in range(planes):
            out_ref[k, d + 1] = own[d]
        out_ref[k, before] = beyond[...]
        out_ref[k, planes + 1 - before] = facing[...]


def rows_kernel(rows, tiles, cot, first_ref, last_ref):
    sources, count = tiles.shape[:2]
    for ref, t, row in ((first_ref, 0, 0), (last_ref, rows // 2 - 1, rows - 1)):
        for p in range(count):
            ref[p * sources : (p + 1) * sources] = tiles[:, p, t]
        for d in range(count - 2):
            ref[count * sources + d] = cot[d * rows + row]


def sum_kernel(blocks, out_ref):
    for r in range(blocks.shape[1]):
        total = blocks[0, r].astype(F32)
        for k in range(1, blocks.shape[0]):
            total = total + blocks[k, r].astype(F32)
        for k in range(out_ref.shape[0]):
            out_ref[k, r] = total.astype(BF16)


def pair_kernel(kept, other, out_ref):
    first = other.shape[0] - kept.shape[0]
    for r in range(kept.shape[0]):
        total = (kept[r].astype(F32) + other[first + r].astype(F32)).astype(BF16)
        for k in range(out_ref.shape[0]):
            out_ref[k, r] = total


def unpack_kernel(parts, out_ref, wide):
    pairs, size = parts.shape[1:3]
    count, lines = out_ref.shape[:2]
    for t in range(pairs):
        total = parts[0, t].astype(F32)
        for k in range(1, parts.shape[0]):
            total = total + parts[k, t].astype(F32)
        wide[t * size : (t + 1) * size] = total
    for c in range(count):
        out_ref[c] = wide[pl.ds(c, lines, stride=count), :].astype(BF16)


def forward_kernel(planes, rows, at_ref, bias_ref, w_ref, cot, tiles, before, after, *refs):
    out_ref, face_ref, far_ref, kept_ref, grads, halves = refs
    cout, width = cot.shape[1:]
    sources = tiles.shape[0]
    edge = sources * (planes + 2)
    core = at_ref[0]

    def tile(s, p, t):
        if t == 0:
            return before[p * sources + s]
        if t == rows // 2 + 1:
            return after[p * sources + s]
        return tiles[s, p, t - 1]

    lane = lax.broadcasted_iota(jnp.int32, (cout, width), 1)
    channel = lax.broadcasted_iota(jnp.int32, (cout, width), 0)
    bias = jnp.zeros((cout, width), F32)
    for o in range(cout):
        bias = jnp.where(channel == o, bias_ref[o], bias)
    lefts, rights = [], []
    bias_sum = jnp.zeros((cout, width), F32)
    for d in range(planes):
        for pair in range(rows // 2 + 1):
            cells = [
                jnp.concatenate(
                    [tile(s, d + kd, pair + t) for t in range(2) for s in range(sources)], axis=0
                )
                for kd in range(3)
            ]
            acc = jnp.dot(w_ref[0], cells[0], preferred_element_type=F32)
            for kd in range(1, 3):
                acc = acc + jnp.dot(w_ref[kd], cells[kd], preferred_element_type=F32)
            stacks = []
            for e in range(2):
                z = acc[3 * e * cout : 3 * (e + 1) * cout]
                pre = (
                    z[cout : 2 * cout]
                    + jnp.where(lane == 0, 0.0, pltpu.roll(z[:cout], 1, 1))
                    + jnp.where(lane == width - 1, 0.0, pltpu.roll(z[2 * cout :], width - 1, 1))
                    + bias
                )
                small = jnp.exp(-jnp.abs(pre))
                sigmoid = jnp.where(pre >= 0, 1.0, small) / (1.0 + small)
                row = 2 * pair + e
                if row == 0:
                    cotangent = before[edge + d]
                elif row == rows + 1:
                    cotangent = after[edge + d]
                else:
                    cotangent = cot[d * rows + row - 1]
                grad = (cotangent.astype(F32) * (0.2 + 0.8 * sigmoid)).astype(BF16)
                grads[d, row] = grad
                if row == 0 or row == rows + 1:
                    stacks.append(jnp.zeros((3 * cout, width), BF16))
                    continue
                softplus = jnp.maximum(pre, 0.0) + jnp.log1p(small)
                out_ref[d * rows + row - 1] = (0.2 * pre + 0.8 * softplus).astype(BF16)
                grad = grad.astype(F32)
                bias_sum = bias_sum + grad
                stacks.append(shifted(grad, lane).astype(BF16))
            lefts.append(jnp.concatenate(stacks, axis=0))
            rights.append(cells)
    left = jnp.concatenate(lefts, axis=1)
    sums = [
        lax.dot_general(
            left,
            jnp.concatenate([cells[kd] for cells in rights], axis=1),
            (((1,), (1,)), ((), ())),
            preferred_element_type=F32,
        )
        for kd in range(3)
    ]

    first = (lane // PART) % 2 == 0
    blocks, last = [], []
    for kd in range(3):
        for kw in range(3):
            one = sums[kd][kw * cout : (kw + 1) * cout]
            two = sums[kd][(3 + kw) * cout : (4 + kw) * cout]
            back = pltpu.roll(two[:, width:], width - PART, 1)
            blocks.append(
                one[:, :width]
                + jnp.where(
                    first,
                    pltpu.roll(two[:, :width], width - PART, 1),
                    pltpu.roll(two[:, width:], PART, 1),
                )
            )
            last.append(one[:, width:] + back)
    last.append(jnp.broadcast_to(jnp.sum(bias_sum, axis=1, keepdims=True), (cout, width)))
    for k in range(0, len(last), 2):
        blocks.append(jnp.where(first, last[k], pltpu.roll(last[k + 1], PART, 1)))
    source = lax.broadcasted_iota(jnp.int32, (width, width), 0)
    target = (source // PART) % 2 * (width // 2) + source // (2 * PART) * PART + source % PART
    order = jnp.where(lax.broadcasted_iota(jnp.int32, (width, width), 1) == target, 1.0, 0.0).astype(BF16)
    placed = jnp.dot(jnp.concatenate(blocks, axis=0).astype(BF16), order, preferred_element_type=F32)
    count = len(blocks) // 2
    for k in range(2 * count):
        halves[k // count, k % count] = placed[k * cout : (k + 1) * cout].astype(BF16)
    face_ref[: rows + 2] = grads[1 - core]
    face_ref[rows + 2 :] = halves[1 - core]
    far_ref[...] = grads[core]
    kept_ref[...] = halves[core]


def backward_kernel(planes, rows, at_ref, w_ref, face, far, face_in, far_in, parts, stack):
    cout, width = far.shape[1:]
    cin = w_ref.shape[1]
    count = parts.shape[0]
    part = cin // count
    lane = lax.broadcasted_iota(jnp.int32, (cout, width), 1)
    step = 3 * cout
    core = at_ref[0]
    for q, source in enumerate((face_in, face, far, far_in)):
        p = jnp.where(core == 1, q, planes + 1 - q)
        for r in range(rows + 2):
            stack[p, r * step : (r + 1) * step, :] = shifted(source[r].astype(F32), lane).astype(BF16)
    w = jnp.transpose(w_ref[...].astype(F32)).astype(BF16)
    for d in range(planes):
        for h in range(0, rows, 2):
            cells = jnp.concatenate(
                [
                    jnp.concatenate(
                        [
                            stack[d + 2 - kd, (h + e + 2 - kh) * step : (h + e + 3 - kh) * step, :]
                            for kd in range(3)
                            for kh in range(3)
                        ],
                        axis=0,
                    )
                    for e in range(2)
                ],
                axis=1,
            )
            acc = jnp.dot(w, cells, preferred_element_type=F32)
            pair = (d * rows + h) // 2
            for f in range(count):
                piece = acc[f * part : (f + 1) * part]
                piece = jnp.concatenate([piece[:, :width], piece[:, width:]], axis=0).astype(BF16)
                parts[f, pair] = piece


def placing(cin):
    ones = np.zeros((2, 3, cin, 2, cin // PART, 2, PART), np.float32)
    for e in range(2):
        for kh in range(3):
            for i in range(cin):
                ones[e, kh, i, (kh + e) // 2, i // PART, (kh + e) % 2, i % PART] = 1
    return ones.reshape(2, 3 * cin, 4 * cin)


def weights_kernel(at_ref, mine, other, w_ref, b_ref):
    count, cout, width = mine.shape
    half = width // 2
    for k in range(2 * count):
        own = at_ref[0] == k // count
        block = jnp.where(own, mine[k % count].astype(F32), other[k % count].astype(F32))
        for e in range(2):
            piece = block[:, e * half : (e + 1) * half]
            at, kh = (k, e) if k < 9 else (2 * (k - 9) + e, 2)
            if at < 9:
                w_ref[at // 3 * 9 + kh * 3 + at % 3] = piece
    spare = block[:, half : half + cout]
    row = lax.broadcasted_iota(jnp.int32, (cout, cout), 0)
    lane = lax.broadcasted_iota(jnp.int32, (cout, cout), 1)
    b_ref[...] = jnp.sum(jnp.where(row == lane, spare, 0.0), axis=0, keepdims=True)


def call(body, name, *args, out, scratch=(), dtype=BF16, flops=0, moved=1 << 18, waves=0, scalars=0):
    smem, vmem = pl.BlockSpec(memory_space=pltpu.SMEM), pl.BlockSpec(memory_space=pltpu.VMEM)
    outs = tuple(jax.ShapeDtypeStruct(shape, dtype) for shape in out)
    results = pl.pallas_call(
        body,
        out_shape=outs,
        in_specs=[smem] * scalars + [vmem] * (len(args) - scalars),
        out_specs=(vmem,) * len(outs),
        scratch_shapes=[pltpu.VMEM(shape, kind) for shape, kind in scratch],
        compiler_params=pltpu.CompilerParams(vmem_limit_bytes=12 << 20),
        cost_estimate=pl.CostEstimate(flops=flops, bytes_accessed=moved, transcendentals=waves),
        name=name,
    )(*args)
    return results[0] if len(outs) == 1 else results


def per_device(activations, weights, bias, cotangent):
    cin_dev, planes, rows, width = activations.shape
    taps, cin, cout = weights.shape
    cells = planes * rows
    depth, height, filt = (lax.axis_size(axis) for axis in ("depth", "height", "filt"))
    swap = [(i, i ^ 1) for i in range(depth)]
    cross = [(i, i - 1 if i % 2 == 0 else i + 1) for i in range(1, depth - 1)]
    at = (lax.axis_index("depth") % 2).astype(jnp.int32).reshape(1)
    pairs, double = rows // 2, 2 * cin_dev

    work = 2 * cells * width * taps * cin * cout
    own, face = call(
        pack_kernel,
        "pack",
        at,
        activations.reshape(cin_dev, cells, width),
        out=[(planes, pairs, double, width), (pairs, double, width)],
        scratch=[((cin_dev * cells, width), F32)],
        scalars=1,
    )
    facing = lax.ppermute(face, "depth", swap)
    far = call(far_kernel, "far", at, own, out=[face.shape], flops=64 * work, scalars=1)
    beyond = lax.ppermute(far, "depth", cross)
    grid = call(
        grid_kernel,
        "grid",
        at,
        own,
        facing,
        beyond,
        out=[(filt, planes + 2, pairs, double, width)],
        scalars=1,
    )
    tiles = swapped(grid, "filt")

    cot = cotangent.transpose(1, 2, 0, 3).reshape(cells, cout, width)
    split = weights.reshape(3, 3, 3, cin, cout)
    w_forward = jnp.einsum(
        "akj,ejn->aekn",
        split.transpose(0, 2, 4, 1, 3).reshape(3, 3 * cout, 3 * cin),
        jnp.asarray(placing(cin), BF16),
        preferred_element_type=F32,
    )
    w_forward = w_forward.astype(BF16).reshape(3, 6 * cout, 4 * cin)
    w_back = weights.transpose(0, 2, 1).reshape(taps * cout, cin)
    first, last = call(
        functools.partial(rows_kernel, rows),
        "rows",
        tiles,
        cot,
        out=[((planes + 2) * filt + planes, cout, width)] * 2,
    )
    first, last, w_forward = lax.optimization_barrier((first, last, w_forward))
    before, after = neighbours(first, last, "height")

    count = (taps + 1) // 4
    out, face, far, kept_sums = call(
        functools.partial(forward_kernel, planes, rows),
        "forward",
        at,
        bias,
        w_forward,
        cot,
        tiles,
        before,
        after,
        out=[(k, cout, width) for k in (cells, rows + 2 + count, rows + 2, count)],
        scratch=[((planes, rows + 2, cout, width), BF16), ((2, count, cout, width), BF16)],
        flops=3 * work,
        waves=1 << 17,
        scalars=2,
    )
    output = out.reshape(planes, rows, cout, width).transpose(2, 0, 1, 3)

    size = kept_sums.shape
    face_in = lax.ppermute(face, "depth", swap)
    far_in = lax.ppermute(far, "depth", cross)
    sums = swapped(call(pair_kernel, "pair", kept_sums, face_in, out=[(height,) + size]), "height")
    parts = call(
        functools.partial(backward_kernel, planes, rows),
        "backward",
        at,
        w_back,
        face,
        far,
        face_in,
        far_in,
        out=[(filt, cells // 2, double, width)],
        scratch=[((planes + 2, (rows + 2) * 3 * cout, width), BF16)],
        flops=64 * work,
        scalars=1,
    )
    groups = [[i for i in range(depth) if i % 2 == k] for k in range(2)]
    sums = swapped(call(sum_kernel, "sums", sums, out=[(depth // 2,) + size]), "depth", groups)
    sums, parts = lax.optimization_barrier((sums, parts))
    parts = swapped(parts, "filt")
    summed = call(
        unpack_kernel,
        "unpack",
        parts,
        out=[(cin_dev, cells, width)],
        scratch=[((cin_dev * cells, width), F32)],
    ).reshape(activations.shape)

    mine = call(sum_kernel, "sums", sums, out=[(1,) + size])[0]
    other = lax.ppermute(mine, "depth", swap)
    weight_grad, bias_grad = call(
        weights_kernel,
        "weights",
        at,
        mine,
        other,
        out=[(taps, cout, cin), (1, cout)],
        dtype=F32,
        scalars=1,
    )
    return (output, summed, weight_grad.transpose(0, 2, 1), bias_grad.reshape(cout))


def solution(mesh):
    placed = (
        P("filt", "depth", "height", None),
        P(None, None, "filt"),
        P("filt"),
        P("filt", "depth", "height", None),
    )
    return jax.shard_map(
        per_device,
        mesh=mesh,
        in_specs=placed,
        out_specs=(
            P("filt", "depth", "height", None),
            P("filt", "depth", "height", None),
            P(None, None, "filt"),
            P("filt"),
        ),
        check_vma=False,
    )
```

```python
import functools

import jax
import jax.numpy as jnp
import numpy as np
from jax import lax
from jax.experimental import pallas as pl
from jax.experimental.pallas import tpu as pltpu
from jax.sharding import PartitionSpec as P

BF16 = jnp.bfloat16
F32 = jnp.float32
PART = 8


def swapped(blocks, axis, groups=None):
    return lax.all_to_all(blocks, axis, 0, 0, tiled=True, axis_index_groups=groups)


def neighbours(first, last, axis):
    ends = lax.axis_size(axis) - 1
    before = lax.ppermute(last, axis, [(i, i + 1) for i in range(ends)])
    after = lax.ppermute(first, axis, [(i + 1, i) for i in range(ends)])
    return before, after


def shifted(value, lane):
    width = value.shape[-1]
    ahead = jnp.where(lane == width - 1, 0.0, pltpu.roll(value, width - 1, 1))
    behind = jnp.where(lane == 0, 0.0, pltpu.roll(value, 1, 1))
    return jnp.concatenate([ahead, value, behind], axis=0)


def pack_kernel(at_ref, cells, own, face_ref, wide):
    planes, pairs = own.shape[:2]
    count, lines = cells.shape[:2]
    for c in range(count):
        wide[c * lines : (c + 1) * lines] = cells[c].astype(F32)
    for d in range(planes):
        for t in range(pairs):
            row = 2 * (d * pairs + t)
            own[d, t] = jnp.concatenate(
                [wide[pl.ds(row + e, count, stride=lines), :] for e in range(2)], axis=0
            ).astype(BF16)
    face_ref[...] = own[jnp.where(at_ref[0] == 0, planes - 1, 0)]


def far_kernel(at_ref, own, far_ref):
    far_ref[...] = own[jnp.where(at_ref[0] == 0, 0, own.shape[0] - 1)]


def grid_kernel(at_ref, own, facing, beyond, out_ref):
    planes = own.shape[0]
    before = jnp.where(at_ref[0] == 0, 0, planes + 1)
    for k in range(out_ref.shape[0]):
        for d in range(planes):
            out_ref[k, d + 1] = own[d]
        out_ref[k, before] = beyond[...]
        out_ref[k, planes + 1 - before] = facing[...]


def rows_kernel(rows, tiles, cot, first_ref, last_ref):
    sources, count = tiles.shape[:2]
    for ref, t, row in ((first_ref, 0, 0), (last_ref, rows // 2 - 1, rows - 1)):
        for p in range(count):
            ref[p * sources : (p + 1) * sources] = tiles[:, p, t]
        for d in range(count - 2):
            ref[count * sources + d] = cot[d * rows + row]


def sum_kernel(blocks, out_ref):
    for r in range(blocks.shape[1]):
        total = blocks[0, r].astype(F32)
        for k in range(1, blocks.shape[0]):
            total = total + blocks[k, r].astype(F32)
        for k in range(out_ref.shape[0]):
            out_ref[k, r] = total.astype(BF16)


def pair_kernel(kept, other, out_ref):
    first = other.shape[0] - kept.shape[0]
    for r in range(kept.shape[0]):
        total = (kept[r].astype(F32) + other[first + r].astype(F32)).astype(BF16)
        for k in range(out_ref.shape[0]):
            out_ref[k, r] = total


def unpack_kernel(parts, out_ref, wide):
    pairs, size = parts.shape[1:3]
    count, lines = out_ref.shape[:2]
    for t in range(pairs):
        total = parts[0, t].astype(F32)
        for k in range(1, parts.shape[0]):
            total = total + parts[k, t].astype(F32)
        wide[t * size : (t + 1) * size] = total
    for c in range(count):
        out_ref[c] = wide[pl.ds(c, lines, stride=count), :].astype(BF16)


def forward_kernel(planes, rows, at_ref, bias_ref, w_ref, cot, tiles, before, after, *refs):
    out_ref, face_ref, far_ref, kept_ref, grads, halves = refs
    cout, width = cot.shape[1:]
    sources = tiles.shape[0]
    edge = sources * (planes + 2)
    core = at_ref[0]

    def tile(s, p, t):
        if t == 0:
            return before[p * sources + s]
        if t == rows // 2 + 1:
            return after[p * sources + s]
        return tiles[s, p, t - 1]

    lane = lax.broadcasted_iota(jnp.int32, (cout, width), 1)
    channel = lax.broadcasted_iota(jnp.int32, (cout, width), 0)
    bias = jnp.zeros((cout, width), F32)
    for o in range(cout):
        bias = jnp.where(channel == o, bias_ref[o], bias)
    lefts, rights = [], []
    bias_sum = jnp.zeros((cout, width), F32)
    for d in range(planes):
        for pair in range(rows // 2 + 1):
            cells = [
                jnp.concatenate(
                    [tile(s, d + kd, pair + t) for t in range(2) for s in range(sources)], axis=0
                )
                for kd in range(3)
            ]
            acc = jnp.dot(w_ref[0], cells[0], preferred_element_type=F32)
            for kd in range(1, 3):
                acc = acc + jnp.dot(w_ref[kd], cells[kd], preferred_element_type=F32)
            stacks = []
            for e in range(2):
                z = acc[3 * e * cout : 3 * (e + 1) * cout]
                pre = (
                    z[cout : 2 * cout]
                    + jnp.where(lane == 0, 0.0, pltpu.roll(z[:cout], 1, 1))
                    + jnp.where(lane == width - 1, 0.0, pltpu.roll(z[2 * cout :], width - 1, 1))
                    + bias
                )
                small = jnp.exp(-jnp.abs(pre))
                sigmoid = jnp.where(pre >= 0, 1.0, small) / (1.0 + small)
                row = 2 * pair + e
                if row == 0:
                    cotangent = before[edge + d]
                elif row == rows + 1:
                    cotangent = after[edge + d]
                else:
                    cotangent = cot[d * rows + row - 1]
                grad = (cotangent.astype(F32) * (0.2 + 0.8 * sigmoid)).astype(BF16)
                grads[d, row] = grad
                if row == 0 or row == rows + 1:
                    stacks.append(jnp.zeros((3 * cout, width), BF16))
                    continue
                softplus = jnp.maximum(pre, 0.0) + jnp.log1p(small)
                out_ref[d * rows + row - 1] = (0.2 * pre + 0.8 * softplus).astype(BF16)
                grad = grad.astype(F32)
                bias_sum = bias_sum + grad
                stacks.append(shifted(grad, lane).astype(BF16))
            lefts.append(jnp.concatenate(stacks, axis=0))
            rights.append(cells)
    left = jnp.concatenate(lefts, axis=1)
    sums = [
        lax.dot_general(
            left,
            jnp.concatenate([cells[kd] for cells in rights], axis=1),
            (((1,), (1,)), ((), ())),
            preferred_element_type=F32,
        )
        for kd in range(3)
    ]

    first = (lane // PART) % 2 == 0
    blocks, last = [], []
    for kd in range(3):
        for kw in range(3):
            one = sums[kd][kw * cout : (kw + 1) * cout]
            two = sums[kd][(3 + kw) * cout : (4 + kw) * cout]
            back = pltpu.roll(two[:, width:], width - PART, 1)
            blocks.append(
                one[:, :width]
                + jnp.where(
                    first,
                    pltpu.roll(two[:, :width], width - PART, 1),
                    pltpu.roll(two[:, width:], PART, 1),
                )
            )
            last.append(one[:, width:] + back)
    last.append(jnp.broadcast_to(jnp.sum(bias_sum, axis=1, keepdims=True), (cout, width)))
    for k in range(0, len(last), 2):
        blocks.append(jnp.where(first, last[k], pltpu.roll(last[k + 1], PART, 1)))
    source = lax.broadcasted_iota(jnp.int32, (width, width), 0)
    target = (source // PART) % 2 * (width // 2) + source // (2 * PART) * PART + source % PART
    order = jnp.where(lax.broadcasted_iota(jnp.int32, (width, width), 1) == target, 1.0, 0.0).astype(BF16)
    placed = jnp.dot(jnp.concatenate(blocks, axis=0).astype(BF16), order, preferred_element_type=F32)
    count = len(blocks) // 2
    for k in range(2 * count):
        halves[k // count, k % count] = placed[k * cout : (k + 1) * cout].astype(BF16)
    face_ref[: rows + 2] = grads[1 - core]
    face_ref[rows + 2 :] = halves[1 - core]
    far_ref[...] = grads[core]
    kept_ref[...] = halves[core]


def backward_kernel(planes, rows, at_ref, w_ref, face, far, face_in, far_in, parts, stack):
    cout, width = far.shape[1:]
    cin = w_ref.shape[1]
    count = parts.shape[0]
    part = cin // count
    lane = lax.broadcasted_iota(jnp.int32, (cout, width), 1)
    step = 3 * cout
    core = at_ref[0]
    for q, source in enumerate((face_in, face, far, far_in)):
        p = jnp.where(core == 1, q, planes + 1 - q)
        for r in range(rows + 2):
            stack[p, r * step : (r + 1) * step, :] = shifted(source[r].astype(F32), lane).astype(BF16)
    w = jnp.transpose(w_ref[...].astype(F32)).astype(BF16)
    for d in range(planes):
        for h in range(0, rows, 2):
            cells = jnp.concatenate(
                [
                    jnp.concatenate(
                        [
                            stack[d + 2 - kd, (h + e + 2 - kh) * step : (h + e + 3 - kh) * step, :]
                            for kd in range(3)
                            for kh in range(3)
                        ],
                        axis=0,
                    )
                    for e in range(2)
                ],
                axis=1,
            )
            acc = jnp.dot(w, cells, preferred_element_type=F32)
            pair = (d * rows + h) // 2
            for f in range(count):
                piece = acc[f * part : (f + 1) * part]
                piece = jnp.concatenate([piece[:, :width], piece[:, width:]], axis=0).astype(BF16)
                parts[f, pair] = piece


def placing(cin):
    ones = np.zeros((2, 3, cin, 2, cin // PART, 2, PART), np.float32)
    for e in range(2):
        for kh in range(3):
            for i in range(cin):
                ones[e, kh, i, (kh + e) // 2, i // PART, (kh + e) % 2, i % PART] = 1
    return ones.reshape(2, 3 * cin, 4 * cin)


def weights_kernel(at_ref, mine, other, w_ref, b_ref):
    count, cout, width = mine.shape
    half = width // 2
    for k in range(2 * count):
        own = at_ref[0] == k // count
        block = jnp.where(own, mine[k % count].astype(F32), other[k % count].astype(F32))
        for e in range(2):
            piece = block[:, e * half : (e + 1) * half]
            at, kh = (k, e) if k < 9 else (2 * (k - 9) + e, 2)
            if at < 9:
                w_ref[at // 3 * 9 + kh * 3 + at % 3] = piece
    spare = block[:, half : half + cout]
    row = lax.broadcasted_iota(jnp.int32, (cout, cout), 0)
    lane = lax.broadcasted_iota(jnp.int32, (cout, cout), 1)
    b_ref[...] = jnp.sum(jnp.where(row == lane, spare, 0.0), axis=0, keepdims=True)


def call(body, name, *args, out, scratch=(), dtype=BF16, flops=0, moved=1 << 18, waves=0, scalars=0):
    smem, vmem = pl.BlockSpec(memory_space=pltpu.SMEM), pl.BlockSpec(memory_space=pltpu.VMEM)
    outs = tuple(jax.ShapeDtypeStruct(shape, dtype) for shape in out)
    results = pl.pallas_call(
        body,
        out_shape=outs,
        in_specs=[smem] * scalars + [vmem] * (len(args) - scalars),
        out_specs=(vmem,) * len(outs),
        scratch_shapes=[pltpu.VMEM(shape, kind) for shape, kind in scratch],
        compiler_params=pltpu.CompilerParams(vmem_limit_bytes=12 << 20),
        cost_estimate=pl.CostEstimate(flops=flops, bytes_accessed=moved, transcendentals=waves),
        name=name,
    )(*args)
    return results[0] if len(outs) == 1 else results


def per_device(activations, weights, bias, cotangent):
    cin_dev, planes, rows, width = activations.shape
    taps, cin, cout = weights.shape
    cells = planes * rows
    depth, height, filt = (lax.axis_size(axis) for axis in ("depth", "height", "filt"))
    swap = [(i, i ^ 1) for i in range(depth)]
    cross = [(i, i - 1 if i % 2 == 0 else i + 1) for i in range(1, depth - 1)]
    at = (lax.axis_index("depth") % 2).astype(jnp.int32).reshape(1)
    pairs, double = rows // 2, 2 * cin_dev

    work = 2 * cells * width * taps * cin * cout
    own, face = call(
        pack_kernel,
        "pack",
        at,
        activations.reshape(cin_dev, cells, width),
        out=[(planes, pairs, double, width), (pairs, double, width)],
        scratch=[((cin_dev * cells, width), F32)],
        scalars=1,
    )
    facing = lax.ppermute(face, "depth", swap)
    far = call(far_kernel, "far", at, own, out=[face.shape], flops=64 * work, scalars=1)
    beyond = lax.ppermute(far, "depth", cross)
    grid = call(
        grid_kernel,
        "grid",
        at,
        own,
        facing,
        beyond,
        out=[(filt, planes + 2, pairs, double, width)],
        scalars=1,
    )
    tiles = swapped(grid, "filt")

    cot = cotangent.transpose(1, 2, 0, 3).reshape(cells, cout, width)
    split = weights.reshape(3, 3, 3, cin, cout)
    w_forward = jnp.einsum(
        "akj,ejn->aekn",
        split.transpose(0, 2, 4, 1, 3).reshape(3, 3 * cout, 3 * cin),
        jnp.asarray(placing(cin), BF16),
        preferred_element_type=F32,
    )
    w_forward = w_forward.astype(BF16).reshape(3, 6 * cout, 4 * cin)
    w_back = weights.transpose(0, 2, 1).reshape(taps * cout, cin)
    first, last = call(
        functools.partial(rows_kernel, rows),
        "rows",
        tiles,
        cot,
        out=[((planes + 2) * filt + planes, cout, width)] * 2,
    )
    first, last, w_forward = lax.optimization_barrier((first, last, w_forward))
    before, after = neighbours(first, last, "height")

    count = (taps + 1) // 4
    out, face, far, kept_sums = call(
        functools.partial(forward_kernel, planes, rows),
        "forward",
        at,
        bias,
        w_forward,
        cot,
        tiles,
        before,
        after,
        out=[(k, cout, width) for k in (cells, rows + 2 + count, rows + 2, count)],
        scratch=[((planes, rows + 2, cout, width), BF16), ((2, count, cout, width), BF16)],
        flops=3 * work,
        waves=1 << 17,
        scalars=2,
    )
    output = out.reshape(planes, rows, cout, width).transpose(2, 0, 1, 3)

    size = kept_sums.shape
    face_in = lax.ppermute(face, "depth", swap)
    far_in = lax.ppermute(far, "depth", cross)
    groups = [[(i + height - 2) % height for i in range(height)]]
    sums = call(pair_kernel, "pair", kept_sums, face_in, out=[(height,) + size])
    sums = swapped(sums, "height", groups)
    parts = call(
        functools.partial(backward_kernel, planes, rows),
        "backward",
        at,
        w_back,
        face,
        far,
        face_in,
        far_in,
        out=[(filt, cells // 2, double, width)],
        scratch=[((planes + 2, (rows + 2) * 3 * cout, width), BF16)],
        flops=64 * work,
        scalars=1,
    )
    groups = [[(i + depth // 2) % depth for i in range(k, depth, 2)] for k in range(2)]
    sums = swapped(call(sum_kernel, "sums", sums, out=[(depth // 2,) + size]), "depth", groups)
    sums, parts = lax.optimization_barrier((sums, parts))
    parts = swapped(parts, "filt")
    summed = call(
        unpack_kernel,
        "unpack",
        parts,
        out=[(cin_dev, cells, width)],
        scratch=[((cin_dev * cells, width), F32)],
    ).reshape(activations.shape)

    mine = call(sum_kernel, "sums", sums, out=[(1,) + size])[0]
    other = lax.ppermute(mine, "depth", swap)
    weight_grad, bias_grad = call(
        weights_kernel,
        "weights",
        at,
        mine,
        other,
        out=[(taps, cout, cin), (1, cout)],
        dtype=F32,
        scalars=1,
    )
    return (output, summed, weight_grad.transpose(0, 2, 1), bias_grad.reshape(cout))


def solution(mesh):
    placed = (
        P("filt", "depth", "height", None),
        P(None, None, "filt"),
        P("filt"),
        P("filt", "depth", "height", None),
    )
    return jax.shard_map(
        per_device,
        mesh=mesh,
        in_specs=placed,
        out_specs=(
            P("filt", "depth", "height", None),
            P("filt", "depth", "height", None),
            P(None, None, "filt"),
            P("filt"),
        ),
        check_vma=False,
    )
```

```python
import functools

import jax
import jax.numpy as jnp
import numpy as np
from jax import lax
from jax.experimental import pallas as pl
from jax.experimental.pallas import tpu as pltpu
from jax.sharding import PartitionSpec as P

BF16 = jnp.bfloat16
F32 = jnp.float32
PART = 8


def swapped(blocks, axis, groups=None):
    return lax.all_to_all(blocks, axis, 0, 0, tiled=True, axis_index_groups=groups)


def neighbours(first, last, axis):
    ends = lax.axis_size(axis) - 1
    before = lax.ppermute(last, axis, [(i, i + 1) for i in range(ends)])
    after = lax.ppermute(first, axis, [(i + 1, i) for i in range(ends)])
    return before, after


def shifted(value, lane):
    width = value.shape[-1]
    ahead = jnp.where(lane == width - 1, 0.0, pltpu.roll(value, width - 1, 1))
    behind = jnp.where(lane == 0, 0.0, pltpu.roll(value, 1, 1))
    return jnp.concatenate([ahead, value, behind], axis=0)


def pack_kernel(at_ref, cells, own, face_ref, wide):
    planes, pairs = own.shape[:2]
    count, lines = cells.shape[:2]
    for c in range(count):
        wide[c * lines : (c + 1) * lines] = cells[c].astype(F32)
    for d in range(planes):
        for t in range(pairs):
            row = 2 * (d * pairs + t)
            own[d, t] = jnp.concatenate(
                [wide[pl.ds(row + e, count, stride=lines), :] for e in range(2)], axis=0
            ).astype(BF16)
    face_ref[...] = own[jnp.where(at_ref[0] == 0, planes - 1, 0)]


def far_kernel(at_ref, own, far_ref):
    far_ref[...] = own[jnp.where(at_ref[0] == 0, 0, own.shape[0] - 1)]


def grid_kernel(at_ref, own, facing, beyond, out_ref):
    planes = own.shape[0]
    before = jnp.where(at_ref[0] == 0, 0, planes + 1)
    for k in range(out_ref.shape[0]):
        for d in range(planes):
            out_ref[k, d + 1] = own[d]
        out_ref[k, before] = beyond[...]
        out_ref[k, planes + 1 - before] = facing[...]


def rows_kernel(rows, tiles, cot, first_ref, last_ref):
    sources, count = tiles.shape[:2]
    for ref, t, row in ((first_ref, 0, 0), (last_ref, rows // 2 - 1, rows - 1)):
        for p in range(count):
            ref[p * sources : (p + 1) * sources] = tiles[:, p, t]
        for d in range(count - 2):
            ref[count * sources + d] = cot[d * rows + row]


def sum_kernel(blocks, out_ref):
    for r in range(blocks.shape[1]):
        total = blocks[0, r].astype(F32)
        for k in range(1, blocks.shape[0]):
            total = total + blocks[k, r].astype(F32)
        for k in range(out_ref.shape[0]):
            out_ref[k, r] = total.astype(BF16)


def pair_kernel(kept, other, out_ref):
    first = other.shape[0] - kept.shape[0]
    for r in range(kept.shape[0]):
        total = (kept[r].astype(F32) + other[first + r].astype(F32)).astype(BF16)
        for k in range(out_ref.shape[0]):
            out_ref[k, r] = total


def unpack_kernel(parts, out_ref, wide):
    pairs, size = parts.shape[1:3]
    count, lines = out_ref.shape[:2]
    for t in range(pairs):
        total = parts[0, t].astype(F32)
        for k in range(1, parts.shape[0]):
            total = total + parts[k, t].astype(F32)
        wide[t * size : (t + 1) * size] = total
    for c in range(count):
        out_ref[c] = wide[pl.ds(c, lines, stride=count), :].astype(BF16)


def forward_kernel(planes, rows, at_ref, bias_ref, w_ref, cot, tiles, before, after, *refs):
    out_ref, face_ref, far_ref, kept_ref, grads, halves = refs
    cout, width = cot.shape[1:]
    sources = tiles.shape[0]
    edge = sources * (planes + 2)
    core = at_ref[0]

    def tile(s, p, t):
        if t == 0:
            return before[p * sources + s]
        if t == rows // 2 + 1:
            return after[p * sources + s]
        return tiles[s, p, t - 1]

    lane = lax.broadcasted_iota(jnp.int32, (cout, width), 1)
    channel = lax.broadcasted_iota(jnp.int32, (cout, width), 0)
    bias = jnp.zeros((cout, width), F32)
    for o in range(cout):
        bias = jnp.where(channel == o, bias_ref[o], bias)
    lefts, rights = [], []
    bias_sum = jnp.zeros((cout, width), F32)
    for d in range(planes):
        for pair in range(rows // 2 + 1):
            cells = [
                jnp.concatenate(
                    [tile(s, d + kd, pair + t) for t in range(2) for s in range(sources)], axis=0
                )
                for kd in range(3)
            ]
            acc = jnp.dot(w_ref[0], cells[0], preferred_element_type=F32)
            for kd in range(1, 3):
                acc = acc + jnp.dot(w_ref[kd], cells[kd], preferred_element_type=F32)
            stacks = []
            for e in range(2):
                z = acc[3 * e * cout : 3 * (e + 1) * cout]
                pre = (
                    z[cout : 2 * cout]
                    + jnp.where(lane == 0, 0.0, pltpu.roll(z[:cout], 1, 1))
                    + jnp.where(lane == width - 1, 0.0, pltpu.roll(z[2 * cout :], width - 1, 1))
                    + bias
                )
                small = jnp.exp(-jnp.abs(pre))
                sigmoid = jnp.where(pre >= 0, 1.0, small) / (1.0 + small)
                row = 2 * pair + e
                if row == 0:
                    cotangent = before[edge + d]
                elif row == rows + 1:
                    cotangent = after[edge + d]
                else:
                    cotangent = cot[d * rows + row - 1]
                grad = (cotangent.astype(F32) * (0.2 + 0.8 * sigmoid)).astype(BF16)
                grads[d, row] = grad
                if row == 0 or row == rows + 1:
                    stacks.append(jnp.zeros((3 * cout, width), BF16))
                    continue
                softplus = jnp.maximum(pre, 0.0) + jnp.log1p(small)
                out_ref[d * rows + row - 1] = (0.2 * pre + 0.8 * softplus).astype(BF16)
                grad = grad.astype(F32)
                bias_sum = bias_sum + grad
                stacks.append(shifted(grad, lane).astype(BF16))
            lefts.append(jnp.concatenate(stacks, axis=0))
            rights.append(cells)
    left = jnp.concatenate(lefts, axis=1)
    sums = [
        lax.dot_general(
            left,
            jnp.concatenate([cells[kd] for cells in rights], axis=1),
            (((1,), (1,)), ((), ())),
            preferred_element_type=F32,
        )
        for kd in range(3)
    ]

    first = (lane // PART) % 2 == 0
    blocks, last = [], []
    for kd in range(3):
        for kw in range(3):
            one = sums[kd][kw * cout : (kw + 1) * cout]
            two = sums[kd][(3 + kw) * cout : (4 + kw) * cout]
            back = pltpu.roll(two[:, width:], width - PART, 1)
            blocks.append(
                one[:, :width]
                + jnp.where(
                    first,
                    pltpu.roll(two[:, :width], width - PART, 1),
                    pltpu.roll(two[:, width:], PART, 1),
                )
            )
            last.append(one[:, width:] + back)
    last.append(jnp.broadcast_to(jnp.sum(bias_sum, axis=1, keepdims=True), (cout, width)))
    for k in range(0, len(last), 2):
        blocks.append(jnp.where(first, last[k], pltpu.roll(last[k + 1], PART, 1)))
    source = lax.broadcasted_iota(jnp.int32, (width, width), 0)
    target = (source // PART) % 2 * (width // 2) + source // (2 * PART) * PART + source % PART
    order = jnp.where(lax.broadcasted_iota(jnp.int32, (width, width), 1) == target, 1.0, 0.0).astype(BF16)
    placed = jnp.dot(jnp.concatenate(blocks, axis=0).astype(BF16), order, preferred_element_type=F32)
    count = len(blocks) // 2
    for k in range(2 * count):
        halves[k // count, k % count] = placed[k * cout : (k + 1) * cout].astype(BF16)
    face_ref[: rows + 2] = grads[1 - core]
    face_ref[rows + 2 :] = halves[1 - core]
    far_ref[...] = grads[core]
    kept_ref[...] = halves[core]


def backward_kernel(planes, rows, at_ref, w_ref, face, far, face_in, far_in, parts, stack):
    cout, width = far.shape[1:]
    cin = w_ref.shape[1]
    count = parts.shape[0]
    part = cin // count
    lane = lax.broadcasted_iota(jnp.int32, (cout, width), 1)
    step = 3 * cout
    core = at_ref[0]
    for q, source in enumerate((face_in, face, far, far_in)):
        p = jnp.where(core == 1, q, planes + 1 - q)
        for r in range(rows + 2):
            stack[p, r * step : (r + 1) * step, :] = shifted(source[r].astype(F32), lane).astype(BF16)
    w = jnp.transpose(w_ref[...].astype(F32)).astype(BF16)
    for d in range(planes):
        for h in range(0, rows, 2):
            cells = jnp.concatenate(
                [
                    jnp.concatenate(
                        [
                            stack[d + 2 - kd, (h + e + 2 - kh) * step : (h + e + 3 - kh) * step, :]
                            for kd in range(3)
                            for kh in range(3)
                        ],
                        axis=0,
                    )
                    for e in range(2)
                ],
                axis=1,
            )
            acc = jnp.dot(w, cells, preferred_element_type=F32)
            pair = (d * rows + h) // 2
            for f in range(count):
                piece = acc[f * part : (f + 1) * part]
                piece = jnp.concatenate([piece[:, :width], piece[:, width:]], axis=0).astype(BF16)
                parts[f, pair] = piece


def placing(cin):
    ones = np.zeros((2, 3, cin, 2, cin // PART, 2, PART), np.float32)
    for e in range(2):
        for kh in range(3):
            for i in range(cin):
                ones[e, kh, i, (kh + e) // 2, i // PART, (kh + e) % 2, i % PART] = 1
    return ones.reshape(2, 3 * cin, 4 * cin)


def weights_kernel(at_ref, mine, other, w_ref, b_ref):
    count, cout, width = mine.shape
    half = width // 2
    for k in range(2 * count):
        own = at_ref[0] == k // count
        block = jnp.where(own, mine[k % count].astype(F32), other[k % count].astype(F32))
        for e in range(2):
            piece = block[:, e * half : (e + 1) * half]
            at, kh = (k, e) if k < 9 else (2 * (k - 9) + e, 2)
            if at < 9:
                w_ref[at // 3 * 9 + kh * 3 + at % 3] = piece
    spare = block[:, half : half + cout]
    row = lax.broadcasted_iota(jnp.int32, (cout, cout), 0)
    lane = lax.broadcasted_iota(jnp.int32, (cout, cout), 1)
    b_ref[...] = jnp.sum(jnp.where(row == lane, spare, 0.0), axis=0, keepdims=True)


def call(body, name, *args, out, scratch=(), dtype=BF16, flops=0, moved=1 << 18, waves=0, scalars=0):
    smem, vmem = pl.BlockSpec(memory_space=pltpu.SMEM), pl.BlockSpec(memory_space=pltpu.VMEM)
    outs = tuple(jax.ShapeDtypeStruct(shape, dtype) for shape in out)
    results = pl.pallas_call(
        body,
        out_shape=outs,
        in_specs=[smem] * scalars + [vmem] * (len(args) - scalars),
        out_specs=(vmem,) * len(outs),
        scratch_shapes=[pltpu.VMEM(shape, kind) for shape, kind in scratch],
        compiler_params=pltpu.CompilerParams(vmem_limit_bytes=12 << 20),
        cost_estimate=pl.CostEstimate(flops=flops, bytes_accessed=moved, transcendentals=waves),
        name=name,
    )(*args)
    return results[0] if len(outs) == 1 else results


def per_device(activations, weights, bias, cotangent):
    cin_dev, planes, rows, width = activations.shape
    taps, cin, cout = weights.shape
    cells = planes * rows
    depth, height, filt = (lax.axis_size(axis) for axis in ("depth", "height", "filt"))
    swap = [(i, i ^ 1) for i in range(depth)]
    cross = [(i, i - 1 if i % 2 == 0 else i + 1) for i in range(1, depth - 1)]
    at = (lax.axis_index("depth") % 2).astype(jnp.int32).reshape(1)
    pairs, double = rows // 2, 2 * cin_dev

    work = 2 * cells * width * taps * cin * cout
    own, face = call(
        pack_kernel,
        "pack",
        at,
        activations.reshape(cin_dev, cells, width),
        out=[(planes, pairs, double, width), (pairs, double, width)],
        scratch=[((cin_dev * cells, width), F32)],
        scalars=1,
    )
    facing = lax.ppermute(face, "depth", swap)
    far = call(far_kernel, "far", at, own, out=[face.shape], flops=64 * work, scalars=1)
    beyond = lax.ppermute(far, "depth", cross)
    grid = call(
        grid_kernel,
        "grid",
        at,
        own,
        facing,
        beyond,
        out=[(filt, planes + 2, pairs, double, width)],
        scalars=1,
    )
    tiles = swapped(grid, "filt")

    cot = cotangent.transpose(1, 2, 0, 3).reshape(cells, cout, width)
    split = weights.reshape(3, 3, 3, cin, cout)
    w_forward = jnp.einsum(
        "akj,ejn->aekn",
        split.transpose(0, 2, 4, 1, 3).reshape(3, 3 * cout, 3 * cin),
        jnp.asarray(placing(cin), BF16),
        preferred_element_type=F32,
    )
    w_forward = w_forward.astype(BF16).reshape(3, 6 * cout, 4 * cin)
    w_back = weights.transpose(0, 2, 1).reshape(taps * cout, cin)
    first, last = call(
        functools.partial(rows_kernel, rows),
        "rows",
        tiles,
        cot,
        out=[((planes + 2) * filt + planes, cout, width)] * 2,
    )
    first, last, w_forward = lax.optimization_barrier((first, last, w_forward))
    before, after = neighbours(first, last, "height")

    count = (taps + 1) // 4
    out, face, far, kept_sums = call(
        functools.partial(forward_kernel, planes, rows),
        "forward",
        at,
        bias,
        w_forward,
        cot,
        tiles,
        before,
        after,
        out=[(k, cout, width) for k in (cells, rows + 2 + count, rows + 2, count)],
        scratch=[((planes, rows + 2, cout, width), BF16), ((2, count, cout, width), BF16)],
        flops=3 * work,
        waves=1 << 17,
        scalars=2,
    )
    output = out.reshape(planes, rows, cout, width).transpose(2, 0, 1, 3)

    size = kept_sums.shape
    face_in = lax.ppermute(face, "depth", swap)
    far_in = lax.ppermute(far, "depth", cross)
    groups = [list(range(height))[::-1]]
    sums = call(pair_kernel, "pair", kept_sums, face_in, out=[(height,) + size])
    sums = swapped(sums, "height", groups)
    parts = call(
        functools.partial(backward_kernel, planes, rows),
        "backward",
        at,
        w_back,
        face,
        far,
        face_in,
        far_in,
        out=[(filt, cells // 2, double, width)],
        scratch=[((planes + 2, (rows + 2) * 3 * cout, width), BF16)],
        flops=64 * work,
        scalars=1,
    )
    groups = [[(i + depth // 2) % depth for i in range(k, depth, 2)] for k in range(2)]
    sums = swapped(call(sum_kernel, "sums", sums, out=[(depth // 2,) + size]), "depth", groups)
    sums, parts = lax.optimization_barrier((sums, parts))
    parts = swapped(parts, "filt")
    summed = call(
        unpack_kernel,
        "unpack",
        parts,
        out=[(cin_dev, cells, width)],
        scratch=[((cin_dev * cells, width), F32)],
    ).reshape(activations.shape)

    mine = call(sum_kernel, "sums", sums, out=[(1,) + size])[0]
    other = lax.ppermute(mine, "depth", swap)
    weight_grad, bias_grad = call(
        weights_kernel,
        "weights",
        at,
        mine,
        other,
        out=[(taps, cout, cin), (1, cout)],
        dtype=F32,
        scalars=1,
    )
    return (output, summed, weight_grad.transpose(0, 2, 1), bias_grad.reshape(cout))


def solution(mesh):
    placed = (
        P("filt", "depth", "height", None),
        P(None, None, "filt"),
        P("filt"),
        P("filt", "depth", "height", None),
    )
    return jax.shard_map(
        per_device,
        mesh=mesh,
        in_specs=placed,
        out_specs=(
            P("filt", "depth", "height", None),
            P("filt", "depth", "height", None),
            P(None, None, "filt"),
            P("filt"),
        ),
        check_vma=False,
    )
```

```python
import functools

import jax
import jax.numpy as jnp
import numpy as np
from jax import lax
from jax.experimental import pallas as pl
from jax.experimental.pallas import tpu as pltpu
from jax.sharding import PartitionSpec as P

BF16 = jnp.bfloat16
F32 = jnp.float32
PART = 8


def swapped(blocks, axis, groups=None):
    return lax.all_to_all(blocks, axis, 0, 0, tiled=True, axis_index_groups=groups)


def neighbours(first, last, axis):
    ends = lax.axis_size(axis) - 1
    before = lax.ppermute(last, axis, [(i, i + 1) for i in range(ends)])
    after = lax.ppermute(first, axis, [(i + 1, i) for i in range(ends)])
    return before, after


def shifted(value, lane):
    width = value.shape[-1]
    ahead = jnp.where(lane == width - 1, 0.0, pltpu.roll(value, width - 1, 1))
    behind = jnp.where(lane == 0, 0.0, pltpu.roll(value, 1, 1))
    return jnp.concatenate([ahead, value, behind], axis=0)


def pack_kernel(at_ref, cells, own, face_ref, wide):
    planes, pairs = own.shape[:2]
    count, lines = cells.shape[:2]
    for c in range(count):
        wide[c * lines : (c + 1) * lines] = cells[c].astype(F32)
    for d in range(planes):
        for t in range(pairs):
            row = 2 * (d * pairs + t)
            own[d, t] = jnp.concatenate(
                [wide[pl.ds(row + e, count, stride=lines), :] for e in range(2)], axis=0
            ).astype(BF16)
    face_ref[...] = own[jnp.where(at_ref[0] == 0, planes - 1, 0)]


def far_kernel(at_ref, own, far_ref):
    far_ref[...] = own[jnp.where(at_ref[0] == 0, 0, own.shape[0] - 1)]


def grid_kernel(at_ref, own, facing, beyond, out_ref):
    planes = own.shape[0]
    before = jnp.where(at_ref[0] == 0, 0, planes + 1)
    for k in range(out_ref.shape[0]):
        for d in range(planes):
            out_ref[k, d + 1] = own[d]
        out_ref[k, before] = beyond[...]
        out_ref[k, planes + 1 - before] = facing[...]


def rows_kernel(rows, tiles, cot, first_ref, last_ref):
    sources, count = tiles.shape[:2]
    for ref, t, row in ((first_ref, 0, 0), (last_ref, rows // 2 - 1, rows - 1)):
        for p in range(count):
            ref[p * sources : (p + 1) * sources] = tiles[:, p, t]
        for d in range(count - 2):
            ref[count * sources + d] = cot[d * rows + row]


def sum_kernel(blocks, out_ref):
    for r in range(blocks.shape[1]):
        total = blocks[0, r].astype(F32)
        for k in range(1, blocks.shape[0]):
            total = total + blocks[k, r].astype(F32)
        for k in range(out_ref.shape[0]):
            out_ref[k, r] = total.astype(BF16)


def pair_kernel(kept, other, out_ref):
    first = other.shape[0] - kept.shape[0]
    for r in range(kept.shape[0]):
        total = (kept[r].astype(F32) + other[first + r].astype(F32)).astype(BF16)
        for k in range(out_ref.shape[0]):
            out_ref[k, r] = total


def unpack_kernel(parts, out_ref, wide):
    pairs, size = parts.shape[1:3]
    count, lines = out_ref.shape[:2]
    for t in range(pairs):
        total = parts[0, t].astype(F32)
        for k in range(1, parts.shape[0]):
            total = total + parts[k, t].astype(F32)
        wide[t * size : (t + 1) * size] = total
    for c in range(count):
        out_ref[c] = wide[pl.ds(c, lines, stride=count), :].astype(BF16)


def forward_kernel(planes, rows, at_ref, bias_ref, w_ref, cot, tiles, before, after, *refs):
    out_ref, face_ref, far_ref, kept_ref, grads, halves = refs
    cout, width = cot.shape[1:]
    sources = tiles.shape[0]
    edge = sources * (planes + 2)
    core = at_ref[0]

    def tile(s, p, t):
        if t == 0:
            return before[p * sources + s]
        if t == rows // 2 + 1:
            return after[p * sources + s]
        return tiles[s, p, t - 1]

    lane = lax.broadcasted_iota(jnp.int32, (cout, width), 1)
    channel = lax.broadcasted_iota(jnp.int32, (cout, width), 0)
    bias = jnp.zeros((cout, width), F32)
    for o in range(cout):
        bias = jnp.where(channel == o, bias_ref[o], bias)
    lefts, rights = [], []
    bias_sum = jnp.zeros((cout, width), F32)
    for d in range(planes):
        for pair in range(rows // 2 + 1):
            cells = [
                jnp.concatenate(
                    [tile(s, d + kd, pair + t) for t in range(2) for s in range(sources)], axis=0
                )
                for kd in range(3)
            ]
            acc = jnp.dot(w_ref[0], cells[0], preferred_element_type=F32)
            for kd in range(1, 3):
                acc = acc + jnp.dot(w_ref[kd], cells[kd], preferred_element_type=F32)
            stacks = []
            for e in range(2):
                z = acc[3 * e * cout : 3 * (e + 1) * cout]
                pre = (
                    z[cout : 2 * cout]
                    + jnp.where(lane == 0, 0.0, pltpu.roll(z[:cout], 1, 1))
                    + jnp.where(lane == width - 1, 0.0, pltpu.roll(z[2 * cout :], width - 1, 1))
                    + bias
                )
                small = jnp.exp(-jnp.abs(pre))
                sigmoid = jnp.where(pre >= 0, 1.0, small) / (1.0 + small)
                row = 2 * pair + e
                if row == 0:
                    cotangent = before[edge + d]
                elif row == rows + 1:
                    cotangent = after[edge + d]
                else:
                    cotangent = cot[d * rows + row - 1]
                grad = (cotangent.astype(F32) * (0.2 + 0.8 * sigmoid)).astype(BF16)
                grads[d, row] = grad
                if row == 0 or row == rows + 1:
                    stacks.append(jnp.zeros((3 * cout, width), BF16))
                    continue
                softplus = jnp.maximum(pre, 0.0) + jnp.log1p(small)
                out_ref[d * rows + row - 1] = (0.2 * pre + 0.8 * softplus).astype(BF16)
                grad = grad.astype(F32)
                bias_sum = bias_sum + grad
                stacks.append(shifted(grad, lane).astype(BF16))
            lefts.append(jnp.concatenate(stacks, axis=0))
            rights.append(cells)
    left = jnp.concatenate(lefts, axis=1)
    sums = [
        lax.dot_general(
            left,
            jnp.concatenate([cells[kd] for cells in rights], axis=1),
            (((1,), (1,)), ((), ())),
            preferred_element_type=F32,
        )
        for kd in range(3)
    ]

    first = (lane // PART) % 2 == 0
    blocks, last = [], []
    for kd in range(3):
        for kw in range(3):
            one = sums[kd][kw * cout : (kw + 1) * cout]
            two = sums[kd][(3 + kw) * cout : (4 + kw) * cout]
            back = pltpu.roll(two[:, width:], width - PART, 1)
            blocks.append(
                one[:, :width]
                + jnp.where(
                    first,
                    pltpu.roll(two[:, :width], width - PART, 1),
                    pltpu.roll(two[:, width:], PART, 1),
                )
            )
            last.append(one[:, width:] + back)
    last.append(jnp.broadcast_to(jnp.sum(bias_sum, axis=1, keepdims=True), (cout, width)))
    for k in range(0, len(last), 2):
        blocks.append(jnp.where(first, last[k], pltpu.roll(last[k + 1], PART, 1)))
    source = lax.broadcasted_iota(jnp.int32, (width, width), 0)
    target = (source // PART) % 2 * (width // 2) + source // (2 * PART) * PART + source % PART
    order = jnp.where(lax.broadcasted_iota(jnp.int32, (width, width), 1) == target, 1.0, 0.0).astype(BF16)
    placed = jnp.dot(jnp.concatenate(blocks, axis=0).astype(BF16), order, preferred_element_type=F32)
    count = len(blocks) // 2
    for k in range(2 * count):
        halves[k // count, k % count] = placed[k * cout : (k + 1) * cout].astype(BF16)
    face_ref[: rows + 2] = grads[1 - core]
    face_ref[rows + 2 :] = halves[1 - core]
    far_ref[...] = grads[core]
    kept_ref[...] = halves[core]


def backward_kernel(planes, rows, at_ref, w_ref, face, far, face_in, far_in, parts, stack):
    cout, width = far.shape[1:]
    cin = w_ref.shape[1]
    count = parts.shape[0]
    part = cin // count
    lane = lax.broadcasted_iota(jnp.int32, (cout, width), 1)
    step = 3 * cout
    core = at_ref[0]
    for q, source in enumerate((face_in, face, far, far_in)):
        p = jnp.where(core == 1, q, planes + 1 - q)
        for r in range(rows + 2):
            stack[p, r * step : (r + 1) * step, :] = shifted(source[r].astype(F32), lane).astype(BF16)
    w = jnp.transpose(w_ref[...].astype(F32)).astype(BF16)
    for d in range(planes):
        for h in range(0, rows, 2):
            cells = jnp.concatenate(
                [
                    jnp.concatenate(
                        [
                            stack[d + 2 - kd, (h + e + 2 - kh) * step : (h + e + 3 - kh) * step, :]
                            for kd in range(3)
                            for kh in range(3)
                        ],
                        axis=0,
                    )
                    for e in range(2)
                ],
                axis=1,
            )
            acc = jnp.dot(w, cells, preferred_element_type=F32)
            pair = (d * rows + h) // 2
            for f in range(count):
                piece = acc[f * part : (f + 1) * part]
                piece = jnp.concatenate([piece[:, :width], piece[:, width:]], axis=0).astype(BF16)
                parts[count - 1 - f, pair] = piece


def placing(cin):
    ones = np.zeros((2, 3, cin, 2, cin // PART, 2, PART), np.float32)
    for e in range(2):
        for kh in range(3):
            for i in range(cin):
                ones[e, kh, i, (kh + e) // 2, i // PART, (kh + e) % 2, i % PART] = 1
    return ones.reshape(2, 3 * cin, 4 * cin)


def weights_kernel(at_ref, mine, other, w_ref, b_ref):
    count, cout, width = mine.shape
    half = width // 2
    for k in range(2 * count):
        own = at_ref[0] == k // count
        block = jnp.where(own, mine[k % count].astype(F32), other[k % count].astype(F32))
        for e in range(2):
            piece = block[:, e * half : (e + 1) * half]
            at, kh = (k, e) if k < 9 else (2 * (k - 9) + e, 2)
            if at < 9:
                w_ref[at // 3 * 9 + kh * 3 + at % 3] = piece
    spare = block[:, half : half + cout]
    row = lax.broadcasted_iota(jnp.int32, (cout, cout), 0)
    lane = lax.broadcasted_iota(jnp.int32, (cout, cout), 1)
    b_ref[...] = jnp.sum(jnp.where(row == lane, spare, 0.0), axis=0, keepdims=True)


def call(body, name, *args, out, scratch=(), dtype=BF16, flops=0, moved=1 << 18, waves=0, scalars=0):
    smem, vmem = pl.BlockSpec(memory_space=pltpu.SMEM), pl.BlockSpec(memory_space=pltpu.VMEM)
    outs = tuple(jax.ShapeDtypeStruct(shape, dtype) for shape in out)
    results = pl.pallas_call(
        body,
        out_shape=outs,
        in_specs=[smem] * scalars + [vmem] * (len(args) - scalars),
        out_specs=(vmem,) * len(outs),
        scratch_shapes=[pltpu.VMEM(shape, kind) for shape, kind in scratch],
        compiler_params=pltpu.CompilerParams(vmem_limit_bytes=12 << 20),
        cost_estimate=pl.CostEstimate(flops=flops, bytes_accessed=moved, transcendentals=waves),
        name=name,
    )(*args)
    return results[0] if len(outs) == 1 else results


def per_device(activations, weights, bias, cotangent):
    cin_dev, planes, rows, width = activations.shape
    taps, cin, cout = weights.shape
    cells = planes * rows
    depth, height, filt = (lax.axis_size(axis) for axis in ("depth", "height", "filt"))
    swap = [(i, i ^ 1) for i in range(depth)]
    cross = [(i, i - 1 if i % 2 == 0 else i + 1) for i in range(1, depth - 1)]
    at = (lax.axis_index("depth") % 2).astype(jnp.int32).reshape(1)
    pairs, double = rows // 2, 2 * cin_dev

    work = 2 * cells * width * taps * cin * cout
    own, face = call(
        pack_kernel,
        "pack",
        at,
        activations.reshape(cin_dev, cells, width),
        out=[(planes, pairs, double, width), (pairs, double, width)],
        scratch=[((cin_dev * cells, width), F32)],
        scalars=1,
    )
    facing = lax.ppermute(face, "depth", swap)
    far = call(far_kernel, "far", at, own, out=[face.shape], flops=64 * work, scalars=1)
    beyond = lax.ppermute(far, "depth", cross)
    grid = call(
        grid_kernel,
        "grid",
        at,
        own,
        facing,
        beyond,
        out=[(filt, planes + 2, pairs, double, width)],
        scalars=1,
    )
    tiles = swapped(grid, "filt")

    cot = cotangent.transpose(1, 2, 0, 3).reshape(cells, cout, width)
    split = weights.reshape(3, 3, 3, cin, cout)
    w_forward = jnp.einsum(
        "akj,ejn->aekn",
        split.transpose(0, 2, 4, 1, 3).reshape(3, 3 * cout, 3 * cin),
        jnp.asarray(placing(cin), BF16),
        preferred_element_type=F32,
    )
    w_forward = w_forward.astype(BF16).reshape(3, 6 * cout, 4 * cin)
    w_back = weights.transpose(0, 2, 1).reshape(taps * cout, cin)
    first, last = call(
        functools.partial(rows_kernel, rows),
        "rows",
        tiles,
        cot,
        out=[((planes + 2) * filt + planes, cout, width)] * 2,
    )
    first, last, w_forward = lax.optimization_barrier((first, last, w_forward))
    before, after = neighbours(first, last, "height")

    count = (taps + 1) // 4
    out, face, far, kept_sums = call(
        functools.partial(forward_kernel, planes, rows),
        "forward",
        at,
        bias,
        w_forward,
        cot,
        tiles,
        before,
        after,
        out=[(k, cout, width) for k in (cells, rows + 2 + count, rows + 2, count)],
        scratch=[((planes, rows + 2, cout, width), BF16), ((2, count, cout, width), BF16)],
        flops=3 * work,
        waves=1 << 17,
        scalars=2,
    )
    output = out.reshape(planes, rows, cout, width).transpose(2, 0, 1, 3)

    size = kept_sums.shape
    face_in = lax.ppermute(face, "depth", swap)
    far_in = lax.ppermute(far, "depth", cross)
    groups = [list(range(2, height))[::-1] + [0, 1]]
    sums = call(pair_kernel, "pair", kept_sums, face_in, out=[(height,) + size])
    sums = swapped(sums, "height", groups)
    parts = call(
        functools.partial(backward_kernel, planes, rows),
        "backward",
        at,
        w_back,
        face,
        far,
        face_in,
        far_in,
        out=[(filt, cells // 2, double, width)],
        scratch=[((planes + 2, (rows + 2) * 3 * cout, width), BF16)],
        flops=64 * work,
        scalars=1,
    )
    groups = [[(i + depth // 2) % depth for i in range(k, depth, 2)] for k in range(2)]
    sums = swapped(call(sum_kernel, "sums", sums, out=[(depth // 2,) + size]), "depth", groups)
    sums, parts = lax.optimization_barrier((sums, parts))
    parts = swapped(parts, "filt", [list(range(filt))[::-1]])
    summed = call(
        unpack_kernel,
        "unpack",
        parts,
        out=[(cin_dev, cells, width)],
        scratch=[((cin_dev * cells, width), F32)],
    ).reshape(activations.shape)

    mine = call(sum_kernel, "sums", sums, out=[(1,) + size])[0]
    other = lax.ppermute(mine, "depth", swap)
    weight_grad, bias_grad = call(
        weights_kernel,
        "weights",
        at,
        mine,
        other,
        out=[(taps, cout, cin), (1, cout)],
        dtype=F32,
        scalars=1,
    )
    return (output, summed, weight_grad.transpose(0, 2, 1), bias_grad.reshape(cout))


def solution(mesh):
    placed = (
        P("filt", "depth", "height", None),
        P(None, None, "filt"),
        P("filt"),
        P("filt", "depth", "height", None),
    )
    return jax.shard_map(
        per_device,
        mesh=mesh,
        in_specs=placed,
        out_specs=(
            P("filt", "depth", "height", None),
            P("filt", "depth", "height", None),
            P(None, None, "filt"),
            P("filt"),
        ),
        check_vma=False,
    )
```

```python
import functools

import jax
import jax.numpy as jnp
import numpy as np
from jax import lax
from jax.experimental import pallas as pl
from jax.experimental.pallas import tpu as pltpu
from jax.sharding import PartitionSpec as P

BF16 = jnp.bfloat16
F32 = jnp.float32
PART = 8


def swapped(blocks, axis, groups=None):
    return lax.all_to_all(blocks, axis, 0, 0, tiled=True, axis_index_groups=groups)


def neighbours(first, last, axis):
    ends = lax.axis_size(axis) - 1
    before = lax.ppermute(last, axis, [(i, i + 1) for i in range(ends)])
    after = lax.ppermute(first, axis, [(i + 1, i) for i in range(ends)])
    return before, after


def shifted(value, lane):
    width = value.shape[-1]
    ahead = jnp.where(lane == width - 1, 0.0, pltpu.roll(value, width - 1, 1))
    behind = jnp.where(lane == 0, 0.0, pltpu.roll(value, 1, 1))
    return jnp.concatenate([ahead, value, behind], axis=0)


def pack_kernel(at_ref, cells, own, face_ref, wide):
    planes, pairs = own.shape[:2]
    count, lines = cells.shape[:2]
    for c in range(count):
        wide[c * lines : (c + 1) * lines] = cells[c].astype(F32)
    for d in range(planes):
        for t in range(pairs):
            row = 2 * (d * pairs + t)
            own[d, t] = jnp.concatenate(
                [wide[pl.ds(row + e, count, stride=lines), :] for e in range(2)], axis=0
            ).astype(BF16)
    face_ref[...] = own[jnp.where(at_ref[0] == 0, planes - 1, 0)]


def far_kernel(at_ref, own, far_ref):
    far_ref[...] = own[jnp.where(at_ref[0] == 0, 0, own.shape[0] - 1)]


def grid_kernel(at_ref, own, facing, beyond, out_ref):
    planes = own.shape[0]
    before = jnp.where(at_ref[0] == 0, 0, planes + 1)
    for k in range(out_ref.shape[0]):
        for d in range(planes):
            out_ref[k, d + 1] = own[d]
        out_ref[k, before] = beyond[...]
        out_ref[k, planes + 1 - before] = facing[...]


def rows_kernel(rows, tiles, cot, first_ref, last_ref):
    sources, count = tiles.shape[:2]
    for ref, t, row in ((first_ref, 0, 0), (last_ref, rows // 2 - 1, rows - 1)):
        for p in range(count):
            ref[p * sources : (p + 1) * sources] = tiles[:, p, t]
        for d in range(count - 2):
            ref[count * sources + d] = cot[d * rows + row]


def sum_kernel(blocks, out_ref):
    for r in range(blocks.shape[1]):
        total = blocks[0, r].astype(F32)
        for k in range(1, blocks.shape[0]):
            total = total + blocks[k, r].astype(F32)
        for k in range(out_ref.shape[0]):
            out_ref[k, r] = total.astype(BF16)


def pair_kernel(kept, other, out_ref):
    first = other.shape[0] - kept.shape[0]
    for r in range(kept.shape[0]):
        total = (kept[r].astype(F32) + other[first + r].astype(F32)).astype(BF16)
        for k in range(out_ref.shape[0]):
            out_ref[k, r] = total


def unpack_kernel(parts, out_ref, wide):
    pairs, size = parts.shape[1:3]
    count, lines = out_ref.shape[:2]
    for t in range(pairs):
        total = parts[0, t].astype(F32)
        for k in range(1, parts.shape[0]):
            total = total + parts[k, t].astype(F32)
        wide[t * size : (t + 1) * size] = total
    for c in range(count):
        out_ref[c] = wide[pl.ds(c, lines, stride=count), :].astype(BF16)


def forward_kernel(planes, rows, at_ref, bias_ref, w_ref, cot, tiles, before, after, *refs):
    out_ref, face_ref, far_ref, kept_ref, grads, halves = refs
    cout, width = cot.shape[1:]
    sources = tiles.shape[0]
    edge = sources * (planes + 2)
    core = at_ref[0]

    def tile(s, p, t):
        if t == 0:
            return before[p * sources + s]
        if t == rows // 2 + 1:
            return after[p * sources + s]
        return tiles[s, p, t - 1]

    lane = lax.broadcasted_iota(jnp.int32, (cout, width), 1)
    channel = lax.broadcasted_iota(jnp.int32, (cout, width), 0)
    bias = jnp.zeros((cout, width), F32)
    for o in range(cout):
        bias = jnp.where(channel == o, bias_ref[o], bias)
    lefts, rights = [], []
    bias_sum = jnp.zeros((cout, width), F32)
    for d in range(planes):
        for pair in range(rows // 2 + 1):
            cells = [
                jnp.concatenate(
                    [tile(s, d + kd, pair + t) for t in range(2) for s in range(sources)], axis=0
                )
                for kd in range(3)
            ]
            acc = jnp.dot(w_ref[0], cells[0], preferred_element_type=F32)
            for kd in range(1, 3):
                acc = acc + jnp.dot(w_ref[kd], cells[kd], preferred_element_type=F32)
            stacks = []
            for e in range(2):
                z = acc[3 * e * cout : 3 * (e + 1) * cout]
                pre = (
                    z[cout : 2 * cout]
                    + jnp.where(lane == 0, 0.0, pltpu.roll(z[:cout], 1, 1))
                    + jnp.where(lane == width - 1, 0.0, pltpu.roll(z[2 * cout :], width - 1, 1))
                    + bias
                )
                small = jnp.exp(-jnp.abs(pre))
                sigmoid = jnp.where(pre >= 0, 1.0, small) / (1.0 + small)
                row = 2 * pair + e
                if row == 0:
                    cotangent = before[edge + d]
                elif row == rows + 1:
                    cotangent = after[edge + d]
                else:
                    cotangent = cot[d * rows + row - 1]
                grad = (cotangent.astype(F32) * (0.2 + 0.8 * sigmoid)).astype(BF16)
                grads[d, row] = grad
                if row == 0 or row == rows + 1:
                    stacks.append(jnp.zeros((3 * cout, width), BF16))
                    continue
                softplus = jnp.maximum(pre, 0.0) + jnp.log1p(small)
                out_ref[d * rows + row - 1] = (0.2 * pre + 0.8 * softplus).astype(BF16)
                grad = grad.astype(F32)
                bias_sum = bias_sum + grad
                stacks.append(shifted(grad, lane).astype(BF16))
            lefts.append(jnp.concatenate(stacks, axis=0))
            rights.append(cells)
    left = jnp.concatenate(lefts, axis=1)
    sums = [
        lax.dot_general(
            left,
            jnp.concatenate([cells[kd] for cells in rights], axis=1),
            (((1,), (1,)), ((), ())),
            preferred_element_type=F32,
        )
        for kd in range(3)
    ]

    first = (lane // PART) % 2 == 0
    blocks, last = [], []
    for kd in range(3):
        for kw in range(3):
            one = sums[kd][kw * cout : (kw + 1) * cout]
            two = sums[kd][(3 + kw) * cout : (4 + kw) * cout]
            back = pltpu.roll(two[:, width:], width - PART, 1)
            blocks.append(
                one[:, :width]
                + jnp.where(
                    first,
                    pltpu.roll(two[:, :width], width - PART, 1),
                    pltpu.roll(two[:, width:], PART, 1),
                )
            )
            last.append(one[:, width:] + back)
    last.append(jnp.broadcast_to(jnp.sum(bias_sum, axis=1, keepdims=True), (cout, width)))
    for k in range(0, len(last), 2):
        blocks.append(jnp.where(first, last[k], pltpu.roll(last[k + 1], PART, 1)))
    source = lax.broadcasted_iota(jnp.int32, (width, width), 0)
    target = (source // PART) % 2 * (width // 2) + source // (2 * PART) * PART + source % PART
    order = jnp.where(lax.broadcasted_iota(jnp.int32, (width, width), 1) == target, 1.0, 0.0).astype(BF16)
    placed = jnp.dot(jnp.concatenate(blocks, axis=0).astype(BF16), order, preferred_element_type=F32)
    count = len(blocks) // 2
    for k in range(2 * count):
        halves[k // count, k % count] = placed[k * cout : (k + 1) * cout].astype(BF16)
    face_ref[: rows + 2] = grads[1 - core]
    face_ref[rows + 2 :] = halves[1 - core]
    far_ref[...] = grads[core]
    kept_ref[...] = halves[core]


def backward_kernel(planes, rows, at_ref, w_ref, face, far, face_in, far_in, parts, stack):
    cout, width = far.shape[1:]
    cin = w_ref.shape[1]
    count = parts.shape[0]
    part = cin // count
    lane = lax.broadcasted_iota(jnp.int32, (cout, width), 1)
    step = 3 * cout
    core = at_ref[0]
    for q, source in enumerate((face_in, face, far, far_in)):
        p = jnp.where(core == 1, q, planes + 1 - q)
        for r in range(rows + 2):
            stack[p, r * step : (r + 1) * step, :] = shifted(source[r].astype(F32), lane).astype(BF16)
    w = jnp.transpose(w_ref[...].astype(F32)).astype(BF16)
    for d in range(planes):
        for h in range(0, rows, 2):
            cells = jnp.concatenate(
                [
                    jnp.concatenate(
                        [
                            stack[d + 2 - kd, (h + e + 2 - kh) * step : (h + e + 3 - kh) * step, :]
                            for kd in range(3)
                            for kh in range(3)
                        ],
                        axis=0,
                    )
                    for e in range(2)
                ],
                axis=1,
            )
            acc = jnp.dot(w, cells, preferred_element_type=F32)
            pair = (d * rows + h) // 2
            for f in range(count):
                piece = acc[f * part : (f + 1) * part]
                piece = jnp.concatenate([piece[:, :width], piece[:, width:]], axis=0).astype(BF16)
                parts[f, pair] = piece


def placing(cin):
    ones = np.zeros((2, 3, cin, 2, cin // PART, 2, PART), np.float32)
    for e in range(2):
        for kh in range(3):
            for i in range(cin):
                ones[e, kh, i, (kh + e) // 2, i // PART, (kh + e) % 2, i % PART] = 1
    return ones.reshape(2, 3 * cin, 4 * cin)


def weights_kernel(at_ref, mine, other, w_ref, b_ref):
    count, cout, width = mine.shape
    half = width // 2
    for k in range(2 * count):
        own = at_ref[0] == k // count
        block = jnp.where(own, mine[k % count].astype(F32), other[k % count].astype(F32))
        for e in range(2):
            piece = block[:, e * half : (e + 1) * half]
            at, kh = (k, e) if k < 9 else (2 * (k - 9) + e, 2)
            if at < 9:
                w_ref[at // 3 * 9 + kh * 3 + at % 3] = piece
    spare = block[:, half : half + cout]
    row = lax.broadcasted_iota(jnp.int32, (cout, cout), 0)
    lane = lax.broadcasted_iota(jnp.int32, (cout, cout), 1)
    b_ref[...] = jnp.sum(jnp.where(row == lane, spare, 0.0), axis=0, keepdims=True)


def call(body, name, *args, out, scratch=(), dtype=BF16, flops=0, moved=1 << 18, waves=0, scalars=0):
    smem, vmem = pl.BlockSpec(memory_space=pltpu.SMEM), pl.BlockSpec(memory_space=pltpu.VMEM)
    outs = tuple(jax.ShapeDtypeStruct(shape, dtype) for shape in out)
    results = pl.pallas_call(
        body,
        out_shape=outs,
        in_specs=[smem] * scalars + [vmem] * (len(args) - scalars),
        out_specs=(vmem,) * len(outs),
        scratch_shapes=[pltpu.VMEM(shape, kind) for shape, kind in scratch],
        compiler_params=pltpu.CompilerParams(vmem_limit_bytes=12 << 20),
        cost_estimate=pl.CostEstimate(flops=flops, bytes_accessed=moved, transcendentals=waves),
        name=name,
    )(*args)
    return results[0] if len(outs) == 1 else results


def per_device(activations, weights, bias, cotangent):
    cin_dev, planes, rows, width = activations.shape
    taps, cin, cout = weights.shape
    cells = planes * rows
    depth, height, filt = (lax.axis_size(axis) for axis in ("depth", "height", "filt"))
    swap = [(i, i ^ 1) for i in range(depth)]
    cross = [(i, i - 1 if i % 2 == 0 else i + 1) for i in range(1, depth - 1)]
    at = (lax.axis_index("depth") % 2).astype(jnp.int32).reshape(1)
    pairs, double = rows // 2, 2 * cin_dev

    work = 2 * cells * width * taps * cin * cout
    own, face = call(
        pack_kernel,
        "pack",
        at,
        activations.reshape(cin_dev, cells, width),
        out=[(planes, pairs, double, width), (pairs, double, width)],
        scratch=[((cin_dev * cells + cells, width), F32)],
        scalars=1,
    )
    facing = lax.ppermute(face, "depth", swap)
    far = call(far_kernel, "far", at, own, out=[face.shape], flops=64 * work, scalars=1)
    beyond = lax.ppermute(far, "depth", cross)
    grid = call(
        grid_kernel,
        "grid",
        at,
        own,
        facing,
        beyond,
        out=[(filt, planes + 2, pairs, double, width)],
        scalars=1,
    )
    tiles = swapped(grid, "filt")

    cot = cotangent.transpose(1, 2, 0, 3).reshape(cells, cout, width)
    split = weights.reshape(3, 3, 3, cin, cout)
    w_forward = jnp.einsum(
        "akj,ejn->aekn",
        split.transpose(0, 2, 4, 1, 3).reshape(3, 3 * cout, 3 * cin),
        jnp.asarray(placing(cin), BF16),
        preferred_element_type=F32,
    )
    w_forward = w_forward.astype(BF16).reshape(3, 6 * cout, 4 * cin)
    w_back = weights.transpose(0, 2, 1).reshape(taps * cout, cin)
    first, last = call(
        functools.partial(rows_kernel, rows),
        "rows",
        tiles,
        cot,
        out=[((planes + 2) * filt + planes, cout, width)] * 2,
    )
    first, last, w_forward = lax.optimization_barrier((first, last, w_forward))
    before, after = neighbours(first, last, "height")

    count = (taps + 1) // 4
    out, face, far, kept_sums = call(
        functools.partial(forward_kernel, planes, rows),
        "forward",
        at,
        bias,
        w_forward,
        cot,
        tiles,
        before,
        after,
        out=[(k, cout, width) for k in (cells, rows + 2 + count, rows + 2, count)],
        scratch=[((planes, rows + 2, cout, width), BF16), ((2, count, cout, width), BF16)],
        flops=3 * work,
        waves=1 << 17,
        scalars=2,
    )
    output = out.reshape(planes, rows, cout, width).transpose(2, 0, 1, 3)

    size = kept_sums.shape
    face_in = lax.ppermute(face, "depth", swap)
    far_in = lax.ppermute(far, "depth", cross)
    groups = [[(i + height - 2) % height for i in range(height)]]
    sums = call(pair_kernel, "pair", kept_sums, face_in, out=[(height,) + size])
    sums = swapped(sums, "height", groups)
    parts = call(
        functools.partial(backward_kernel, planes, rows),
        "backward",
        at,
        w_back,
        face,
        far,
        face_in,
        far_in,
        out=[(filt, cells // 2, double, width)],
        scratch=[((planes + 2, (rows + 2) * 3 * cout, width), BF16)],
        flops=64 * work,
        scalars=1,
    )
    groups = [[(i + depth // 2) % depth for i in range(k, depth, 2)] for k in range(2)]
    sums = swapped(call(sum_kernel, "sums", sums, out=[(depth // 2,) + size]), "depth", groups)
    sums, parts = lax.optimization_barrier((sums, parts))
    parts = swapped(parts, "filt")
    summed = call(
        unpack_kernel,
        "unpack",
        parts,
        out=[(cin_dev, cells, width)],
        scratch=[((cin_dev * cells + cin_dev, width), F32)],
    ).reshape(activations.shape)

    mine = call(sum_kernel, "sums", sums, out=[(1,) + size])[0]
    other = lax.ppermute(mine, "depth", swap)
    weight_grad, bias_grad = call(
        weights_kernel,
        "weights",
        at,
        mine,
        other,
        out=[(taps, cout, cin), (1, cout)],
        dtype=F32,
        scalars=1,
    )
    return (output, summed, weight_grad.transpose(0, 2, 1), bias_grad.reshape(cout))


def solution(mesh):
    placed = (
        P("filt", "depth", "height", None),
        P(None, None, "filt"),
        P("filt"),
        P("filt", "depth", "height", None),
    )
    return jax.shard_map(
        per_device,
        mesh=mesh,
        in_specs=placed,
        out_specs=(
            P("filt", "depth", "height", None),
            P("filt", "depth", "height", None),
            P(None, None, "filt"),
            P("filt"),
        ),
        check_vma=False,
    )
```

```python
import functools

import jax
import jax.numpy as jnp
import numpy as np
from jax import lax
from jax.experimental import pallas as pl
from jax.experimental.pallas import tpu as pltpu
from jax.sharding import PartitionSpec as P

BF16 = jnp.bfloat16
F32 = jnp.float32
PART = 8


def swapped(blocks, axis, groups=None):
    return lax.all_to_all(blocks, axis, 0, 0, tiled=True, axis_index_groups=groups)


def neighbours(first, last, axis):
    ends = lax.axis_size(axis) - 1
    after = lax.ppermute(first, axis, [(i + 1, i) for i in range(ends)])
    before = lax.ppermute(last, axis, [(i, i + 1) for i in range(ends)])
    return before, after


def shifted(value, lane):
    width = value.shape[-1]
    ahead = jnp.where(lane == width - 1, 0.0, pltpu.roll(value, width - 1, 1))
    behind = jnp.where(lane == 0, 0.0, pltpu.roll(value, 1, 1))
    return jnp.concatenate([ahead, value, behind], axis=0)


def pack_kernel(at_ref, cells, own, face_ref, wide):
    planes, pairs = own.shape[:2]
    count, lines = cells.shape[:2]
    for c in range(count):
        wide[c * lines : (c + 1) * lines] = cells[c].astype(F32)
    for d in range(planes):
        for t in range(pairs):
            row = 2 * (d * pairs + t)
            own[d, t] = jnp.concatenate(
                [wide[pl.ds(row + e, count, stride=lines), :] for e in range(2)], axis=0
            ).astype(BF16)
    face_ref[...] = own[jnp.where(at_ref[0] == 0, planes - 1, 0)]


def far_kernel(at_ref, own, far_ref):
    far_ref[...] = own[jnp.where(at_ref[0] == 0, 0, own.shape[0] - 1)]


def grid_kernel(at_ref, own, facing, beyond, out_ref):
    planes = own.shape[0]
    before = jnp.where(at_ref[0] == 0, 0, planes + 1)
    for k in range(out_ref.shape[0]):
        for d in range(planes):
            out_ref[k, d + 1] = own[d]
        out_ref[k, before] = beyond[...]
        out_ref[k, planes + 1 - before] = facing[...]


def rows_kernel(rows, tiles, cot, first_ref, last_ref):
    sources, count = tiles.shape[:2]
    for ref, t, row in ((first_ref, 0, 0), (last_ref, rows // 2 - 1, rows - 1)):
        for p in range(count):
            ref[p * sources : (p + 1) * sources] = tiles[:, p, t]
        for d in range(count - 2):
            ref[count * sources + d] = cot[d * rows + row]


def sum_kernel(blocks, out_ref):
    for r in range(blocks.shape[1]):
        total = blocks[0, r].astype(F32)
        for k in range(1, blocks.shape[0]):
            total = total + blocks[k, r].astype(F32)
        for k in range(out_ref.shape[0]):
            out_ref[k, r] = total.astype(BF16)


def pair_kernel(kept, other, out_ref):
    first = other.shape[0] - kept.shape[0]
    for r in range(kept.shape[0]):
        total = (kept[r].astype(F32) + other[first + r].astype(F32)).astype(BF16)
        for k in range(out_ref.shape[0]):
            out_ref[k, r] = total


def unpack_kernel(parts, out_ref, wide):
    pairs, size = parts.shape[1:3]
    count, lines = out_ref.shape[:2]
    for t in range(pairs):
        total = parts[0, t].astype(F32)
        for k in range(1, parts.shape[0]):
            total = total + parts[k, t].astype(F32)
        wide[t * size : (t + 1) * size] = total
    for c in range(count):
        out_ref[c] = wide[pl.ds(c, lines, stride=count), :].astype(BF16)


def forward_kernel(planes, rows, at_ref, bias_ref, w_ref, cot, tiles, after, before, *refs):
    out_ref, face_ref, far_ref, kept_ref, grads, halves = refs
    cout, width = cot.shape[1:]
    sources = tiles.shape[0]
    edge = sources * (planes + 2)
    core = at_ref[0]

    def tile(s, p, t):
        if t == 0:
            return before[p * sources + s]
        if t == rows // 2 + 1:
            return after[p * sources + s]
        return tiles[s, p, t - 1]

    lane = lax.broadcasted_iota(jnp.int32, (cout, width), 1)
    channel = lax.broadcasted_iota(jnp.int32, (cout, width), 0)
    bias = jnp.zeros((cout, width), F32)
    for o in range(cout):
        bias = jnp.where(channel == o, bias_ref[o], bias)
    lefts, rights = [], []
    bias_sum = jnp.zeros((cout, width), F32)
    for d in range(planes):
        for pair in range(rows // 2 + 1):
            cells = [
                jnp.concatenate(
                    [tile(s, d + kd, pair + t) for t in range(2) for s in range(sources)], axis=0
                )
                for kd in range(3)
            ]
            acc = jnp.dot(w_ref[0], cells[0], preferred_element_type=F32)
            for kd in range(1, 3):
                acc = acc + jnp.dot(w_ref[kd], cells[kd], preferred_element_type=F32)
            stacks = []
            for e in range(2):
                z = acc[3 * e * cout : 3 * (e + 1) * cout]
                pre = (
                    z[cout : 2 * cout]
                    + jnp.where(lane == 0, 0.0, pltpu.roll(z[:cout], 1, 1))
                    + jnp.where(lane == width - 1, 0.0, pltpu.roll(z[2 * cout :], width - 1, 1))
                    + bias
                )
                small = jnp.exp(-jnp.abs(pre))
                sigmoid = jnp.where(pre >= 0, 1.0, small) / (1.0 + small)
                row = 2 * pair + e
                if row == 0:
                    cotangent = before[edge + d]
                elif row == rows + 1:
                    cotangent = after[edge + d]
                else:
                    cotangent = cot[d * rows + row - 1]
                grad = (cotangent.astype(F32) * (0.2 + 0.8 * sigmoid)).astype(BF16)
                grads[d, row] = grad
                if row == 0 or row == rows + 1:
                    stacks.append(jnp.zeros((3 * cout, width), BF16))
                    continue
                softplus = jnp.maximum(pre, 0.0) + jnp.log1p(small)
                out_ref[d * rows + row - 1] = (0.2 * pre + 0.8 * softplus).astype(BF16)
                grad = grad.astype(F32)
                bias_sum = bias_sum + grad
                stacks.append(shifted(grad, lane).astype(BF16))
            lefts.append(jnp.concatenate(stacks, axis=0))
            rights.append(cells)
    left = jnp.concatenate(lefts, axis=1)
    sums = [
        lax.dot_general(
            left,
            jnp.concatenate([cells[kd] for cells in rights], axis=1),
            (((1,), (1,)), ((), ())),
            preferred_element_type=F32,
        )
        for kd in range(3)
    ]

    first = (lane // PART) % 2 == 0
    blocks, last = [], []
    for kd in range(3):
        for kw in range(3):
            one = sums[kd][kw * cout : (kw + 1) * cout]
            two = sums[kd][(3 + kw) * cout : (4 + kw) * cout]
            back = pltpu.roll(two[:, width:], width - PART, 1)
            blocks.append(
                one[:, :width]
                + jnp.where(
                    first,
                    pltpu.roll(two[:, :width], width - PART, 1),
                    pltpu.roll(two[:, width:], PART, 1),
                )
            )
            last.append(one[:, width:] + back)
    last.append(jnp.broadcast_to(jnp.sum(bias_sum, axis=1, keepdims=True), (cout, width)))
    for k in range(0, len(last), 2):
        blocks.append(jnp.where(first, last[k], pltpu.roll(last[k + 1], PART, 1)))
    source = lax.broadcasted_iota(jnp.int32, (width, width), 0)
    target = (source // PART) % 2 * (width // 2) + source // (2 * PART) * PART + source % PART
    order = jnp.where(lax.broadcasted_iota(jnp.int32, (width, width), 1) == target, 1.0, 0.0).astype(BF16)
    placed = jnp.dot(jnp.concatenate(blocks, axis=0).astype(BF16), order, preferred_element_type=F32)
    count = len(blocks) // 2
    for k in range(2 * count):
        halves[k // count, k % count] = placed[k * cout : (k + 1) * cout].astype(BF16)
    face_ref[: rows + 2] = grads[1 - core]
    face_ref[rows + 2 :] = halves[1 - core]
    far_ref[...] = grads[core]
    kept_ref[...] = halves[core]


def backward_kernel(planes, rows, at_ref, w_ref, face, far, face_in, far_in, parts, stack):
    cout, width = far.shape[1:]
    cin = w_ref.shape[1]
    count = parts.shape[0]
    part = cin // count
    lane = lax.broadcasted_iota(jnp.int32, (cout, width), 1)
    step = 3 * cout
    core = at_ref[0]
    for q, source in enumerate((face_in, face, far, far_in)):
        p = jnp.where(core == 1, q, planes + 1 - q)
        for r in range(rows + 2):
            stack[p, r * step : (r + 1) * step, :] = shifted(source[r].astype(F32), lane).astype(BF16)
    w = jnp.transpose(w_ref[...].astype(F32)).astype(BF16)
    for d in range(planes):
        for h in range(0, rows, 2):
            cells = jnp.concatenate(
                [
                    jnp.concatenate(
                        [
                            stack[d + 2 - kd, (h + e + 2 - kh) * step : (h + e + 3 - kh) * step, :]
                            for kd in range(3)
                            for kh in range(3)
                        ],
                        axis=0,
                    )
                    for e in range(2)
                ],
                axis=1,
            )
            acc = jnp.dot(w, cells, preferred_element_type=F32)
            pair = (d * rows + h) // 2
            for f in range(count):
                piece = acc[f * part : (f + 1) * part]
                piece = jnp.concatenate([piece[:, :width], piece[:, width:]], axis=0).astype(BF16)
                parts[f, pair] = piece


def placing(cin):
    ones = np.zeros((2, 3, cin, 2, cin // PART, 2, PART), np.float32)
    for e in range(2):
        for kh in range(3):
            for i in range(cin):
                ones[e, kh, i, (kh + e) // 2, i // PART, (kh + e) % 2, i % PART] = 1
    return ones.reshape(2, 3 * cin, 4 * cin)


def weights_kernel(at_ref, mine, other, w_ref, b_ref):
    count, cout, width = mine.shape
    half = width // 2
    for k in range(2 * count):
        own = at_ref[0] == k // count
        block = jnp.where(own, mine[k % count].astype(F32), other[k % count].astype(F32))
        for e in range(2):
            piece = block[:, e * half : (e + 1) * half]
            at, kh = (k, e) if k < 9 else (2 * (k - 9) + e, 2)
            if at < 9:
                w_ref[at // 3 * 9 + kh * 3 + at % 3] = piece
    spare = block[:, half : half + cout]
    row = lax.broadcasted_iota(jnp.int32, (cout, cout), 0)
    lane = lax.broadcasted_iota(jnp.int32, (cout, cout), 1)
    b_ref[...] = jnp.sum(jnp.where(row == lane, spare, 0.0), axis=0, keepdims=True)


def call(body, name, *args, out, scratch=(), dtype=BF16, flops=0, moved=1 << 18, waves=0, scalars=0):
    smem, vmem = pl.BlockSpec(memory_space=pltpu.SMEM), pl.BlockSpec(memory_space=pltpu.VMEM)
    outs = tuple(jax.ShapeDtypeStruct(shape, dtype) for shape in out)
    results = pl.pallas_call(
        body,
        out_shape=outs,
        in_specs=[smem] * scalars + [vmem] * (len(args) - scalars),
        out_specs=(vmem,) * len(outs),
        scratch_shapes=[pltpu.VMEM(shape, kind) for shape, kind in scratch],
        compiler_params=pltpu.CompilerParams(vmem_limit_bytes=12 << 20),
        cost_estimate=pl.CostEstimate(flops=flops, bytes_accessed=moved, transcendentals=waves),
        name=name,
    )(*args)
    return results[0] if len(outs) == 1 else results


def per_device(activations, weights, bias, cotangent):
    cin_dev, planes, rows, width = activations.shape
    taps, cin, cout = weights.shape
    cells = planes * rows
    depth, height, filt = (lax.axis_size(axis) for axis in ("depth", "height", "filt"))
    swap = [(i, i ^ 1) for i in range(depth)]
    cross = [(i, i - 1 if i % 2 == 0 else i + 1) for i in range(1, depth - 1)]
    at = (lax.axis_index("depth") % 2).astype(jnp.int32).reshape(1)
    pairs, double = rows // 2, 2 * cin_dev

    work = 2 * cells * width * taps * cin * cout
    own, face = call(
        pack_kernel,
        "pack",
        at,
        activations.reshape(cin_dev, cells, width),
        out=[(planes, pairs, double, width), (pairs, double, width)],
        scratch=[((cin_dev * cells + cells, width), F32)],
        scalars=1,
    )
    facing = lax.ppermute(face, "depth", swap)
    far = call(far_kernel, "far", at, own, out=[face.shape], flops=64 * work, scalars=1)
    beyond = lax.ppermute(far, "depth", cross)
    grid = call(
        grid_kernel,
        "grid",
        at,
        own,
        facing,
        beyond,
        out=[(filt, planes + 2, pairs, double, width)],
        scalars=1,
    )
    tiles = swapped(grid, "filt")

    cot = cotangent.transpose(1, 2, 0, 3).reshape(cells, cout, width)
    split = weights.reshape(3, 3, 3, cin, cout)
    w_forward = jnp.einsum(
        "akj,ejn->aekn",
        split.transpose(0, 2, 4, 1, 3).reshape(3, 3 * cout, 3 * cin),
        jnp.asarray(placing(cin), BF16),
        preferred_element_type=F32,
    )
    w_forward = w_forward.astype(BF16).reshape(3, 6 * cout, 4 * cin)
    w_back = weights.transpose(0, 2, 1).reshape(taps * cout, cin)
    first, last = call(
        functools.partial(rows_kernel, rows),
        "rows",
        tiles,
        cot,
        out=[((planes + 2) * filt + planes, cout, width)] * 2,
    )
    first, last, w_forward = lax.optimization_barrier((first, last, w_forward))
    before, after = neighbours(first, last, "height")

    count = (taps + 1) // 4
    out, face, far, kept_sums = call(
        functools.partial(forward_kernel, planes, rows),
        "forward",
        at,
        bias,
        w_forward,
        cot,
        tiles,
        after,
        before,
        out=[(k, cout, width) for k in (cells, rows + 2 + count, rows + 2, count)],
        scratch=[((planes, rows + 2, cout, width), BF16), ((2, count, cout, width), BF16)],
        flops=3 * work,
        waves=1 << 17,
        scalars=2,
    )
    output = out.reshape(planes, rows, cout, width).transpose(2, 0, 1, 3)

    size = kept_sums.shape
    face_in = lax.ppermute(face, "depth", swap)
    far_in = lax.ppermute(far, "depth", cross)
    groups = [[(i + height - 2) % height for i in range(height)]]
    sums = call(pair_kernel, "pair", kept_sums, face_in, out=[(height,) + size])
    sums = swapped(sums, "height", groups)
    parts = call(
        functools.partial(backward_kernel, planes, rows),
        "backward",
        at,
        w_back,
        face,
        far,
        face_in,
        far_in,
        out=[(filt, cells // 2, double, width)],
        scratch=[((planes + 2, (rows + 2) * 3 * cout, width), BF16)],
        flops=64 * work,
        scalars=1,
    )
    groups = [[(i + depth // 2) % depth for i in range(k, depth, 2)] for k in range(2)]
    sums = swapped(call(sum_kernel, "sums", sums, out=[(depth // 2,) + size]), "depth", groups)
    sums, parts = lax.optimization_barrier((sums, parts))
    parts = swapped(parts, "filt")
    summed = call(
        unpack_kernel,
        "unpack",
        parts,
        out=[(cin_dev, cells, width)],
        scratch=[((cin_dev * cells + cin_dev, width), F32)],
    ).reshape(activations.shape)

    mine = call(sum_kernel, "sums", sums, out=[(1,) + size])[0]
    other = lax.ppermute(mine, "depth", swap)
    weight_grad, bias_grad = call(
        weights_kernel,
        "weights",
        at,
        mine,
        other,
        out=[(taps, cout, cin), (1, cout)],
        dtype=F32,
        scalars=1,
    )
    return (output, summed, weight_grad.transpose(0, 2, 1), bias_grad.reshape(cout))


def solution(mesh):
    placed = (
        P("filt", "depth", "height", None),
        P(None, None, "filt"),
        P("filt"),
        P("filt", "depth", "height", None),
    )
    return jax.shard_map(
        per_device,
        mesh=mesh,
        in_specs=placed,
        out_specs=(
            P("filt", "depth", "height", None),
            P("filt", "depth", "height", None),
            P(None, None, "filt"),
            P("filt"),
        ),
        check_vma=False,
    )
```

```python
import functools

import jax
import jax.numpy as jnp
import numpy as np
from jax import lax
from jax.experimental import pallas as pl
from jax.experimental.pallas import tpu as pltpu
from jax.sharding import PartitionSpec as P

BF16 = jnp.bfloat16
F32 = jnp.float32
PART = 8


def swapped(blocks, axis, groups=None):
    return lax.all_to_all(blocks, axis, 0, 0, tiled=True, axis_index_groups=groups)


def neighbours(first, last, axis):
    ends = lax.axis_size(axis) - 1
    after = lax.ppermute(first, axis, [(i + 1, i) for i in range(ends)])
    before = lax.ppermute(last, axis, [(i, i + 1) for i in range(ends)])
    return before, after


def shifted(value, lane):
    width = value.shape[-1]
    ahead = jnp.where(lane == width - 1, 0.0, pltpu.roll(value, width - 1, 1))
    behind = jnp.where(lane == 0, 0.0, pltpu.roll(value, 1, 1))
    return jnp.concatenate([ahead, value, behind], axis=0)


def pack_kernel(at_ref, cells, own, face_ref, wide):
    planes, pairs = own.shape[:2]
    count, lines = cells.shape[:2]
    for c in range(count):
        wide[c * lines : (c + 1) * lines] = cells[c].astype(F32)
    for d in range(planes):
        for t in range(pairs):
            row = 2 * (d * pairs + t)
            own[d, t] = jnp.concatenate(
                [wide[pl.ds(row + e, count, stride=lines), :] for e in range(2)], axis=0
            ).astype(BF16)
    face_ref[...] = own[jnp.where(at_ref[0] == 0, planes - 1, 0)]


def far_kernel(at_ref, own, far_ref):
    far_ref[...] = own[jnp.where(at_ref[0] == 0, 0, own.shape[0] - 1)]


def grid_kernel(at_ref, own, facing, beyond, out_ref):
    planes = own.shape[0]
    before = jnp.where(at_ref[0] == 0, 0, planes + 1)
    for k in range(out_ref.shape[0]):
        for d in range(planes):
            out_ref[k, d + 1] = own[d]
        out_ref[k, before] = beyond[...]
        out_ref[k, planes + 1 - before] = facing[...]


def rows_kernel(rows, tiles, cot, first_ref, last_ref):
    sources, count = tiles.shape[:2]
    for ref, t, row in ((first_ref, 0, 0), (last_ref, rows // 2 - 1, rows - 1)):
        for p in range(count):
            ref[p * sources : (p + 1) * sources] = tiles[:, p, t]
        for d in range(count - 2):
            ref[count * sources + d] = cot[d * rows + row]


def sum_kernel(blocks, out_ref):
    for r in range(blocks.shape[1]):
        total = blocks[0, r].astype(F32)
        for k in range(1, blocks.shape[0]):
            total = total + blocks[k, r].astype(F32)
        for k in range(out_ref.shape[0]):
            out_ref[k, r] = total.astype(BF16)


def pair_kernel(kept, other, out_ref):
    first = other.shape[0] - kept.shape[0]
    for r in range(kept.shape[0]):
        total = (kept[r].astype(F32) + other[first + r].astype(F32)).astype(BF16)
        for k in range(out_ref.shape[0]):
            out_ref[k, r] = total


def unpack_kernel(parts, out_ref, wide):
    pairs, size = parts.shape[1:3]
    count, lines = out_ref.shape[:2]
    for t in range(pairs):
        total = parts[0, t].astype(F32)
        for k in range(1, parts.shape[0]):
            total = total + parts[k, t].astype(F32)
        wide[t * size : (t + 1) * size] = total
    for c in range(count):
        out_ref[c] = wide[pl.ds(c, lines, stride=count), :].astype(BF16)


def forward_kernel(planes, rows, at_ref, bias_ref, w_ref, cot, tiles, after, before, *refs):
    out_ref, face_ref, far_ref, kept_ref, grads, halves = refs
    cout, width = cot.shape[1:]
    sources = tiles.shape[0]
    edge = sources * (planes + 2)
    core = at_ref[0]

    def tile(s, p, t):
        if t == 0:
            return before[p * sources + s]
        if t == rows // 2 + 1:
            return after[p * sources + s]
        return tiles[s, p, t - 1]

    lane = lax.broadcasted_iota(jnp.int32, (cout, width), 1)
    channel = lax.broadcasted_iota(jnp.int32, (cout, width), 0)
    bias = jnp.zeros((cout, width), F32)
    for o in range(cout):
        bias = jnp.where(channel == o, bias_ref[o], bias)
    lefts, rights = [], []
    bias_sum = jnp.zeros((cout, width), F32)
    for d in range(planes):
        for pair in range(rows // 2 + 1):
            cells = [
                jnp.concatenate(
                    [tile(s, d + kd, pair + t) for t in range(2) for s in range(sources)], axis=0
                )
                for kd in range(3)
            ]
            acc = jnp.dot(w_ref[0], cells[0], preferred_element_type=F32)
            for kd in range(1, 3):
                acc = acc + jnp.dot(w_ref[kd], cells[kd], preferred_element_type=F32)
            stacks = []
            for e in range(2):
                z = acc[3 * e * cout : 3 * (e + 1) * cout]
                pre = (
                    z[cout : 2 * cout]
                    + jnp.where(lane == 0, 0.0, pltpu.roll(z[:cout], 1, 1))
                    + jnp.where(lane == width - 1, 0.0, pltpu.roll(z[2 * cout :], width - 1, 1))
                    + bias
                )
                small = jnp.exp(-jnp.abs(pre))
                sigmoid = jnp.where(pre >= 0, 1.0, small) / (1.0 + small)
                row = 2 * pair + e
                if row == 0:
                    cotangent = before[edge + d]
                elif row == rows + 1:
                    cotangent = after[edge + d]
                else:
                    cotangent = cot[d * rows + row - 1]
                grad = (cotangent.astype(F32) * (0.2 + 0.8 * sigmoid)).astype(BF16)
                grads[d, row] = grad
                if row == 0 or row == rows + 1:
                    stacks.append(jnp.zeros((3 * cout, width), BF16))
                    continue
                softplus = jnp.maximum(pre, 0.0) + jnp.log1p(small)
                out_ref[d * rows + row - 1] = (0.2 * pre + 0.8 * softplus).astype(BF16)
                grad = grad.astype(F32)
                bias_sum = bias_sum + grad
                stacks.append(shifted(grad, lane).astype(BF16))
            lefts.append(jnp.concatenate(stacks, axis=0))
            rights.append(cells)
    left = jnp.concatenate(lefts, axis=1)
    sums = [
        lax.dot_general(
            left,
            jnp.concatenate([cells[kd] for cells in rights], axis=1),
            (((1,), (1,)), ((), ())),
            preferred_element_type=F32,
        )
        for kd in range(3)
    ]

    first = (lane // PART) % 2 == 0
    blocks, last = [], []
    for kd in range(3):
        for kw in range(3):
            one = sums[kd][kw * cout : (kw + 1) * cout]
            two = sums[kd][(3 + kw) * cout : (4 + kw) * cout]
            back = pltpu.roll(two[:, width:], width - PART, 1)
            blocks.append(
                one[:, :width]
                + jnp.where(
                    first,
                    pltpu.roll(two[:, :width], width - PART, 1),
                    pltpu.roll(two[:, width:], PART, 1),
                )
            )
            last.append(one[:, width:] + back)
    last.append(jnp.broadcast_to(jnp.sum(bias_sum, axis=1, keepdims=True), (cout, width)))
    for k in range(0, len(last), 2):
        blocks.append(jnp.where(first, last[k], pltpu.roll(last[k + 1], PART, 1)))
    source = lax.broadcasted_iota(jnp.int32, (width, width), 0)
    target = (source // PART) % 2 * (width // 2) + source // (2 * PART) * PART + source % PART
    order = jnp.where(lax.broadcasted_iota(jnp.int32, (width, width), 1) == target, 1.0, 0.0).astype(BF16)
    placed = jnp.dot(jnp.concatenate(blocks, axis=0).astype(BF16), order, preferred_element_type=F32)
    count = len(blocks) // 2
    for k in range(2 * count):
        halves[k // count, k % count] = placed[k * cout : (k + 1) * cout].astype(BF16)
    face_ref[: rows + 2] = grads[1 - core]
    face_ref[rows + 2 :] = halves[1 - core]
    far_ref[...] = grads[core]
    kept_ref[...] = halves[core]


def backward_kernel(planes, rows, at_ref, w_ref, face, far, face_in, far_in, parts, stack):
    cout, width = far.shape[1:]
    cin = w_ref.shape[1]
    count = parts.shape[0]
    part = cin // count
    lane = lax.broadcasted_iota(jnp.int32, (cout, width), 1)
    step = 3 * cout
    core = at_ref[0]
    for q, source in enumerate((face_in, face, far, far_in)):
        p = jnp.where(core == 1, q, planes + 1 - q)
        for r in range(rows + 2):
            stack[p, r * step : (r + 1) * step, :] = shifted(source[r].astype(F32), lane).astype(BF16)
    w = jnp.transpose(w_ref[...].astype(F32)).astype(BF16)
    for d in range(planes):
        for h in range(0, rows, 2):
            cells = jnp.concatenate(
                [
                    jnp.concatenate(
                        [
                            stack[d + 2 - kd, (h + e + 2 - kh) * step : (h + e + 3 - kh) * step, :]
                            for kd in range(3)
                            for kh in range(3)
                        ],
                        axis=0,
                    )
                    for e in range(2)
                ],
                axis=1,
            )
            acc = jnp.dot(w, cells, preferred_element_type=F32)
            pair = (d * rows + h) // 2
            for f in range(count):
                piece = acc[f * part : (f + 1) * part]
                piece = jnp.concatenate([piece[:, :width], piece[:, width:]], axis=0).astype(BF16)
                parts[f, pair] = piece


def placing(cin):
    ones = np.zeros((2, 3, cin, 2, cin // PART, 2, PART), np.float32)
    for e in range(2):
        for kh in range(3):
            for i in range(cin):
                ones[e, kh, i, (kh + e) // 2, i // PART, (kh + e) % 2, i % PART] = 1
    return ones.reshape(2, 3 * cin, 4 * cin)


def weights_kernel(at_ref, mine, other, w_ref, b_ref):
    count, cout, width = mine.shape
    half = width // 2
    for k in range(2 * count):
        own = at_ref[0] == k // count
        block = jnp.where(own, mine[k % count].astype(F32), other[k % count].astype(F32))
        for e in range(2):
            piece = block[:, e * half : (e + 1) * half]
            at, kh = (k, e) if k < 9 else (2 * (k - 9) + e, 2)
            if at < 9:
                w_ref[at // 3 * 9 + kh * 3 + at % 3] = piece
    spare = block[:, half : half + cout]
    row = lax.broadcasted_iota(jnp.int32, (cout, cout), 0)
    lane = lax.broadcasted_iota(jnp.int32, (cout, cout), 1)
    b_ref[...] = jnp.sum(jnp.where(row == lane, spare, 0.0), axis=0, keepdims=True)


def call(body, name, *args, out, scratch=(), dtype=BF16, flops=0, moved=1 << 18, waves=0, scalars=0):
    smem, vmem = pl.BlockSpec(memory_space=pltpu.SMEM), pl.BlockSpec(memory_space=pltpu.VMEM)
    outs = tuple(jax.ShapeDtypeStruct(shape, dtype) for shape in out)
    results = pl.pallas_call(
        body,
        out_shape=outs,
        in_specs=[smem] * scalars + [vmem] * (len(args) - scalars),
        out_specs=(vmem,) * len(outs),
        scratch_shapes=[pltpu.VMEM(shape, kind) for shape, kind in scratch],
        compiler_params=pltpu.CompilerParams(vmem_limit_bytes=12 << 20),
        cost_estimate=pl.CostEstimate(flops=flops, bytes_accessed=moved, transcendentals=waves),
        name=name,
    )(*args)
    return results[0] if len(outs) == 1 else results


def per_device(activations, weights, bias, cotangent):
    cin_dev, planes, rows, width = activations.shape
    taps, cin, cout = weights.shape
    cells = planes * rows
    depth, height, filt = (lax.axis_size(axis) for axis in ("depth", "height", "filt"))
    swap = [(i, i ^ 1) for i in range(depth)]
    cross = [(i, i - 1 if i % 2 == 0 else i + 1) for i in range(1, depth - 1)]
    at = (lax.axis_index("depth") % 2).astype(jnp.int32).reshape(1)
    pairs, double = rows // 2, 2 * cin_dev

    work = 2 * cells * width * taps * cin * cout
    own, face = call(
        pack_kernel,
        "pack",
        at,
        activations.reshape(cin_dev, cells, width),
        out=[(planes, pairs, double, width), (pairs, double, width)],
        scratch=[((cin_dev * cells + cells, width), F32)],
        scalars=1,
    )
    facing = lax.ppermute(face, "depth", swap)
    far = call(far_kernel, "far", at, own, out=[face.shape], flops=64 * work, scalars=1)
    beyond = lax.ppermute(far, "depth", cross)
    grid = call(
        grid_kernel,
        "grid",
        at,
        own,
        facing,
        beyond,
        out=[(filt, planes + 2, pairs, double, width)],
        scalars=1,
    )
    tiles = swapped(grid, "filt")

    cot = cotangent.transpose(1, 2, 0, 3).reshape(cells, cout, width)
    split = weights.reshape(3, 3, 3, cin, cout)
    w_forward = jnp.einsum(
        "akj,ejn->aekn",
        split.transpose(0, 2, 4, 1, 3).reshape(3, 3 * cout, 3 * cin),
        jnp.asarray(placing(cin), BF16),
        preferred_element_type=F32,
    )
    w_forward = w_forward.astype(BF16).reshape(3, 6 * cout, 4 * cin)
    w_back = weights.transpose(0, 2, 1).reshape(taps * cout, cin)
    first, last = call(
        functools.partial(rows_kernel, rows),
        "rows",
        tiles,
        cot,
        out=[((planes + 2) * filt + planes, cout, width)] * 2,
    )
    first, last, w_forward = lax.optimization_barrier((first, last, w_forward))
    before, after = neighbours(first, last, "height")

    count = (taps + 1) // 4
    out, face, far, kept_sums = call(
        functools.partial(forward_kernel, planes, rows),
        "forward",
        at,
        bias,
        w_forward,
        cot,
        tiles,
        after,
        before,
        out=[(k, cout, width) for k in (cells, rows + 2 + count, rows + 2, count)],
        scratch=[((planes, rows + 2, cout, width), BF16), ((2, count, cout, width), BF16)],
        flops=3 * work,
        waves=1 << 17,
        scalars=2,
    )
    output = out.reshape(planes, rows, cout, width).transpose(2, 0, 1, 3)

    size = kept_sums.shape
    face_in = lax.ppermute(face, "depth", swap)
    far_in = lax.ppermute(far, "depth", cross)
    groups = [list(range(2, height))[::-1] + [0, 1]]
    sums = call(pair_kernel, "pair", kept_sums, face_in, out=[(height,) + size])
    sums = swapped(sums, "height", groups)
    parts = call(
        functools.partial(backward_kernel, planes, rows),
        "backward",
        at,
        w_back,
        face,
        far,
        face_in,
        far_in,
        out=[(filt, cells // 2, double, width)],
        scratch=[((planes + 2, (rows + 2) * 3 * cout, width), BF16)],
        flops=64 * work,
        scalars=1,
    )
    groups = [[(i + depth // 2) % depth for i in range(k, depth, 2)] for k in range(2)]
    sums = swapped(call(sum_kernel, "sums", sums, out=[(depth // 2,) + size]), "depth", groups)
    sums, parts = lax.optimization_barrier((sums, parts))
    parts = swapped(parts, "filt")
    summed = call(
        unpack_kernel,
        "unpack",
        parts,
        out=[(cin_dev, cells, width)],
        scratch=[((cin_dev * cells + cin_dev, width), F32)],
    ).reshape(activations.shape)

    mine = call(sum_kernel, "sums", sums, out=[(1,) + size])[0]
    other = lax.ppermute(mine, "depth", swap)
    weight_grad, bias_grad = call(
        weights_kernel,
        "weights",
        at,
        mine,
        other,
        out=[(taps, cout, cin), (1, cout)],
        dtype=F32,
        scalars=1,
    )
    return (output, summed, weight_grad.transpose(0, 2, 1), bias_grad.reshape(cout))


def solution(mesh):
    placed = (
        P("filt", "depth", "height", None),
        P(None, None, "filt"),
        P("filt"),
        P("filt", "depth", "height", None),
    )
    return jax.shard_map(
        per_device,
        mesh=mesh,
        in_specs=placed,
        out_specs=(
            P("filt", "depth", "height", None),
            P("filt", "depth", "height", None),
            P(None, None, "filt"),
            P("filt"),
        ),
        check_vma=False,
    )
```
